32 devices in a mesh: expert: 8 (over y, x, core), fsdp: 4 (over z).
Axes of the slice: x: 2, y: 2, z: 4, core: 2. Of those that a mesh axis runs over, the one named last changes fastest.
Arguments:
- tokens: bfloat16 [1024, 7168], P('expert', 'fsdp'), may hold values from -6 to 6
- counts: int32 [8, 4], P('expert'), may hold values from 1 to 64, as said below
- gate_values: bfloat16 [8, 7168, 1024], P('expert', 'fsdp'), may hold values from -0.0625 to 0.0625
- up_values: bfloat16 [8, 7168, 1024], P('expert', 'fsdp'), may hold values from -0.0625 to 0.0625
- gate_scales: float32 [8, 56, 8], P('expert'), may hold values from 0.5 to 2
- up_scales: float32 [8, 56, 8], P('expert'), may hold values from 0.5 to 2
- grad_hidden: bfloat16 [8, 512, 1024], P('expert', 'fsdp'), may hold values from -6 to 6
Outputs:
- hidden: bfloat16 [8, 512, 1024], P('expert', 'fsdp')
- grad_gate: bfloat16 [8, 7168, 1024], P('expert', 'fsdp')
- grad_up: bfloat16 [8, 7168, 1024], P('expert', 'fsdp')
- grad_tokens: bfloat16 [1024, 7168], P('expert', 'fsdp')
The draws below stay inside these ranges and needn't reach their ends.
Inputs may be any that keep to these rules, and one draw needn't show every extreme that they name: Each row of counts sums to 128. In every draw one expert, drawn from the seed, receives exactly 64 rows from every source index.
All inputs are finite; a program needn't handle non-finite values.
Results may differ from the reference program's by a relative error of at most 0.025.
Values may be sent and summed in bfloat16 or wider, within the bound.
No kernel may reach another device: no remote copies, remote signals or barrier semaphores. Data moves between devices by JAX's collectives and lax.ppermute only.
A program may use at most 64 MiB of HBM per device.

```python
import math
import jax
import jax.numpy as jnp
from jax import lax

D = 7168
ROWS = 128
EXPERTS = 4
HALF = 1024
CAP = 64
SLOTS = 512
N_EXPERT = 8
N_FSDP = 4


def draw_counts(key, part):
    capacity = CAP
    hot_key, seat_key = jax.random.split(jax.random.fold_in(key, 11))
    hot_expert = jax.random.randint(hot_key, (), 0, EXPERTS)
    extra_rows = ROWS - capacity - (EXPERTS - 1)
    seat_count = (EXPERTS - 1) * (capacity - 1)

    def one_source(sub_key):
        shuffled = jax.random.permutation(sub_key, seat_count)
        chosen = (shuffled < extra_rows).astype(jnp.int32)
        return chosen.reshape(EXPERTS - 1, capacity - 1).sum(axis=1) + 1
    sub_keys = jax.random.split(seat_key, N_EXPERT)
    others = jax.vmap(one_source)(sub_keys)
    columns = jnp.arange(EXPERTS, dtype=jnp.int32)
    shifted = jnp.clip(columns - (columns > hot_expert).astype(jnp.int32), 0, EXPERTS - 2)
    picked = others[:, shifted]
    return jnp.where(columns[None, :] == hot_expert, capacity, picked).astype(jnp.int32)


def shard_levels(own_key, shape, shards, least, largest):
    def one(position, parts):
        draws = jax.random.uniform(jax.random.fold_in(jax.random.fold_in(own_key, 6), position), (parts,), jnp.float32, least / len(shards), largest / len(shards))
        return jnp.repeat(jnp.exp(draws), shape[position] // parts).reshape((-1,) + (1,) * (len(shape) - position - 1))

    loudness = one(*shards[0])
    for cut in shards[1:]:
        loudness = loudness * one(*cut)
    return loudness


def normal_values(stream_key, shape, deviation, bound, cuts=(), kind=jnp.bfloat16):
    values = jax.random.normal(stream_key, shape, jnp.float32) * deviation
    if len(cuts) > 0:
        values = shard_levels(stream_key, shape, cuts, -0.22, 0.18) * values
    return jnp.clip(values, min=-bound, max=bound).astype(kind)


def setup_inputs(seed: int = 0) -> dict:
    key_list = jax.random.split(jax.random.key(seed), 8)
    return {
        "tokens": normal_values(key_list[0], (N_EXPERT * ROWS, D), 1.0, 6.0, ((0, 8), (1, 4))),
        "counts": draw_counts(jax.random.fold_in(key_list[7], 71), 0),
        "gate_values": normal_values(key_list[2], (2 * EXPERTS, D, HALF), D ** -0.5, 0.0625, ((0, 8), (1, 4))),
        "up_values": normal_values(key_list[3], (2 * EXPERTS, D, HALF), D ** -0.5, 0.0625, ((0, 8), (1, 4))),
        "gate_scales": jnp.clip(jnp.exp(math.log(2.0) - 1.3862944 * jax.random.uniform(key_list[4], (2 * EXPERTS, D // 128, HALF // 128), jnp.float32) ** shard_levels(key_list[4], (2 * EXPERTS, D // 128, HALF // 128), ((0, 8),), -0.2, 0.2)), 0.5, 2.0),
        "up_scales": jnp.clip(jnp.exp(math.log(2.0) - 1.3862944 * jax.random.uniform(key_list[5], (2 * EXPERTS, D // 128, HALF // 128), jnp.float32) ** shard_levels(key_list[5], (2 * EXPERTS, D // 128, HALF // 128), ((0, 8),), -0.2, 0.2)), 0.5, 2.0),
        "grad_hidden": normal_values(key_list[6], (2 * EXPERTS, SLOTS, HALF), 1.0, 6.0, ((0, 8), (1, 4))),
    }


def expand(values, scales):
    grown = jnp.repeat(jnp.repeat(scales, 128, axis=0), 128, axis=1)
    return (values.astype(jnp.float32) * grown).astype(jnp.bfloat16)


def blocked_sum(inputs, weights):
    feat_cols = D // N_FSDP
    slot_count = inputs.shape[0]
    pieces = inputs.reshape(slot_count, N_FSDP, feat_cols).transpose(1, 0, 2)
    blocks = weights.reshape(N_FSDP, feat_cols, weights.shape[1])

    def add_block(running, pair_args):
        in_block, w_block = pair_args
        term_rows = jnp.dot(in_block, w_block, preferred_element_type=jnp.float32).astype(jnp.bfloat16)
        term_rows = lax.optimization_barrier(term_rows)
        return running + term_rows.astype(jnp.float32), None

    running, unused = lax.scan(add_block, jnp.zeros((slot_count, weights.shape[1]), jnp.float32), (pieces, blocks))
    return running


def reference(tokens, counts, gate_values, up_values, gate_scales, up_scales, grad_hidden):
    capacity = CAP
    starts = (jnp.cumsum(counts, axis=1) - counts).astype(jnp.int32)
    slot_ids = jnp.arange(capacity, dtype=jnp.int32)
    source = jnp.arange(N_EXPERT, dtype=jnp.int32)
    spare_row = N_EXPERT * ROWS
    padded = jnp.concatenate([tokens, jnp.zeros((1, D), tokens.dtype)], 0)

    def per_expert(carry, expert):
        live_count = counts[:, expert]
        begin_at = starts[:, expert]
        is_live = slot_ids[None, :] < live_count[:, None]
        gather_ids = jnp.where(is_live, source[:, None] * ROWS + begin_at[:, None] + slot_ids[None, :], spare_row)
        gather_ids = gather_ids.reshape(-1).astype(jnp.int32)
        inputs = padded[gather_ids]
        hiddens, gate_grads, up_grads, backs = [], [], [], []
        for half_id in range(2):
            which = 2 * expert + half_id
            weights = jnp.concatenate([expand(gate_values[which], gate_scales[which]),
                                       expand(up_values[which], up_scales[which])], 1)
            summed = blocked_sum(inputs, weights)
            gate_pre = summed[:, :HALF]
            up_pre = summed[:, HALF:]
            sigmoid_gate = jax.nn.sigmoid(gate_pre)
            hiddens.append((gate_pre * sigmoid_gate * up_pre).astype(jnp.bfloat16))
            cot_rows = grad_hidden[which].astype(jnp.float32)
            grad_gate_pre = (cot_rows * up_pre * sigmoid_gate * (1.0 + gate_pre * (1.0 - sigmoid_gate))).astype(jnp.bfloat16)
            grad_up_pre = (cot_rows * gate_pre * sigmoid_gate).astype(jnp.bfloat16)
            grads = jnp.concatenate([grad_gate_pre, grad_up_pre], 1)
            weight_grad = jnp.dot(inputs.T, grads, preferred_element_type=jnp.float32)
            gate_grads.append(weight_grad[:, :HALF].astype(jnp.bfloat16))
            up_grads.append(weight_grad[:, HALF:].astype(jnp.bfloat16))
            backs.append(jnp.dot(grads, weights.T, preferred_element_type=jnp.float32).astype(jnp.bfloat16))
        combined = (backs[0].astype(jnp.float32) + backs[1].astype(jnp.float32)).astype(jnp.bfloat16)
        carry = carry.at[gather_ids].set(combined)
        return carry, (jnp.stack(hiddens), jnp.stack(gate_grads), jnp.stack(up_grads))

    grad_tokens, stacked = lax.scan(per_expert, jnp.zeros((spare_row + 1, D), jnp.bfloat16),
                                    jnp.arange(EXPERTS, dtype=jnp.int32))
    hidden = stacked[0].reshape(2 * EXPERTS, N_EXPERT * capacity, HALF)
    grad_gate = stacked[1].reshape(2 * EXPERTS, D, HALF)
    grad_up = stacked[2].reshape(2 * EXPERTS, D, HALF)
    return (hidden, grad_gate, grad_up, grad_tokens[:spare_row])
```

```python
import math

import jax
import jax.numpy as jnp
from jax import lax
from jax.experimental import pallas as pl
from jax.experimental.pallas import tpu as pltpu
from jax.sharding import PartitionSpec as P


def swap(value, axis, mask):
    pairs = [(source, source ^ mask) for source in range(lax.axis_size(axis))]
    return lax.ppermute(value, axis, pairs)


def pick(blocks, index):
    return lax.dynamic_index_in_dim(blocks, index, 0, keepdims=False)


def scale_kernel(sub, start_ref, gate_ref, up_ref, gate_row_ref, up_row_ref, out_ref):
    rows, half_units = gate_ref.shape[1:]
    base = start_ref[0] + pl.program_id(0) * rows
    for piece in range(rows // sub):
        block = (base + piece * sub) // 128
        here = slice(piece * sub, (piece + 1) * sub)
        gate = gate_ref[0, here, :].astype(jnp.float32) * gate_row_ref[pl.ds(block, 1), :]
        up = up_ref[0, here, :].astype(jnp.float32) * up_row_ref[pl.ds(block, 1), :]
        out_ref[here, :half_units] = gate.astype(jnp.bfloat16)
        out_ref[here, half_units:] = up.astype(jnp.bfloat16)


def scaled_weights(gate_values, up_values, gate_scales, up_scales, start_row):
    feat_cols, half_units = gate_values.shape[1:]
    blocks = gate_scales.shape[1]
    sub = math.gcd(feat_cols, 128)
    rows = max(r for r in range(sub, 257, sub) if feat_cols % r == 0)
    value_spec = pl.BlockSpec((1, rows, half_units), lambda i, start: (0, i, 0))
    scale_spec = pl.BlockSpec((blocks, half_units), lambda i, start: (0, 0))
    return pl.pallas_call(
        lambda *refs: scale_kernel(sub, *refs),
        out_shape=jax.ShapeDtypeStruct((feat_cols, 2 * half_units), jnp.bfloat16),
        grid_spec=pltpu.PrefetchScalarGridSpec(
            num_scalar_prefetch=1,
            grid=(feat_cols // rows,),
            in_specs=[value_spec, value_spec, scale_spec, scale_spec],
            out_specs=pl.BlockSpec((rows, 2 * half_units), lambda i, start: (i, 0)),
        ),
        compiler_params=pltpu.CompilerParams(vmem_limit_bytes=24 * 2**20),
        cost_estimate=pl.CostEstimate(
            flops=2 * feat_cols * half_units,
            bytes_accessed=8 * feat_cols * half_units,
            transcendentals=0,
        ),
        name="scale_weights",
    )(
        start_row[None],
        gate_values,
        up_values,
        jnp.repeat(gate_scales[0], 128, axis=1),
        jnp.repeat(up_scales[0], 128, axis=1),
    )


def add_rounded(first, second):
    return (first.astype(jnp.float32) + second.astype(jnp.float32)).astype(jnp.bfloat16)


def line_reduce(own, axis, chip):
    size = lax.axis_size(axis)
    index = lax.axis_index(axis)
    mirror = size - 1 - index

    def block(owner):
        return pick(own, jnp.clip(owner, 0, size - 1) ^ chip)

    rising = falling = None
    for step in range(1, size):
        up = block(size - step + index)
        down = block(step - 1 - mirror)
        if step > 1:
            up = add_rounded(up, rising)
            down = add_rounded(down, falling)
        rising = lax.ppermute(up, axis, [(j, j + 1) for j in range(step)])
        falling = lax.ppermute(
            down, axis, [(size - 1 - j, size - 2 - j) for j in range(step)]
        )
    return (
        block(index).astype(jnp.float32)
        + rising.astype(jnp.float32)
        + falling.astype(jnp.float32)
    )


def line_gather(own, axis, chip):
    size = lax.axis_size(axis)
    index = lax.axis_index(axis)
    rising, falling = [own], [own]
    for step in range(1, size):
        rising.append(
            lax.ppermute(rising[-1], axis, [(j, j + 1) for j in range(step - 1, size - 1)])
        )
        falling.append(
            lax.ppermute(
                falling[-1],
                axis,
                [(size - 1 - j, size - 2 - j) for j in range(step - 1, size - 1)],
            )
        )
    whole = jnp.zeros((size,) + own.shape, own.dtype)
    whole = lax.dynamic_update_index_in_dim(whole, own, index ^ chip, 0)
    for step in range(1, size):
        piece = jnp.where(index >= step, rising[step], falling[size - step])
        whole = lax.dynamic_update_index_in_dim(
            whole, piece, lax.rem(index - step + size, size) ^ chip, 0
        )
    return whole


def on_device(tokens, counts, gate_values, up_values, gate_scales, up_scales, grad_hidden):
    row_total, feat_cols = tokens.shape
    experts = counts.shape[1]
    capacity = min(4 * row_total // experts, row_total // 2)
    n_expert = lax.axis_size("expert")
    chips = n_expert // 2
    half_units = gate_values.shape[2]
    parity = lax.axis_index("expert") % 2
    chip = lax.axis_index("expert") // 2
    index = lax.axis_index("fsdp")

    own_counts = counts[0]
    starts = jnp.cumsum(own_counts) - own_counts
    slot_ids = jnp.arange(capacity, dtype=jnp.int32)
    row_ids = jnp.arange(row_total, dtype=jnp.int32)
    chooser = (
        (row_ids[None, None, :] == (starts[:, None] + slot_ids[None, :])[:, :, None])
        & (slot_ids[None, :] < own_counts[:, None])[:, :, None]
    ).astype(jnp.bfloat16)
    packed = jnp.dot(
        chooser.reshape(experts * capacity, row_total),
        tokens,
        preferred_element_type=jnp.float32,
    ).astype(jnp.bfloat16)
    packed = packed.reshape(experts, capacity, feat_cols)
    arrived = [pick(packed, chip)]
    for mask in range(1, chips):
        arrived.append(swap(pick(packed, chip ^ mask), "expert", 2 * mask))
    own_inputs = jnp.concatenate(arrived, 0)
    other_inputs = swap(own_inputs, "expert", 1)

    weights = scaled_weights(
        gate_values, up_values, gate_scales, up_scales, index * feat_cols
    )
    cots = grad_hidden[0].reshape(2, capacity, half_units)

    hiddens, grads = [], []
    for inputs, which in ((own_inputs, parity), (other_inputs, 1 - parity)):
        partial = jnp.dot(inputs, weights, preferred_element_type=jnp.float32).astype(
            jnp.bfloat16
        )
        pre = line_reduce(partial.reshape(chips, capacity, 2 * half_units), "fsdp", chip)
        gate_pre = pre[:, :half_units]
        up_pre = pre[:, half_units:]
        cot = pick(cots, which).astype(jnp.float32)
        sigmoid_gate = jax.nn.sigmoid(gate_pre)
        hiddens.append((gate_pre * sigmoid_gate * up_pre).astype(jnp.bfloat16))
        grad_gate_pre = cot * up_pre * sigmoid_gate * (1.0 + gate_pre * (1.0 - sigmoid_gate))
        grad_up_pre = cot * gate_pre * sigmoid_gate
        grads.append(
            jnp.concatenate(
                [grad_gate_pre.astype(jnp.bfloat16), grad_up_pre.astype(jnp.bfloat16)], 1
            )
        )
    hidden = jnp.where(
        parity == 0, jnp.stack(hiddens), jnp.stack([hiddens[1], hiddens[0]])
    ).reshape(2 * capacity, half_units)

    gathered, returned = [], []
    for side in range(2):
        whole = line_gather(grads[side], "fsdp", chip).reshape(chips * capacity, 2 * half_units)
        gathered.append(whole)
        back = lax.dot_general(
            whole, weights, (((1,), (1,)), ((), ())), preferred_element_type=jnp.float32
        ).astype(jnp.bfloat16)
        back = back.reshape(chips, capacity, feat_cols)
        came = []
        for mask in range(chips):
            jump = 2 * mask + side
            came.append(swap(back[mask], "expert", jump) if jump else back[mask])
        returned.append(jnp.concatenate(came, 0))

    weight_sum = lax.dot_general(
        jnp.concatenate([own_inputs, other_inputs], 0),
        jnp.concatenate(gathered, 0),
        (((0,), (0,)), ((), ())),
        preferred_element_type=jnp.float32,
    )
    grad_gate = weight_sum[:, :half_units].astype(jnp.bfloat16)[None]
    grad_up = weight_sum[:, half_units:].astype(jnp.bfloat16)[None]

    near = jnp.arange(chips, dtype=jnp.int32) ^ chip
    placer = (chooser[near].reshape(chips * capacity, row_total)).astype(jnp.bfloat16)
    grad_tokens = lax.dot_general(
        jnp.concatenate([placer, placer], 0),
        jnp.concatenate(returned, 0),
        (((0,), (0,)), ((), ())),
        preferred_element_type=jnp.float32,
    ).astype(jnp.bfloat16)
    return (hidden[None], grad_gate, grad_up, grad_tokens)


def solution(mesh):
    in_specs = (
        P("expert", "fsdp"),
        P("expert", None),
        P("expert", "fsdp", None),
        P("expert", "fsdp", None),
        P("expert", None, None),
        P("expert", None, None),
        P("expert", "fsdp", None),
    )
    out_specs = (
        P("expert", "fsdp", None),
        P("expert", "fsdp", None),
        P("expert", "fsdp", None),
        P("expert", "fsdp"),
    )
    return jax.shard_map(
        on_device, mesh=mesh, in_specs=in_specs, out_specs=out_specs, check_vma=False
    )
```

```python
import math

import jax
import jax.numpy as jnp
from jax import lax
from jax.experimental import pallas as pl
from jax.experimental.pallas import tpu as pltpu
from jax.sharding import PartitionSpec as P


def swap(value, axis, mask):
    pairs = [(source, source ^ mask) for source in range(lax.axis_size(axis))]
    return lax.ppermute(value, axis, pairs)


def pick(blocks, index):
    return lax.dynamic_index_in_dim(blocks, index, 0, keepdims=False)


def scale_kernel(sub, start_ref, gate_ref, up_ref, gate_scale_ref, up_scale_ref, out_ref):
    rows, half_units = gate_ref.shape[1:]
    base = start_ref[0] + pl.program_id(0) * rows
    for value_ref, scale_ref, offset in (
        (gate_ref, gate_scale_ref, 0),
        (up_ref, up_scale_ref, half_units),
    ):
        for piece in range(rows // sub):
            block = (base + piece * sub) // 128
            here = slice(piece * sub, (piece + 1) * sub)
            for column in range(half_units // 128):
                there = slice(column * 128, (column + 1) * 128)
                scaled = value_ref[0, here, there].astype(jnp.float32) * scale_ref[block, column]
                out_ref[here, offset + column * 128 : offset + (column + 1) * 128] = (
                    scaled.astype(jnp.bfloat16)
                )


def scaled_weights(gate_values, up_values, gate_scales, up_scales, start_row):
    feat_cols, half_units = gate_values.shape[1:]
    sub = math.gcd(feat_cols, 128)
    rows = max(r for r in range(sub, 257, sub) if feat_cols % r == 0)
    value_spec = pl.BlockSpec((1, rows, half_units), lambda i, start: (0, i, 0))
    scale_spec = pl.BlockSpec(memory_space=pltpu.SMEM)
    return pl.pallas_call(
        lambda *refs: scale_kernel(sub, *refs),
        out_shape=jax.ShapeDtypeStruct((feat_cols, 2 * half_units), jnp.bfloat16),
        grid_spec=pltpu.PrefetchScalarGridSpec(
            num_scalar_prefetch=1,
            grid=(feat_cols // rows,),
            in_specs=[value_spec, value_spec, scale_spec, scale_spec],
            out_specs=pl.BlockSpec((rows, 2 * half_units), lambda i, start: (i, 0)),
        ),
        compiler_params=pltpu.CompilerParams(vmem_limit_bytes=24 * 2**20),
        cost_estimate=pl.CostEstimate(
            flops=2 * feat_cols * half_units,
            bytes_accessed=8 * feat_cols * half_units,
            transcendentals=0,
        ),
        name="scale_weights",
    )(start_row[None], gate_values, up_values, gate_scales[0], up_scales[0])


def earlier(value, *needed):
    return lax.optimization_barrier((value,) + needed)[0]


def add_rounded(first, second):
    return (first.astype(jnp.float32) + second.astype(jnp.float32)).astype(jnp.bfloat16)


def towards_middle(size, step):
    return [(step - 1, step), (size - step, size - 1 - step)]


def from_middle(size, step):
    return [(target, source) for source, target in towards_middle(size, size // 2 - step)]


def between_middle(size):
    return [(size // 2 - 1, size // 2), (size // 2, size // 2 - 1)]


def to_middle(size, end):
    return [(end, size // 2 - 1), (size - 1 - end, size // 2)]


def on_device(tokens, counts, gate_values, up_values, gate_scales, up_scales, grad_hidden):
    row_total, feat_cols = tokens.shape
    experts = counts.shape[1]
    capacity = min(4 * row_total // experts, row_total // 2)
    n_expert = lax.axis_size("expert")
    n_fsdp = lax.axis_size("fsdp")
    chips = n_expert // 2
    high_chip = chips // 2
    half_line = n_fsdp // 2
    half_units = gate_values.shape[2]
    parity = lax.axis_index("expert") % 2
    chip = lax.axis_index("expert") // 2
    index = lax.axis_index("fsdp")
    is_low = index < half_line
    is_middle = (index == half_line - 1) | (index == half_line)
    keeps_first = is_low == (chip < high_chip)

    own_cot = grad_hidden[0].reshape(2, capacity, half_units)
    cots = [
        lax.ppermute(own_cot, "fsdp", to_middle(n_fsdp, end)) for end in range(half_line - 1)
    ]
    cots = jnp.stack(cots + [own_cot])

    row_ids = jnp.arange(row_total, dtype=jnp.int32)
    slot_ids = jnp.arange(capacity, dtype=jnp.int32)
    choosers = []
    start = jnp.int32(0)
    for expert in range(experts):
        live = counts[0, expert]
        choosers.append(
            (row_ids[None, :] == start + slot_ids[:, None]) & (slot_ids[:, None] < live)
        )
        start = start + live
    chooser = jnp.stack(choosers).astype(jnp.bfloat16)
    packed = jnp.dot(
        chooser.reshape(experts * capacity, row_total),
        tokens,
        preferred_element_type=jnp.float32,
    ).astype(jnp.bfloat16)
    packed = packed.reshape(experts, capacity, feat_cols)

    near = [mask for mask in range(high_chip) if mask % 2 == 0]
    far = [mask for mask in range(high_chip) if mask % 2 == 1]
    near = near + [mask + high_chip for mask in near]
    far = far + [mask + high_chip for mask in far]

    def arrive(masks):
        blocks = [
            swap(pick(packed, chip ^ mask), "expert", 2 * mask)
            if mask
            else pick(packed, chip)
            for mask in masks
        ]
        return jnp.concatenate(blocks, 0)

    own_near, own_far = arrive(near), arrive(far)
    groups = [(near, 0), (far, 0), (far, 1), (near, 1)]
    inputs = [
        own_near,
        own_far,
        swap(own_far, "expert", 1),
        swap(own_near, "expert", 1),
    ]

    weights = scaled_weights(
        gate_values, up_values, gate_scales, up_scales, index * feat_cols
    )

    hiddens = jnp.zeros((half_line, 2, capacity, half_units), jnp.bfloat16)
    wholes, pieces, landed = [], [], []
    for order, (masks, side) in enumerate(groups):
        rows = len(masks) * capacity
        which = parity ^ side
        partial = jnp.dot(
            inputs[order], weights, preferred_element_type=jnp.float32
        ).astype(jnp.bfloat16)
        if order >= 2:
            partial = earlier(partial, landed[order - 2])
        running = partial
        for step in range(1, half_line):
            came = lax.ppermute(running, "fsdp", towards_middle(n_fsdp, step))
            running = add_rounded(partial, came)
        landed.append(came)
        first, second = running[: rows // 2], running[rows // 2 :]
        kept = jnp.where(keeps_first, first, second)
        came = lax.ppermute(
            jnp.where(keeps_first, second, first), "fsdp", between_middle(n_fsdp)
        )
        pre = kept.astype(jnp.float32) + came.astype(jnp.float32)
        gate_pre = pre[:, :half_units]
        up_pre = pre[:, half_units:]
        owners = [
            chip ^ jnp.where(keeps_first, mask, mask + high_chip)
            for mask in masks[: len(masks) // 2]
        ]
        places = [jnp.where(is_low, owner, n_fsdp - 1 - owner) for owner in owners]
        places = [jnp.clip(place, 0, half_line - 1) for place in places]
        cot = jnp.concatenate([pick(pick(cots, place), which) for place in places], 0)
        cot = cot.astype(jnp.float32)
        sigmoid_gate = jax.nn.sigmoid(gate_pre)
        hidden = (gate_pre * sigmoid_gate * up_pre).astype(jnp.bfloat16)
        grad_gate_pre = cot * up_pre * sigmoid_gate * (1.0 + gate_pre * (1.0 - sigmoid_gate))
        grad_up_pre = cot * gate_pre * sigmoid_gate
        for turn, place in enumerate(places):
            hiddens = lax.dynamic_update_slice(
                hiddens,
                hidden[None, None, turn * capacity : (turn + 1) * capacity],
                (place, which, 0, 0),
            )
        own_grads = jnp.concatenate(
            [grad_gate_pre.astype(jnp.bfloat16), grad_up_pre.astype(jnp.bfloat16)], 1
        )
        came = lax.ppermute(own_grads, "fsdp", between_middle(n_fsdp))
        whole = jnp.where(
            keeps_first,
            jnp.concatenate([own_grads, came], 0),
            jnp.concatenate([came, own_grads], 0),
        )
        for step in range(1, half_line):
            came = lax.ppermute(whole, "fsdp", from_middle(n_fsdp, step))
            here = (index == half_line - 1 - step) | (index == half_line + step)
            whole = jnp.where(here, came, whole)
        wholes.append(whole)
        if order == len(groups) - 1:
            whole = earlier(whole, *pieces)
        back = lax.dot_general(
            whole, weights, (((1,), (1,)), ((), ())), preferred_element_type=jnp.float32
        ).astype(jnp.bfloat16)
        back = back.reshape(len(masks), capacity, feat_cols)
        for turn, mask in enumerate(masks):
            jump = 2 * mask + side
            pieces.append(swap(back[turn], "expert", jump) if jump else back[turn])

    hiddens = earlier(hiddens, wholes[-1])
    hidden = hiddens[half_line - 1]
    for end in range(half_line - 1):
        came = lax.ppermute(
            hiddens[end],
            "fsdp",
            [(target, source) for source, target in to_middle(n_fsdp, end)],
        )
        hidden = jnp.where((index == end) | (index == n_fsdp - 1 - end), came, hidden)
    hidden = hidden.reshape(1, 2 * capacity, half_units)

    all_inputs = jnp.concatenate(inputs, 0)
    all_grads = jnp.concatenate(wholes, 0)

    def weight_grad(columns):
        return lax.dot_general(
            all_inputs,
            all_grads[:, columns],
            (((0,), (0,)), ((), ())),
            preferred_element_type=jnp.float32,
        ).astype(jnp.bfloat16)[None]

    grad_gate = weight_grad(slice(0, half_units))
    grad_up = weight_grad(slice(half_units, None))

    placer = jnp.concatenate(
        [pick(chooser, chip ^ mask) for masks, side in groups for mask in masks], 0
    )
    grad_tokens = lax.dot_general(
        placer,
        jnp.concatenate(pieces, 0),
        (((0,), (0,)), ((), ())),
        preferred_element_type=jnp.float32,
    ).astype(jnp.bfloat16)
    return (hidden, grad_gate, grad_up, grad_tokens)


def solution(mesh):
    in_specs = (
        P("expert", "fsdp"),
        P("expert", None),
        P("expert", "fsdp", None),
        P("expert", "fsdp", None),
        P("expert", None, None),
        P("expert", None, None),
        P("expert", "fsdp", None),
    )
    out_specs = (
        P("expert", "fsdp", None),
        P("expert", "fsdp", None),
        P("expert", "fsdp", None),
        P("expert", "fsdp"),
    )
    return jax.shard_map(
        on_device, mesh=mesh, in_specs=in_specs, out_specs=out_specs, check_vma=False
    )
```

```python
import math

import jax
import jax.numpy as jnp
from jax import lax
from jax.experimental import pallas as pl
from jax.experimental.pallas import tpu as pltpu
from jax.sharding import PartitionSpec as P


def swap(value, axis, mask):
    pairs = [(source, source ^ mask) for source in range(lax.axis_size(axis))]
    return lax.ppermute(value, axis, pairs)


def pick(blocks, index):
    return lax.dynamic_index_in_dim(blocks, index, 0, keepdims=False)


def scale_kernel(sub, start_ref, gate_ref, up_ref, gate_scale_ref, up_scale_ref, out_ref):
    rows, half_units = gate_ref.shape[1:]
    base = start_ref[0] + pl.program_id(0) * rows
    for value_ref, scale_ref, offset in (
        (gate_ref, gate_scale_ref, 0),
        (up_ref, up_scale_ref, half_units),
    ):
        for piece in range(rows // sub):
            block = (base + piece * sub) // 128
            here = slice(piece * sub, (piece + 1) * sub)
            row = jnp.concatenate(
                [jnp.full((1, 128), scale_ref[block, j]) for j in range(half_units // 128)], 1
            )
            scaled = value_ref[0, here, :].astype(jnp.float32) * row
            out_ref[here, offset : offset + half_units] = scaled.astype(jnp.bfloat16)


def scaled_weights(gate_values, up_values, gate_scales, up_scales, start_row):
    feat_cols, half_units = gate_values.shape[1:]
    sub = math.gcd(feat_cols, 128)
    rows = max(r for r in range(sub, 257, sub) if feat_cols % r == 0)
    value_spec = pl.BlockSpec((1, rows, half_units), lambda i, start: (0, i, 0))
    scale_spec = pl.BlockSpec(memory_space=pltpu.SMEM)
    return pl.pallas_call(
        lambda *refs: scale_kernel(sub, *refs),
        out_shape=jax.ShapeDtypeStruct((feat_cols, 2 * half_units), jnp.bfloat16),
        grid_spec=pltpu.PrefetchScalarGridSpec(
            num_scalar_prefetch=1,
            grid=(feat_cols // rows,),
            in_specs=[value_spec, value_spec, scale_spec, scale_spec],
            out_specs=pl.BlockSpec((rows, 2 * half_units), lambda i, start: (i, 0)),
        ),
        compiler_params=pltpu.CompilerParams(vmem_limit_bytes=24 * 2**20),
        cost_estimate=pl.CostEstimate(
            flops=2 * feat_cols * half_units,
            bytes_accessed=8 * feat_cols * half_units,
            transcendentals=0,
        ),
        name="scale_weights",
    )(start_row[None], gate_values, up_values, gate_scales[0], up_scales[0])


def rows_of(counts_ref, expert):
    first = jnp.int32(0)
    live = jnp.int32(0)
    for other in range(counts_ref.shape[1]):
        count = counts_ref[0, other]
        first = first + jnp.where(other < expert, count, 0)
        live = jnp.where(other == expert, count, live)
    return first, live


def pack_kernel(capacity, chip_ref, counts_ref, tokens_ref, out_ref):
    row_total = tokens_ref.shape[0]
    row = lax.broadcasted_iota(jnp.int32, (capacity, row_total), 1)
    slot = lax.broadcasted_iota(jnp.int32, (capacity, row_total), 0)
    hits = []
    for mask in range(out_ref.shape[0] // capacity):
        first, live = rows_of(counts_ref, chip_ref[0] ^ mask)
        hits.append(((row == first + slot) & (slot < live)).astype(jnp.float32))
    chooser = jnp.concatenate(hits, 0).astype(jnp.bfloat16)
    out_ref[...] = jnp.dot(
        chooser, tokens_ref[...], preferred_element_type=jnp.float32
    ).astype(jnp.bfloat16)


def packed_rows(tokens, counts, chip, capacity):
    row_total, feat_cols = tokens.shape
    experts = counts.shape[1]
    smem = pl.BlockSpec(memory_space=pltpu.SMEM)
    vmem = pl.BlockSpec(memory_space=pltpu.VMEM)
    return pl.pallas_call(
        lambda *refs: pack_kernel(capacity, *refs),
        out_shape=jax.ShapeDtypeStruct((experts * capacity, feat_cols), jnp.bfloat16),
        in_specs=[smem, smem, vmem],
        out_specs=vmem,
        cost_estimate=pl.CostEstimate(
            flops=2 * experts * capacity * row_total * feat_cols,
            bytes_accessed=2 * (row_total + experts * capacity) * feat_cols,
            transcendentals=0,
        ),
        name="pack_rows",
    )(chip[None], counts, tokens)


def combine_kernel(masks, chip_ref, counts_ref, *refs):
    piece_refs, out_ref = refs[:-1], refs[-1]
    capacity = piece_refs[0].shape[0]
    row_total = out_ref.shape[0]
    row = lax.broadcasted_iota(jnp.int32, (row_total, capacity), 0)
    slot = lax.broadcasted_iota(jnp.int32, (row_total, capacity), 1)
    total = None
    for mask, piece_ref in zip(masks, piece_refs):
        first, live = rows_of(counts_ref, chip_ref[0] ^ mask)
        placer = ((row == first + slot) & (slot < live)).astype(jnp.bfloat16)
        term = jnp.dot(placer, piece_ref[...], preferred_element_type=jnp.float32)
        total = term if total is None else total + term
    out_ref[...] = total.astype(jnp.bfloat16)


def combined_rows(pieces, masks, counts, chip, row_total):
    capacity, feat_cols = pieces[0].shape
    smem = pl.BlockSpec(memory_space=pltpu.SMEM)
    vmem = pl.BlockSpec(memory_space=pltpu.VMEM)
    return pl.pallas_call(
        lambda *refs: combine_kernel(masks, *refs),
        out_shape=jax.ShapeDtypeStruct((row_total, feat_cols), jnp.bfloat16),
        in_specs=[smem, smem] + [vmem] * len(pieces),
        out_specs=vmem,
        cost_estimate=pl.CostEstimate(
            flops=2 * len(pieces) * capacity * row_total * feat_cols,
            bytes_accessed=2 * (row_total + len(pieces) * capacity) * feat_cols,
            transcendentals=0,
        ),
        name="combine_rows",
    )(chip[None], counts, *pieces)


def weight_kernel(count, *refs):
    input_refs, grad_refs = refs[:count], refs[count : 2 * count]
    gate_ref, up_ref, held = refs[2 * count :]
    rows = input_refs[0].shape[0]
    half_units = gate_ref.shape[2]

    @pl.when(pl.program_id(0) == 0)
    def _():
        for place, grad_ref in enumerate(grad_refs):
            held[place * rows : (place + 1) * rows, :] = grad_ref[...]

    inputs = jnp.concatenate([input_ref[...] for input_ref in input_refs], 0)
    for out_ref, offset in ((gate_ref, 0), (up_ref, half_units)):
        out_ref[0] = lax.dot_general(
            inputs,
            held[:, offset : offset + half_units],
            (((0,), (0,)), ((), ())),
            preferred_element_type=jnp.float32,
        ).astype(jnp.bfloat16)


def weight_grads(inputs, grads):
    count = len(inputs)
    rows, feat_cols = inputs[0].shape
    units = grads[0].shape[1]
    tile = 256 if feat_cols % 256 == 0 else feat_cols
    out = jax.ShapeDtypeStruct((1, feat_cols, units // 2), jnp.bfloat16)
    out_spec = pl.BlockSpec((1, tile, units // 2), lambda i: (0, i, 0))
    return pl.pallas_call(
        lambda *refs: weight_kernel(count, *refs),
        out_shape=(out, out),
        grid=(feat_cols // tile,),
        in_specs=[pl.BlockSpec((rows, tile), lambda i: (0, i))] * count
        + [pl.BlockSpec((rows, units), lambda i: (0, 0))] * count,
        out_specs=(out_spec, out_spec),
        scratch_shapes=[pltpu.VMEM((count * rows, units), jnp.bfloat16)],
        compiler_params=pltpu.CompilerParams(vmem_limit_bytes=32 * 2**20),
        cost_estimate=pl.CostEstimate(
            flops=2 * count * rows * feat_cols * units,
            bytes_accessed=2 * (count * rows * (feat_cols + units) + feat_cols * units),
            transcendentals=0,
        ),
        name="weight_grads",
    )(*inputs, *grads)


def earlier(value, *needed):
    return lax.optimization_barrier((value,) + needed)[0]


def add_rounded(first, second):
    return (first.astype(jnp.float32) + second.astype(jnp.float32)).astype(jnp.bfloat16)


def towards_middle(size, step):
    return [(step - 1, step), (size - step, size - 1 - step)]


def from_middle(size, step):
    return [(target, source) for source, target in towards_middle(size, size // 2 - step)]


def between_middle(size):
    return [(size // 2 - 1, size // 2), (size // 2, size // 2 - 1)]


def to_middle(size, end):
    return [(end, size // 2 - 1), (size - 1 - end, size // 2)]


def on_device(tokens, counts, gate_values, up_values, gate_scales, up_scales, grad_hidden):
    row_total, feat_cols = tokens.shape
    experts = counts.shape[1]
    capacity = min(4 * row_total // experts, row_total // 2)
    n_expert = lax.axis_size("expert")
    n_fsdp = lax.axis_size("fsdp")
    chips = n_expert // 2
    high_chip = chips // 2
    half_line = n_fsdp // 2
    half_units = gate_values.shape[2]
    parity = lax.axis_index("expert") % 2
    chip = lax.axis_index("expert") // 2
    index = lax.axis_index("fsdp")
    is_low = index < half_line
    keeps_first = is_low == (chip < high_chip)

    packed = packed_rows(tokens, counts, chip, capacity)
    packed = packed.reshape(chips, capacity, feat_cols)
    near = [mask for mask in range(high_chip) if mask % 2 == 0]
    far = [mask for mask in range(high_chip) if mask % 2 == 1]
    near = near + [mask + high_chip for mask in near]
    far = far + [mask + high_chip for mask in far]

    def arrive(masks):
        blocks = [
            swap(packed[mask], "expert", 2 * mask) if mask else packed[mask] for mask in masks
        ]
        return jnp.concatenate(blocks, 0)

    own_near, own_far = arrive(near), arrive(far)

    own_cot = earlier(grad_hidden[0].reshape(2, capacity, half_units), packed)
    cots = [
        lax.ppermute(own_cot, "fsdp", to_middle(n_fsdp, end)) for end in range(half_line - 1)
    ]
    cots = jnp.stack(cots + [own_cot])

    weights = scaled_weights(
        gate_values, up_values, gate_scales, up_scales, index * feat_cols
    )

    groups = [(near, 0), (far, 0), (far, 1), (near, 1)]
    inputs = [own_near, own_far, swap(own_far, "expert", 1), swap(own_near, "expert", 1)]
    inputs[2] = earlier(inputs[2], cots)

    hiddens = jnp.zeros((half_line, 2, capacity, half_units), jnp.bfloat16)
    sums = []
    for order in range(len(groups)):
        running = partial = jnp.dot(
            inputs[order], weights, preferred_element_type=jnp.float32
        ).astype(jnp.bfloat16)
        for step in range(1, half_line):
            if step > 1:
                running = add_rounded(partial, came)
            came = lax.ppermute(running, "fsdp", towards_middle(n_fsdp, step))
        sums.append((partial, came))

    wholes, inner, acts, backs, pieces = [], [], [], [], []
    for order, (masks, side) in enumerate(groups):
        rows = len(masks) * capacity
        which = parity ^ side
        partial, came = sums[order]
        if order >= 1:
            came = earlier(came, acts[order - 1])
        running = add_rounded(partial, came)
        first, second = running[: rows // 2], running[rows // 2 :]
        kept = jnp.where(keeps_first, first, second)
        given = jnp.where(keeps_first, second, first)
        if order >= 2:
            given = earlier(given, inner[order - 2])
        came = lax.ppermute(given, "fsdp", between_middle(n_fsdp))
        pre = kept.astype(jnp.float32) + came.astype(jnp.float32)
        gate_pre = pre[:, :half_units]
        up_pre = pre[:, half_units:]
        owners = [
            chip ^ jnp.where(keeps_first, mask, mask + high_chip)
            for mask in masks[: len(masks) // 2]
        ]
        places = [jnp.where(is_low, owner, n_fsdp - 1 - owner) for owner in owners]
        places = [jnp.clip(place, 0, half_line - 1) for place in places]
        cot = jnp.concatenate([pick(pick(cots, place), which) for place in places], 0)
        cot = cot.astype(jnp.float32)
        sigmoid_gate = jax.nn.sigmoid(gate_pre)
        hidden = (gate_pre * sigmoid_gate * up_pre).astype(jnp.bfloat16)
        grad_gate_pre = cot * up_pre * sigmoid_gate * (1.0 + gate_pre * (1.0 - sigmoid_gate))
        grad_up_pre = cot * gate_pre * sigmoid_gate
        for turn, place in enumerate(places):
            hiddens = lax.dynamic_update_slice(
                hiddens,
                hidden[None, None, turn * capacity : (turn + 1) * capacity],
                (place, which, 0, 0),
            )
        own_grads = jnp.concatenate(
            [grad_gate_pre.astype(jnp.bfloat16), grad_up_pre.astype(jnp.bfloat16)], 1
        )
        acts.append(own_grads)
        if order >= 2:
            own_grads = earlier(own_grads, backs[order - 2])
        came = lax.ppermute(own_grads, "fsdp", between_middle(n_fsdp))
        inner.append(came)
        whole = jnp.where(
            keeps_first,
            jnp.concatenate([own_grads, came], 0),
            jnp.concatenate([came, own_grads], 0),
        )
        for step in range(1, half_line):
            came = lax.ppermute(whole, "fsdp", from_middle(n_fsdp, step))
            here = (index == half_line - 1 - step) | (index == half_line + step)
            whole = jnp.where(here, came, whole)
        wholes.append(whole)
        if order == len(groups) - 1:
            whole, *pieces = lax.optimization_barrier((whole, *pieces))
        back = lax.dot_general(
            whole, weights, (((1,), (1,)), ((), ())), preferred_element_type=jnp.float32
        ).astype(jnp.bfloat16)
        backs.append(back)
        back = back.reshape(len(masks), capacity, feat_cols)
        for turn, mask in enumerate(masks):
            jump = 2 * mask + side
            pieces.append(swap(back[turn], "expert", jump) if jump else back[turn])

    hiddens = earlier(hiddens, wholes[-1])
    hidden = hiddens[half_line - 1]
    for end in range(half_line - 1):
        came = lax.ppermute(
            hiddens[end],
            "fsdp",
            [(target, source) for source, target in to_middle(n_fsdp, end)],
        )
        hidden = jnp.where((index == end) | (index == n_fsdp - 1 - end), came, hidden)
    hidden = hidden.reshape(1, 2 * capacity, half_units)

    grad_gate, grad_up = weight_grads(inputs, wholes)
    grad_tokens = combined_rows(
        pieces, [mask for masks, side in groups for mask in masks], counts, chip, row_total
    )
    return (hidden, grad_gate, grad_up, grad_tokens)


def solution(mesh):
    in_specs = (
        P("expert", "fsdp"),
        P("expert", None),
        P("expert", "fsdp", None),
        P("expert", "fsdp", None),
        P("expert", None, None),
        P("expert", None, None),
        P("expert", "fsdp", None),
    )
    out_specs = (
        P("expert", "fsdp", None),
        P("expert", "fsdp", None),
        P("expert", "fsdp", None),
        P("expert", "fsdp"),
    )
    return jax.shard_map(
        on_device, mesh=mesh, in_specs=in_specs, out_specs=out_specs, check_vma=False
    )
```

```python
import math

import jax
import jax.numpy as jnp
from jax import lax
from jax.experimental import pallas as pl
from jax.experimental.pallas import tpu as pltpu
from jax.sharding import PartitionSpec as P


def swap(value, axis, mask):
    pairs = [(source, source ^ mask) for source in range(lax.axis_size(axis))]
    return lax.ppermute(value, axis, pairs)


def pick(blocks, index):
    return lax.dynamic_index_in_dim(blocks, index, 0, keepdims=False)


def scale_kernel(
    sub, start_ref, gate_ref, up_ref, gate_scale_ref, up_scale_ref, out_ref, gate_rows, up_rows
):
    rows, half_units = gate_ref.shape[1:]
    base = start_ref[0] + pl.program_id(0) * rows

    @pl.when(pl.program_id(0) == 0)
    def _():
        for scale_ref, grown in ((gate_scale_ref, gate_rows), (up_scale_ref, up_rows)):
            for j in range(half_units // 128):
                grown[:, j * 128 : (j + 1) * 128] = jnp.broadcast_to(
                    scale_ref[0, :, j : j + 1], (grown.shape[0], 128)
                )

    for value_ref, grown, offset in ((gate_ref, gate_rows, 0), (up_ref, up_rows, half_units)):
        for piece in range(rows // sub):
            block = (base + piece * sub) // 128
            here = slice(piece * sub, (piece + 1) * sub)
            scaled = value_ref[0, here, :].astype(jnp.float32) * grown[pl.ds(block, 1), :]
            out_ref[here, offset : offset + half_units] = scaled.astype(jnp.bfloat16)


def scaled_weights(gate_values, up_values, gate_scales, up_scales, start_row):
    feat_cols, half_units = gate_values.shape[1:]
    sub = math.gcd(feat_cols, 128)
    rows = max(r for r in range(sub, 257, sub) if feat_cols % r == 0)
    value_spec = pl.BlockSpec((1, rows, half_units), lambda i, start: (0, i, 0))
    scale_spec = pl.BlockSpec(gate_scales.shape, lambda i, start: (0, 0, 0))
    grown = pltpu.VMEM((gate_scales.shape[1], half_units), jnp.float32)
    return pl.pallas_call(
        lambda *refs: scale_kernel(sub, *refs),
        out_shape=jax.ShapeDtypeStruct((feat_cols, 2 * half_units), jnp.bfloat16),
        grid_spec=pltpu.PrefetchScalarGridSpec(
            num_scalar_prefetch=1,
            grid=(feat_cols // rows,),
            in_specs=[value_spec, value_spec, scale_spec, scale_spec],
            out_specs=pl.BlockSpec((rows, 2 * half_units), lambda i, start: (i, 0)),
            scratch_shapes=[grown, grown],
        ),
        compiler_params=pltpu.CompilerParams(vmem_limit_bytes=24 * 2**20),
        cost_estimate=pl.CostEstimate(
            flops=2 * feat_cols * half_units,
            bytes_accessed=8 * feat_cols * half_units,
            transcendentals=0,
        ),
        name="scale_weights",
    )(
        start_row[None],
        pltpu.with_memory_space_constraint(gate_values, pltpu.HBM),
        pltpu.with_memory_space_constraint(up_values, pltpu.HBM),
        gate_scales,
        up_scales,
    )


def rows_of(counts_ref, expert):
    first = jnp.int32(0)
    live = jnp.int32(0)
    for other in range(counts_ref.shape[1]):
        count = counts_ref[0, other]
        first = first + jnp.where(other < expert, count, 0)
        live = jnp.where(other == expert, count, live)
    return first, live


def pack_kernel(chip_ref, counts_ref, tokens_ref, *out_refs):
    row_total = tokens_ref.shape[0]
    capacity = out_refs[0].shape[0]
    row = lax.broadcasted_iota(jnp.int32, (capacity, row_total), 1)
    slot = lax.broadcasted_iota(jnp.int32, (capacity, row_total), 0)
    hits = []
    for mask in range(len(out_refs)):
        first, live = rows_of(counts_ref, chip_ref[0] ^ mask)
        hits.append(((row == first + slot) & (slot < live)).astype(jnp.float32))
    chooser = jnp.concatenate(hits, 0).astype(jnp.bfloat16)
    chosen = jnp.dot(chooser, tokens_ref[...], preferred_element_type=jnp.float32)
    for mask, out_ref in enumerate(out_refs):
        out_ref[...] = chosen[mask * capacity : (mask + 1) * capacity].astype(jnp.bfloat16)


def packed_rows(tokens, counts, chip, capacity):
    row_total, feat_cols = tokens.shape
    experts = counts.shape[1]
    smem = pl.BlockSpec(memory_space=pltpu.SMEM)
    vmem = pl.BlockSpec(memory_space=pltpu.VMEM)
    block = jax.ShapeDtypeStruct((capacity, feat_cols), jnp.bfloat16)
    return pl.pallas_call(
        pack_kernel,
        out_shape=(block,) * experts,
        in_specs=[smem, smem, vmem],
        out_specs=(vmem,) * experts,
        cost_estimate=pl.CostEstimate(
            flops=2 * experts * capacity * row_total * feat_cols,
            bytes_accessed=2 * (row_total + experts * capacity) * feat_cols,
            transcendentals=0,
        ),
        name="pack_rows",
    )(chip[None], counts, tokens)


def combine_kernel(masks, chip_ref, counts_ref, *refs):
    piece_refs, out_ref = refs[:-1], refs[-1]
    capacity = piece_refs[0].shape[0]
    row_total = out_ref.shape[0]
    row = lax.broadcasted_iota(jnp.int32, (capacity, row_total), 1)
    slot = lax.broadcasted_iota(jnp.int32, (capacity, row_total), 0)
    hits = []
    for mask in masks:
        first, live = rows_of(counts_ref, chip_ref[0] ^ mask)
        hits.append(((row == first + slot) & (slot < live)).astype(jnp.float32))
    out_ref[...] = lax.dot_general(
        jnp.concatenate(hits, 0).astype(jnp.bfloat16),
        jnp.concatenate([piece_ref[...] for piece_ref in piece_refs], 0),
        (((0,), (0,)), ((), ())),
        preferred_element_type=jnp.float32,
    ).astype(jnp.bfloat16)


def combined_rows(pieces, masks, counts, chip, row_total):
    capacity, feat_cols = pieces[0].shape
    smem = pl.BlockSpec(memory_space=pltpu.SMEM)
    vmem = pl.BlockSpec(memory_space=pltpu.VMEM)
    return pl.pallas_call(
        lambda *refs: combine_kernel(masks, *refs),
        out_shape=jax.ShapeDtypeStruct((row_total, feat_cols), jnp.bfloat16),
        in_specs=[smem, smem] + [vmem] * len(pieces),
        out_specs=vmem,
        cost_estimate=pl.CostEstimate(
            flops=2 * len(pieces) * capacity * row_total * feat_cols,
            bytes_accessed=2 * (row_total + len(pieces) * capacity) * feat_cols,
            transcendentals=0,
        ),
        name="combine_rows",
    )(chip[None], counts, *pieces)


def weight_kernel(count, *refs):
    input_refs, grad_refs = refs[:count], refs[count : 2 * count]
    gate_ref, up_ref, held = refs[2 * count :]
    half_units = gate_ref.shape[2]

    @pl.when(pl.program_id(0) == 0)
    def _():
        place = 0
        for grad_ref in grad_refs:
            held[place : place + grad_ref.shape[0], :] = grad_ref[...]
            place += grad_ref.shape[0]

    inputs = jnp.concatenate([input_ref[...] for input_ref in input_refs], 0)
    for out_ref, offset in ((gate_ref, 0), (up_ref, half_units)):
        out_ref[0] = lax.dot_general(
            inputs,
            held[:, offset : offset + half_units],
            (((0,), (0,)), ((), ())),
            preferred_element_type=jnp.float32,
        ).astype(jnp.bfloat16)


def weight_grads(inputs, grads):
    count = len(inputs)
    rows = sum(value.shape[0] for value in inputs)
    feat_cols = inputs[0].shape[1]
    units = grads[0].shape[1]
    tile = 256 if feat_cols % 256 == 0 else feat_cols
    out = jax.ShapeDtypeStruct((1, feat_cols, units // 2), jnp.bfloat16)
    out_spec = pl.BlockSpec((1, tile, units // 2), lambda i: (0, i, 0))
    return pl.pallas_call(
        lambda *refs: weight_kernel(count, *refs),
        out_shape=(out, out),
        grid=(feat_cols // tile,),
        in_specs=[pl.BlockSpec((value.shape[0], tile), lambda i: (0, i)) for value in inputs]
        + [pl.BlockSpec(value.shape, lambda i: (0, 0)) for value in grads],
        out_specs=(out_spec, out_spec),
        scratch_shapes=[pltpu.VMEM((rows, units), jnp.bfloat16)],
        compiler_params=pltpu.CompilerParams(vmem_limit_bytes=32 * 2**20),
        cost_estimate=pl.CostEstimate(
            flops=2 * rows * feat_cols * units,
            bytes_accessed=2 * (rows * (feat_cols + units) + feat_cols * units),
            transcendentals=0,
        ),
        name="weight_grads",
    )(*inputs, *grads)


def earlier(value, *needed):
    return lax.optimization_barrier((value,) + needed)[0]


def add_rounded(first, second):
    return (first.astype(jnp.float32) + second.astype(jnp.float32)).astype(jnp.bfloat16)


def towards_middle(size, step):
    return [(step - 1, step), (size - step, size - 1 - step)]


def from_middle(size, step):
    return [(target, source) for source, target in towards_middle(size, size // 2 - step)]


def between_middle(size):
    low = size // 2 - 1
    swapped = {low: low + 1, low + 1: low}
    return [(source, swapped.get(source, source)) for source in range(size)]


def to_middle(size, end):
    return [(end, size // 2 - 1), (size - 1 - end, size // 2)]


def on_device(tokens, counts, gate_values, up_values, gate_scales, up_scales, grad_hidden):
    row_total, feat_cols = tokens.shape
    experts = counts.shape[1]
    capacity = min(4 * row_total // experts, row_total // 2)
    n_expert = lax.axis_size("expert")
    n_fsdp = lax.axis_size("fsdp")
    chips = n_expert // 2
    high_chip = chips // 2
    half_line = n_fsdp // 2
    half_units = gate_values.shape[2]
    parity = lax.axis_index("expert") % 2
    chip = lax.axis_index("expert") // 2
    index = lax.axis_index("fsdp")
    is_low = index < half_line
    keeps_first = is_low == (chip < high_chip)

    packed = packed_rows(tokens, counts, chip, capacity)
    near = [mask for mask in range(chips) if mask % 2 == 0]
    far = [mask for mask in range(chips) if mask % 2 == 1]
    blocks = {}
    for mask in near + far:
        blocks[mask, 0] = swap(packed[mask], "expert", 2 * mask) if mask else packed[mask]
    for masks in (far, near):
        there = swap(jnp.concatenate([blocks[mask, 0] for mask in masks], 0), "expert", 1)
        for turn, mask in enumerate(masks):
            blocks[mask, 1] = there[turn * capacity : (turn + 1) * capacity]

    part = capacity // 2
    own_cot = earlier(grad_hidden[0].reshape(2, 2, part, half_units), packed[0])
    cots = [
        lax.ppermute(own_cot, "fsdp", to_middle(n_fsdp, end)) for end in range(half_line - 1)
    ]
    cots = jnp.stack(cots + [own_cot])

    weights = scaled_weights(
        gate_values, up_values, gate_scales, up_scales, index * feat_cols
    )

    units = [
        (mask, side, half)
        for masks, side in ((near, 0), (far, 0), (far, 1), (near, 1))
        for mask in masks
        if mask < high_chip
        for half in range(2)
    ]
    step = len(units) // 8
    bounds = [0, step, 3 * step, 5 * step, 7 * step, 8 * step]
    groups = [units[low:high] for low, high in zip(bounds[:-1], bounds[1:])]

    def blocks_of(group):
        return [unit for unit in group] + [
            (mask + high_chip, side, half) for mask, side, half in group
        ]

    inputs = []
    for group in groups:
        inputs.append(
            jnp.concatenate(
                [
                    blocks[mask, side][half * part : (half + 1) * part]
                    for mask, side, half in blocks_of(group)
                ],
                0,
            )
        )

    hiddens = jnp.zeros((half_line, 2, 2, part, half_units), jnp.bfloat16)
    wholes, inner, acts, backs, pieces, back_parts = [], [], [], [], {}, {}
    sums = None
    for order, group in enumerate(groups):
        if order == 0:
            partials = []
            for place in range(len(groups)):
                values = inputs[place]
                if place == 2:
                    values = earlier(values, cots)
                partials.append(
                    jnp.dot(values, weights, preferred_element_type=jnp.float32).astype(
                        jnp.bfloat16
                    )
                )
        partial = partials[order]
        running = partial if sums is None else earlier(partial, sums)
        for hop in range(1, half_line):
            if hop > 1:
                running = add_rounded(running_base, came)
            running_base = partial
            came = lax.ppermute(running, "fsdp", towards_middle(n_fsdp, hop))
        if order >= 1:
            came = earlier(came, acts[order - 1])
        sums = add_rounded(partial, came)
        rows = sums.shape[0]
        first, second = sums[: rows // 2], sums[rows // 2 :]
        kept = jnp.where(keeps_first, first, second)
        given = jnp.where(keeps_first, second, first)
        if order >= 2:
            given = earlier(given, inner[order - 2])
        came = lax.ppermute(given, "fsdp", between_middle(n_fsdp))
        if order >= 2:
            came = earlier(came, backs[order - 2])
        pre = kept.astype(jnp.float32) + came.astype(jnp.float32)
        gate_pre = pre[:, :half_units]
        up_pre = pre[:, half_units:]
        spots = []
        for mask, side, half in group:
            owner = chip ^ jnp.where(keeps_first, mask, mask + high_chip)
            place = jnp.where(is_low, owner, n_fsdp - 1 - owner)
            spots.append((jnp.clip(place, 0, half_line - 1), parity ^ side, half))
        cot = jnp.concatenate(
            [
                lax.dynamic_slice(
                    cots, (*spot, 0, 0), (1, 1, 1, part, half_units)
                ).reshape(part, half_units)
                for spot in spots
            ],
            0,
        ).astype(jnp.float32)
        sigmoid_gate = jax.nn.sigmoid(gate_pre)
        hidden = (gate_pre * sigmoid_gate * up_pre).astype(jnp.bfloat16)
        grad_gate_pre = cot * up_pre * sigmoid_gate * (1.0 + gate_pre * (1.0 - sigmoid_gate))
        grad_up_pre = cot * gate_pre * sigmoid_gate
        for turn, spot in enumerate(spots):
            hiddens = lax.dynamic_update_slice(
                hiddens,
                hidden[None, None, None, turn * part : (turn + 1) * part],
                (*spot, 0, 0),
            )
        own_grads = jnp.concatenate(
            [grad_gate_pre.astype(jnp.bfloat16), grad_up_pre.astype(jnp.bfloat16)], 1
        )
        acts.append(own_grads)
        came = lax.ppermute(own_grads, "fsdp", between_middle(n_fsdp))
        inner.append(came)
        whole = jnp.where(
            keeps_first,
            jnp.concatenate([own_grads, came], 0),
            jnp.concatenate([came, own_grads], 0),
        )
        for hop in range(1, half_line):
            came = lax.ppermute(whole, "fsdp", from_middle(n_fsdp, hop))
            if order >= 1 and hop == half_line - 1:
                came = earlier(came, backs[order - 1])
                early = [key for key in pieces if key not in fresh]
                came, *held = lax.optimization_barrier((came, *(pieces[key] for key in early)))
                pieces.update(zip(early, held))
            here = (index == half_line - 1 - hop) | (index == half_line + hop)
            whole = jnp.where(here, came, whole)
        wholes.append(whole)
        back = lax.dot_general(
            whole, weights, (((1,), (1,)), ((), ())), preferred_element_type=jnp.float32
        ).astype(jnp.bfloat16)
        backs.append(back)
        fresh = []
        for turn, (mask, side, half) in enumerate(blocks_of(group)):
            back_parts[mask, side, half] = back[turn * part : (turn + 1) * part]
            if half == 1:
                block = jnp.concatenate(
                    [back_parts[mask, side, 0], back_parts[mask, side, 1]], 0
                )
                jump = 2 * mask + side
                pieces[mask, side] = swap(block, "expert", jump) if jump else block
                fresh.append((mask, side))

    hiddens = earlier(hiddens, wholes[-1])
    hidden = hiddens[half_line - 1]
    for end in range(half_line - 1):
        came = lax.ppermute(
            hiddens[end],
            "fsdp",
            [(target, source) for source, target in to_middle(n_fsdp, end)],
        )
        hidden = jnp.where((index == end) | (index == n_fsdp - 1 - end), came, hidden)
    hidden = hidden.reshape(1, 2 * capacity, half_units)

    grad_gate, grad_up = weight_grads(inputs, wholes)
    masks = [mask for mask, side in pieces]
    grad_tokens = combined_rows(list(pieces.values()), masks, counts, chip, row_total)
    return (hidden, grad_gate, grad_up, grad_tokens)


def solution(mesh):
    in_specs = (
        P("expert", "fsdp"),
        P("expert", None),
        P("expert", "fsdp", None),
        P("expert", "fsdp", None),
        P("expert", None, None),
        P("expert", None, None),
        P("expert", "fsdp", None),
    )
    out_specs = (
        P("expert", "fsdp", None),
        P("expert", "fsdp", None),
        P("expert", "fsdp", None),
        P("expert", "fsdp"),
    )
    return jax.shard_map(
        on_device, mesh=mesh, in_specs=in_specs, out_specs=out_specs, check_vma=False
    )
```

```python
import math

import jax
import jax.numpy as jnp
from jax import lax
from jax.experimental import pallas as pl
from jax.experimental.pallas import tpu as pltpu
from jax.sharding import PartitionSpec as P


def swap(value, axis, mask):
    pairs = [(source, source ^ mask) for source in range(lax.axis_size(axis))]
    return lax.ppermute(value, axis, pairs)


def pick(blocks, index):
    return lax.dynamic_index_in_dim(blocks, index, 0, keepdims=False)


def scale_kernel(
    sub,
    start_ref,
    gate_ref,
    up_ref,
    gate_scale_ref,
    up_scale_ref,
    out_ref,
    done_ref,
    gate_rows,
    up_rows,
):
    rows, half_units = gate_ref.shape[1:]
    base = start_ref[0] + pl.program_id(0) * rows

    @pl.when(pl.program_id(0) == 0)
    def _():
        done_ref[...] = jnp.zeros_like(done_ref)
        for scale_ref, grown in ((gate_scale_ref, gate_rows), (up_scale_ref, up_rows)):
            for j in range(half_units // 128):
                grown[:, j * 128 : (j + 1) * 128] = jnp.broadcast_to(
                    scale_ref[0, :, j : j + 1], (grown.shape[0], 128)
                )

    for value_ref, grown, offset in ((gate_ref, gate_rows, 0), (up_ref, up_rows, half_units)):
        for piece in range(rows // sub):
            block = (base + piece * sub) // 128
            here = slice(piece * sub, (piece + 1) * sub)
            scaled = value_ref[0, here, :].astype(jnp.float32) * grown[pl.ds(block, 1), :]
            out_ref[here, offset : offset + half_units] = scaled.astype(jnp.bfloat16)


def scaled_weights(gate_values, up_values, gate_scales, up_scales, start_row):
    feat_cols, half_units = gate_values.shape[1:]
    sub = math.gcd(feat_cols, 128)
    rows = max(r for r in range(sub, 257, sub) if feat_cols % r == 0)
    value_spec = pl.BlockSpec((1, rows, half_units), lambda i, start: (0, i, 0))
    scale_spec = pl.BlockSpec(gate_scales.shape, lambda i, start: (0, 0, 0))
    grown = pltpu.VMEM((gate_scales.shape[1], half_units), jnp.float32)
    return pl.pallas_call(
        lambda *refs: scale_kernel(sub, *refs),
        out_shape=(
            jax.ShapeDtypeStruct((feat_cols, 2 * half_units), jnp.bfloat16),
            jax.ShapeDtypeStruct((8, 128), jnp.float32),
        ),
        grid_spec=pltpu.PrefetchScalarGridSpec(
            num_scalar_prefetch=1,
            grid=(feat_cols // rows,),
            in_specs=[value_spec, value_spec, scale_spec, scale_spec],
            out_specs=(
                pl.BlockSpec((rows, 2 * half_units), lambda i, start: (i, 0)),
                pl.BlockSpec((8, 128), lambda i, start: (0, 0)),
            ),
            scratch_shapes=[grown, grown],
        ),
        compiler_params=pltpu.CompilerParams(vmem_limit_bytes=24 * 2**20),
        cost_estimate=pl.CostEstimate(
            flops=2 * feat_cols * half_units,
            bytes_accessed=8 * feat_cols * half_units,
            transcendentals=0,
        ),
        name="scale_weights",
    )(
        start_row[None],
        pltpu.with_memory_space_constraint(gate_values, pltpu.HBM),
        pltpu.with_memory_space_constraint(up_values, pltpu.HBM),
        gate_scales,
        up_scales,
    )


def rows_of(counts_ref, expert):
    first = jnp.int32(0)
    live = jnp.int32(0)
    for other in range(counts_ref.shape[1]):
        count = counts_ref[0, other]
        first = first + jnp.where(other < expert, count, 0)
        live = jnp.where(other == expert, count, live)
    return first, live


def pack_kernel(chip_ref, counts_ref, tokens_ref, *out_refs):
    row_total = tokens_ref.shape[0]
    capacity = out_refs[0].shape[0]
    row = lax.broadcasted_iota(jnp.int32, (capacity, row_total), 1)
    slot = lax.broadcasted_iota(jnp.int32, (capacity, row_total), 0)
    hits = []
    for mask in range(len(out_refs)):
        first, live = rows_of(counts_ref, chip_ref[0] ^ mask)
        hits.append(((row == first + slot) & (slot < live)).astype(jnp.float32))
    chooser = jnp.concatenate(hits, 0).astype(jnp.bfloat16)
    chosen = jnp.dot(chooser, tokens_ref[...], preferred_element_type=jnp.float32)
    for mask, out_ref in enumerate(out_refs):
        out_ref[...] = chosen[mask * capacity : (mask + 1) * capacity].astype(jnp.bfloat16)


def packed_rows(tokens, counts, chip, capacity):
    row_total, feat_cols = tokens.shape
    experts = counts.shape[1]
    smem = pl.BlockSpec(memory_space=pltpu.SMEM)
    vmem = pl.BlockSpec(memory_space=pltpu.VMEM)
    block = jax.ShapeDtypeStruct((capacity, feat_cols), jnp.bfloat16)
    return pl.pallas_call(
        pack_kernel,
        out_shape=(block,) * experts,
        in_specs=[smem, smem, vmem],
        out_specs=(vmem,) * experts,
        cost_estimate=pl.CostEstimate(
            flops=2 * experts * capacity * row_total * feat_cols,
            bytes_accessed=2 * (row_total + experts * capacity) * feat_cols,
            transcendentals=0,
        ),
        name="pack_rows",
    )(chip[None], counts, tokens)


def combine_kernel(masks, chip_ref, counts_ref, *refs):
    piece_refs, out_ref = refs[:-1], refs[-1]
    capacity = piece_refs[0].shape[0]
    row_total = out_ref.shape[0]
    row = lax.broadcasted_iota(jnp.int32, (capacity, row_total), 1)
    slot = lax.broadcasted_iota(jnp.int32, (capacity, row_total), 0)
    hits = []
    for mask in masks:
        first, live = rows_of(counts_ref, chip_ref[0] ^ mask)
        hits.append(((row == first + slot) & (slot < live)).astype(jnp.float32))
    out_ref[...] = lax.dot_general(
        jnp.concatenate(hits, 0).astype(jnp.bfloat16),
        jnp.concatenate([piece_ref[...] for piece_ref in piece_refs], 0),
        (((0,), (0,)), ((), ())),
        preferred_element_type=jnp.float32,
    ).astype(jnp.bfloat16)


def combined_rows(pieces, masks, counts, chip, row_total):
    capacity, feat_cols = pieces[0].shape
    smem = pl.BlockSpec(memory_space=pltpu.SMEM)
    vmem = pl.BlockSpec(memory_space=pltpu.VMEM)
    return pl.pallas_call(
        lambda *refs: combine_kernel(masks, *refs),
        out_shape=jax.ShapeDtypeStruct((row_total, feat_cols), jnp.bfloat16),
        in_specs=[smem, smem] + [vmem] * len(pieces),
        out_specs=vmem,
        cost_estimate=pl.CostEstimate(
            flops=2 * len(pieces) * capacity * row_total * feat_cols,
            bytes_accessed=2 * (row_total + len(pieces) * capacity) * feat_cols,
            transcendentals=0,
        ),
        name="combine_rows",
    )(chip[None], counts, *pieces)


def weight_kernel(count, *refs):
    input_refs, grad_refs = refs[:count], refs[count : 2 * count]
    gate_ref, up_ref, held = refs[2 * count :]
    half_units = gate_ref.shape[2]

    @pl.when(pl.program_id(0) == 0)
    def _():
        place = 0
        for grad_ref in grad_refs:
            held[place : place + grad_ref.shape[0], :] = grad_ref[...]
            place += grad_ref.shape[0]

    inputs = jnp.concatenate([input_ref[...] for input_ref in input_refs], 0)
    for out_ref, offset in ((gate_ref, 0), (up_ref, half_units)):
        out_ref[0] = lax.dot_general(
            inputs,
            held[:, offset : offset + half_units],
            (((0,), (0,)), ((), ())),
            preferred_element_type=jnp.float32,
        ).astype(jnp.bfloat16)


def weight_grads(inputs, grads):
    count = len(inputs)
    rows = sum(value.shape[0] for value in inputs)
    feat_cols = inputs[0].shape[1]
    units = grads[0].shape[1]
    tile = 256 if feat_cols % 256 == 0 else feat_cols
    out = jax.ShapeDtypeStruct((1, feat_cols, units // 2), jnp.bfloat16)
    out_spec = pl.BlockSpec((1, tile, units // 2), lambda i: (0, i, 0))
    return pl.pallas_call(
        lambda *refs: weight_kernel(count, *refs),
        out_shape=(out, out),
        grid=(feat_cols // tile,),
        in_specs=[pl.BlockSpec((value.shape[0], tile), lambda i: (0, i)) for value in inputs]
        + [pl.BlockSpec(value.shape, lambda i: (0, 0)) for value in grads],
        out_specs=(out_spec, out_spec),
        scratch_shapes=[pltpu.VMEM((rows, units), jnp.bfloat16)],
        compiler_params=pltpu.CompilerParams(vmem_limit_bytes=32 * 2**20),
        cost_estimate=pl.CostEstimate(
            flops=2 * rows * feat_cols * units,
            bytes_accessed=2 * (rows * (feat_cols + units) + feat_cols * units),
            transcendentals=0,
        ),
        name="weight_grads",
    )(*inputs, *grads)


def earlier(value, *needed):
    return lax.optimization_barrier((value,) + needed)[0]


def add_rounded(first, second):
    return (first.astype(jnp.float32) + second.astype(jnp.float32)).astype(jnp.bfloat16)


def on_device(tokens, counts, gate_values, up_values, gate_scales, up_scales, grad_hidden):
    row_total, feat_cols = tokens.shape
    experts = counts.shape[1]
    capacity = min(4 * row_total // experts, row_total // 2)
    n_expert = lax.axis_size("expert")
    n_fsdp = lax.axis_size("fsdp")
    chips = n_expert // 2
    half_units = gate_values.shape[2]
    parity = lax.axis_index("expert") % 2
    chip = lax.axis_index("expert") // 2
    index = lax.axis_index("fsdp")
    ring = [(source, (source + 1) % n_fsdp) for source in range(n_fsdp)]

    def before(steps):
        return lax.rem(index + n_fsdp - steps, n_fsdp)

    packed = packed_rows(tokens, counts, chip, capacity)
    weights, scaled = scaled_weights(
        gate_values, up_values, gate_scales, up_scales, index * feat_cols
    )
    arrived = [swap(packed[mask], "expert", 2 * mask + 1) for mask in range(chips)]
    other = jnp.concatenate([earlier(rows, scaled) for rows in arrived], 0)
    inputs = [other, swap(other, "expert", 1)]
    cots = grad_hidden[0].reshape(2, capacity, half_units)

    def block(partial, owner):
        return pick(partial, owner ^ chip)

    partials, running, came = [], [], [None, None]
    for values in inputs:
        partial = jnp.dot(values, weights, preferred_element_type=jnp.float32)
        partial = partial.astype(jnp.bfloat16).reshape(chips, capacity, 2 * half_units)
        partials.append(partial)
        running.append(block(partial, before(1)))

    for step in range(1, n_fsdp):
        for group in range(2):
            came[group] = lax.ppermute(running[group], "fsdp", ring)
        if step == n_fsdp - 1:
            break
        for group in range(2):
            came[group] = earlier(came[group], running[1 - group])
            running[group] = add_rounded(
                block(partials[group], before(step + 1)), came[group]
            )

    hiddens, grads = [], []
    for group in range(2):
        if group:
            came[group] = earlier(came[group], grads[0])
        pre = block(partials[group], index).astype(jnp.float32) + came[group].astype(
            jnp.float32
        )
        gate_pre = pre[:, :half_units]
        up_pre = pre[:, half_units:]
        cot = pick(cots, parity ^ (1 - group)).astype(jnp.float32)
        sigmoid_gate = jax.nn.sigmoid(gate_pre)
        hiddens.append((gate_pre * sigmoid_gate * up_pre).astype(jnp.bfloat16))
        grad_gate_pre = cot * up_pre * sigmoid_gate * (1.0 + gate_pre * (1.0 - sigmoid_gate))
        grad_up_pre = cot * gate_pre * sigmoid_gate
        grads.append(
            jnp.concatenate(
                [grad_gate_pre.astype(jnp.bfloat16), grad_up_pre.astype(jnp.bfloat16)], 1
            )
        )
    hidden = jnp.where(
        parity == 0, jnp.stack([hiddens[1], hiddens[0]]), jnp.stack(hiddens)
    ).reshape(1, 2 * capacity, half_units)

    wholes, moving = [], list(grads)
    for group in range(2):
        whole = jnp.zeros((chips, capacity, 2 * half_units), jnp.bfloat16)
        wholes.append(lax.dynamic_update_index_in_dim(whole, grads[group], index ^ chip, 0))
    for step in range(1, n_fsdp):
        for group in range(2):
            if step == 2 and group == 0:
                moving[0] = earlier(moving[0], grads[1])
            if step == n_fsdp - 1 and group == 1:
                wholes[0] = earlier(wholes[0], moving[1])
            moving[group] = lax.ppermute(moving[group], "fsdp", ring)
            wholes[group] = lax.dynamic_update_index_in_dim(
                wholes[group], moving[group], before(step) ^ chip, 0
            )
    wholes = [whole.reshape(chips * capacity, 2 * half_units) for whole in wholes]

    def back(whole):
        return lax.dot_general(
            whole, weights, (((1,), (1,)), ((), ())), preferred_element_type=jnp.float32
        ).astype(jnp.bfloat16)

    taken = swap(back(wholes[0]), "expert", 1)
    kept = back(earlier(wholes[1], taken))
    pieces = []
    for mask in range(chips):
        rows = slice(mask * capacity, (mask + 1) * capacity)
        both = add_rounded(kept[rows], taken[rows])
        pieces.append(swap(both, "expert", 2 * mask) if mask else both)

    grad_gate, grad_up = weight_grads(inputs, wholes)
    grad_tokens = combined_rows(pieces, list(range(chips)), counts, chip, row_total)
    return (hidden, grad_gate, grad_up, grad_tokens)


def solution(mesh):
    in_specs = (
        P("expert", "fsdp"),
        P("expert", None),
        P("expert", "fsdp", None),
        P("expert", "fsdp", None),
        P("expert", None, None),
        P("expert", None, None),
        P("expert", "fsdp", None),
    )
    out_specs = (
        P("expert", "fsdp", None),
        P("expert", "fsdp", None),
        P("expert", "fsdp", None),
        P("expert", "fsdp"),
    )
    return jax.shard_map(
        on_device, mesh=mesh, in_specs=in_specs, out_specs=out_specs, check_vma=False
    )
```

```python
import math

import jax
import jax.numpy as jnp
from jax import lax
from jax.experimental import pallas as pl
from jax.experimental.pallas import tpu as pltpu
from jax.sharding import PartitionSpec as P


def swap(value, axis, mask):
    pairs = [(source, source ^ mask) for source in range(lax.axis_size(axis))]
    return lax.ppermute(value, axis, pairs)


def pick(blocks, index):
    return lax.dynamic_index_in_dim(blocks, index, 0, keepdims=False)


def scale_kernel(
    sub,
    start_ref,
    gate_ref,
    up_ref,
    gate_scale_ref,
    up_scale_ref,
    out_ref,
    gate_rows,
    up_rows,
):
    rows, half_units = gate_ref.shape[1:]
    base = start_ref[0] + pl.program_id(0) * rows

    @pl.when(pl.program_id(0) == 0)
    def _():
        for scale_ref, grown in ((gate_scale_ref, gate_rows), (up_scale_ref, up_rows)):
            for j in range(half_units // 128):
                grown[:, j * 128 : (j + 1) * 128] = jnp.broadcast_to(
                    scale_ref[0, :, j : j + 1], (grown.shape[0], 128)
                )

    for value_ref, grown, offset in ((gate_ref, gate_rows, 0), (up_ref, up_rows, half_units)):
        for piece in range(rows // sub):
            block = (base + piece * sub) // 128
            here = slice(piece * sub, (piece + 1) * sub)
            scaled = value_ref[0, here, :].astype(jnp.float32) * grown[pl.ds(block, 1), :]
            out_ref[here, offset : offset + half_units] = scaled.astype(jnp.bfloat16)


def scaled_weights(gate_values, up_values, gate_scales, up_scales, start_row):
    feat_cols, half_units = gate_values.shape[1:]
    sub = math.gcd(feat_cols, 128)
    rows = max(r for r in range(sub, 257, sub) if feat_cols % r == 0)
    value_spec = pl.BlockSpec((1, rows, half_units), lambda i, start: (0, i, 0))
    scale_spec = pl.BlockSpec(gate_scales.shape, lambda i, start: (0, 0, 0))
    grown = pltpu.VMEM((gate_scales.shape[1], half_units), jnp.float32)
    return pl.pallas_call(
        lambda *refs: scale_kernel(sub, *refs),
        out_shape=jax.ShapeDtypeStruct((feat_cols, 2 * half_units), jnp.bfloat16),
        grid_spec=pltpu.PrefetchScalarGridSpec(
            num_scalar_prefetch=1,
            grid=(feat_cols // rows,),
            in_specs=[value_spec, value_spec, scale_spec, scale_spec],
            out_specs=pl.BlockSpec((rows, 2 * half_units), lambda i, start: (i, 0)),
            scratch_shapes=[grown, grown],
        ),
        compiler_params=pltpu.CompilerParams(vmem_limit_bytes=24 * 2**20),
        cost_estimate=pl.CostEstimate(
            flops=2 * feat_cols * half_units,
            bytes_accessed=8 * feat_cols * half_units,
            transcendentals=0,
        ),
        name="scale_weights",
    )(
        start_row[None],
        pltpu.with_memory_space_constraint(gate_values, pltpu.HBM),
        pltpu.with_memory_space_constraint(up_values, pltpu.HBM),
        gate_scales,
        up_scales,
    )


def rows_of(counts_ref, expert):
    first = jnp.int32(0)
    live = jnp.int32(0)
    for other in range(counts_ref.shape[1]):
        count = counts_ref[0, other]
        first = first + jnp.where(other < expert, count, 0)
        live = jnp.where(other == expert, count, live)
    return first, live


def choosers(where_ref, counts_ref, count, capacity, row_total):
    chip, index = where_ref[0], where_ref[1]
    row = lax.broadcasted_iota(jnp.int32, (capacity, row_total), 1)
    slot = lax.broadcasted_iota(jnp.int32, (capacity, row_total), 0)
    hits = []
    for step in range(1, count + 1):
        first, live = rows_of(counts_ref, chip ^ lax.rem(index + count - step, count))
        hits.append(((row == first + slot) & (slot < live)).astype(jnp.float32))
    return jnp.concatenate(hits, 0).astype(jnp.bfloat16)


def pack_kernel(where_ref, counts_ref, tokens_ref, *out_refs):
    capacity = out_refs[0].shape[0]
    chosen = jnp.dot(
        choosers(where_ref, counts_ref, len(out_refs), capacity, tokens_ref.shape[0]),
        tokens_ref[...],
        preferred_element_type=jnp.float32,
    )
    for place, out_ref in enumerate(out_refs):
        out_ref[...] = chosen[place * capacity : (place + 1) * capacity].astype(jnp.bfloat16)


def packed_rows(tokens, counts, where, capacity):
    row_total, feat_cols = tokens.shape
    experts = counts.shape[1]
    smem = pl.BlockSpec(memory_space=pltpu.SMEM)
    vmem = pl.BlockSpec(memory_space=pltpu.VMEM)
    block = jax.ShapeDtypeStruct((capacity, feat_cols), jnp.bfloat16)
    return pl.pallas_call(
        pack_kernel,
        out_shape=(block,) * experts,
        in_specs=[smem, smem, vmem],
        out_specs=(vmem,) * experts,
        cost_estimate=pl.CostEstimate(
            flops=2 * experts * capacity * row_total * feat_cols,
            bytes_accessed=2 * (row_total + experts * capacity) * feat_cols,
            transcendentals=0,
        ),
        name="pack_rows",
    )(where, counts, tokens)


def combine_kernel(where_ref, counts_ref, *refs):
    piece_refs, out_ref = refs[:-1], refs[-1]
    capacity = piece_refs[0].shape[0]
    out_ref[...] = lax.dot_general(
        choosers(where_ref, counts_ref, len(piece_refs), capacity, out_ref.shape[0]),
        jnp.concatenate([piece_ref[...] for piece_ref in piece_refs], 0),
        (((0,), (0,)), ((), ())),
        preferred_element_type=jnp.float32,
    ).astype(jnp.bfloat16)


def combined_rows(pieces, counts, where, row_total):
    capacity, feat_cols = pieces[0].shape
    smem = pl.BlockSpec(memory_space=pltpu.SMEM)
    vmem = pl.BlockSpec(memory_space=pltpu.VMEM)
    return pl.pallas_call(
        combine_kernel,
        out_shape=jax.ShapeDtypeStruct((row_total, feat_cols), jnp.bfloat16),
        in_specs=[smem, smem] + [vmem] * len(pieces),
        out_specs=vmem,
        cost_estimate=pl.CostEstimate(
            flops=2 * len(pieces) * capacity * row_total * feat_cols,
            bytes_accessed=2 * (row_total + len(pieces) * capacity) * feat_cols,
            transcendentals=0,
        ),
        name="combine_rows",
    )(where, counts, *pieces)


def weight_kernel(count, *refs):
    input_refs, grad_refs = refs[:count], refs[count : 2 * count]
    gate_ref, up_ref, held = refs[2 * count :]
    half_units = gate_ref.shape[2]

    @pl.when(pl.program_id(0) == 0)
    def _():
        place = 0
        for grad_ref in grad_refs:
            held[place : place + grad_ref.shape[0], :] = grad_ref[...]
            place += grad_ref.shape[0]

    inputs = jnp.concatenate([input_ref[...] for input_ref in input_refs], 0)
    for out_ref, offset in ((gate_ref, 0), (up_ref, half_units)):
        out_ref[0] = lax.dot_general(
            inputs,
            held[:, offset : offset + half_units],
            (((0,), (0,)), ((), ())),
            preferred_element_type=jnp.float32,
        ).astype(jnp.bfloat16)


def weight_grads(inputs, grads):
    count = len(inputs)
    rows = sum(value.shape[0] for value in inputs)
    feat_cols = inputs[0].shape[1]
    units = grads[0].shape[1]
    tile = 256 if feat_cols % 256 == 0 else feat_cols
    out = jax.ShapeDtypeStruct((1, feat_cols, units // 2), jnp.bfloat16)
    out_spec = pl.BlockSpec((1, tile, units // 2), lambda i: (0, i, 0))
    return pl.pallas_call(
        lambda *refs: weight_kernel(count, *refs),
        out_shape=(out, out),
        grid=(feat_cols // tile,),
        in_specs=[pl.BlockSpec((value.shape[0], tile), lambda i: (0, i)) for value in inputs]
        + [pl.BlockSpec(value.shape, lambda i: (0, 0)) for value in grads],
        out_specs=(out_spec, out_spec),
        scratch_shapes=[pltpu.VMEM((rows, units), jnp.bfloat16)],
        compiler_params=pltpu.CompilerParams(vmem_limit_bytes=32 * 2**20),
        cost_estimate=pl.CostEstimate(
            flops=2 * rows * feat_cols * units,
            bytes_accessed=2 * (rows * (feat_cols + units) + feat_cols * units),
            transcendentals=0,
        ),
        name="weight_grads",
    )(*inputs, *grads)


def earlier(value, *needed):
    return lax.optimization_barrier((value,) + needed)[0]


def add_rounded(first, second):
    return (first.astype(jnp.float32) + second.astype(jnp.float32)).astype(jnp.bfloat16)


def move(value, target):
    n_expert, n_fsdp = lax.axis_size("expert"), lax.axis_size("fsdp")
    pairs = []
    for expert in range(n_expert):
        for index in range(n_fsdp):
            to_expert, to_index = target(expert, index)
            pairs.append((expert * n_fsdp + index, to_expert * n_fsdp + to_index))
    return lax.ppermute(value, ("expert", "fsdp"), pairs)


def on_device(tokens, counts, gate_values, up_values, gate_scales, up_scales, grad_hidden):
    row_total, feat_cols = tokens.shape
    experts = counts.shape[1]
    capacity = min(4 * row_total // experts, row_total // 2)
    n_fsdp = lax.axis_size("fsdp")
    half_units = gate_values.shape[2]
    parity = lax.axis_index("expert") % 2
    chip = lax.axis_index("expert") // 2
    index = lax.axis_index("fsdp")
    where = jnp.stack([chip, index])
    ring = [(source, (source + 1) % n_fsdp) for source in range(n_fsdp)]
    steps = range(1, n_fsdp + 1)

    packed = packed_rows(tokens, counts, where, capacity)
    weights = scaled_weights(
        gate_values, up_values, gate_scales, up_scales, index * feat_cols
    )
    cots = move(
        earlier(grad_hidden[0].reshape(2, capacity, half_units), packed[0]),
        lambda expert, place: (expert, place ^ (expert // 2)),
    )
    inputs, partials = ({}, {}), ({}, {})
    for step in steps:
        rows = packed[step - 1]
        if step > 2:
            rows = earlier(rows, partials[1][1] if step == 3 else partials[0][step - 2])
        rows = move(
            rows,
            lambda expert, place: (expert ^ (2 * ((place - step) % n_fsdp)) ^ 1, place),
        )
        if step == 1:
            rows, weights = lax.optimization_barrier((rows, weights))
        inputs[0][step] = rows
        inputs[1][step] = swap(rows, "expert", 1)
        for group in range(2):
            partials[group][step] = lax.optimization_barrier(
                jnp.dot(
                    inputs[group][step], weights, preferred_element_type=jnp.float32
                ).astype(jnp.bfloat16)
            )

    running = [partials[group][1] for group in range(2)]
    came = [None, None]
    for step in steps[:-1]:
        for group in range(2):
            came[group] = lax.ppermute(running[group], "fsdp", ring)
        if step == n_fsdp - 1:
            break
        for group in range(2):
            needed = (running[1 - group],)
            if step == 1 and group == 0:
                needed += (cots,)
            came[group] = earlier(came[group], *needed)
            running[group] = add_rounded(partials[group][step + 1], came[group])

    hiddens, grads = [], ({}, {})
    for group in range(2):
        came[group] = earlier(came[group], running[1] if group == 0 else grads[0][n_fsdp])
        pre = partials[group][n_fsdp].astype(jnp.float32) + came[group].astype(jnp.float32)
        gate_pre = pre[:, :half_units]
        up_pre = pre[:, half_units:]
        cot = pick(cots, parity ^ (1 - group)).astype(jnp.float32)
        sigmoid_gate = jax.nn.sigmoid(gate_pre)
        hiddens.append((gate_pre * sigmoid_gate * up_pre).astype(jnp.bfloat16))
        grad_gate_pre = cot * up_pre * sigmoid_gate * (1.0 + gate_pre * (1.0 - sigmoid_gate))
        grad_up_pre = cot * gate_pre * sigmoid_gate
        grads[group][n_fsdp] = jnp.concatenate(
            [grad_gate_pre.astype(jnp.bfloat16), grad_up_pre.astype(jnp.bfloat16)], 1
        )

    moving = [grads[group][n_fsdp] for group in range(2)]
    for step in steps[:-1]:
        if step > 1:
            moving[0] = earlier(moving[0], grads[1][n_fsdp if step == 2 else step - 2])
            moving[1] = earlier(moving[1], grads[0][step - 1])
        for group in range(2):
            moving[group] = lax.ppermute(moving[group], "fsdp", ring)
            grads[group][step] = moving[group]

    def back(value):
        return lax.dot_general(
            value, weights, (((1,), (1,)), ((), ())), preferred_element_type=jnp.float32
        ).astype(jnp.bfloat16)

    pieces = {}
    for step in (n_fsdp, *steps[:-1]):
        taken = swap(back(earlier(grads[0][step], grads[1][step])), "expert", 1)
        value = grads[1][step]
        if step != n_fsdp - 1:
            value = earlier(value, grads[0][step % n_fsdp + 1])
        both = add_rounded(back(value), taken)
        pieces[step] = move(
            both, lambda expert, place: (expert ^ (2 * ((place - step) % n_fsdp)), place)
        )

    hidden = jnp.where(
        parity == 0, jnp.stack([hiddens[1], hiddens[0]]), jnp.stack(hiddens)
    )
    hidden = move(
        earlier(hidden, grads[1][n_fsdp - 1]),
        lambda expert, place: (expert, place ^ (expert // 2)),
    ).reshape(1, 2 * capacity, half_units)

    grad_gate, grad_up = weight_grads(
        [inputs[group][step] for group in range(2) for step in steps],
        [grads[group][step] for group in range(2) for step in steps],
    )
    grad_tokens = combined_rows([pieces[step] for step in steps], counts, where, row_total)
    return (hidden, grad_gate, grad_up, grad_tokens)


def solution(mesh):
    in_specs = (
        P("expert", "fsdp"),
        P("expert", None),
        P("expert", "fsdp", None),
        P("expert", "fsdp", None),
        P("expert", None, None),
        P("expert", None, None),
        P("expert", "fsdp", None),
    )
    out_specs = (
        P("expert", "fsdp", None),
        P("expert", "fsdp", None),
        P("expert", "fsdp", None),
        P("expert", "fsdp"),
    )
    return jax.shard_map(
        on_device, mesh=mesh, in_specs=in_specs, out_specs=out_specs, check_vma=False
    )
```

```python
import math

import jax
import jax.numpy as jnp
from jax import lax
from jax.experimental import pallas as pl
from jax.experimental.pallas import tpu as pltpu
from jax.sharding import PartitionSpec as P


def swap(value, axis, mask):
    pairs = [(source, source ^ mask) for source in range(lax.axis_size(axis))]
    return lax.ppermute(value, axis, pairs)


def pick(blocks, index):
    return lax.dynamic_index_in_dim(blocks, index, 0, keepdims=False)


def scale_kernel(
    sub,
    start_ref,
    gate_ref,
    up_ref,
    gate_scale_ref,
    up_scale_ref,
    out_ref,
    gate_held,
    up_held,
    gate_rows,
    up_rows,
    sems,
):
    rows = out_ref.shape[0]
    half_units = gate_held.shape[1]
    step = pl.program_id(0)

    def arrival(which, turn):
        here = pl.ds(pl.multiple_of(turn * rows, rows), rows)
        value_ref, held = ((gate_ref, gate_held), (up_ref, up_held))[which]
        return pltpu.make_async_copy(
            value_ref.at[0, here, :], held.at[here, :], sems.at[which, turn]
        )

    @pl.when(step == 0)
    def _():
        for turn in range(gate_held.shape[0] // rows):
            for which in range(2):
                arrival(which, turn).start()
        shape = (gate_scale_ref.shape[1], half_units)
        spread = (
            lax.broadcasted_iota(jnp.int32, shape, 0)
            == lax.broadcasted_iota(jnp.int32, shape, 1) // 128
        ).astype(jnp.float32)
        for scale_ref, grown in ((gate_scale_ref, gate_rows), (up_scale_ref, up_rows)):
            grown[...] = lax.dot_general(
                scale_ref[0],
                spread,
                (((0,), (0,)), ((), ())),
                precision=lax.Precision.HIGHEST,
                preferred_element_type=jnp.float32,
            )

    for which, held, grown in ((0, gate_held, gate_rows), (1, up_held, up_rows)):
        arrival(which, step).wait()
        for piece in range(rows // sub):
            block = (start_ref[0] + step * rows + piece * sub) // 128
            there = pl.ds(pl.multiple_of(step * rows + piece * sub, sub), sub)
            scaled = held[there, :].astype(jnp.float32) * grown[pl.ds(block, 1), :]
            out_ref[piece * sub : (piece + 1) * sub, which * half_units : (which + 1) * half_units] = (
                scaled.astype(jnp.bfloat16)
            )


def scaled_weights(gate_values, up_values, gate_scales, up_scales, start_row):
    feat_cols, half_units = gate_values.shape[1:]
    sub = math.gcd(feat_cols, 128)
    rows = max(r for r in range(sub, 257, sub) if feat_cols % r == 0)
    gate_scales, up_scales = (jnp.swapaxes(value, 1, 2) for value in (gate_scales, up_scales))
    any_spec = pl.BlockSpec(memory_space=pl.ANY)
    scale_spec = pl.BlockSpec(gate_scales.shape, lambda i, start: (0, 0, 0))
    held = pltpu.VMEM((feat_cols, half_units), jnp.bfloat16)
    grown = pltpu.VMEM((gate_scales.shape[2], half_units), jnp.float32)
    return pl.pallas_call(
        lambda *refs: scale_kernel(sub, *refs),
        out_shape=jax.ShapeDtypeStruct((feat_cols, 2 * half_units), jnp.bfloat16),
        grid_spec=pltpu.PrefetchScalarGridSpec(
            num_scalar_prefetch=1,
            grid=(feat_cols // rows,),
            in_specs=[any_spec, any_spec, scale_spec, scale_spec],
            out_specs=pl.BlockSpec((rows, 2 * half_units), lambda i, start: (i, 0)),
            scratch_shapes=[
                held,
                held,
                grown,
                grown,
                pltpu.SemaphoreType.DMA((2, feat_cols // rows)),
            ],
        ),
        compiler_params=pltpu.CompilerParams(vmem_limit_bytes=24 * 2**20),
        cost_estimate=pl.CostEstimate(
            flops=2 * feat_cols * half_units,
            bytes_accessed=8 * feat_cols * half_units,
            transcendentals=0,
        ),
        name="scale_weights",
    )(
        start_row[None],
        pltpu.with_memory_space_constraint(gate_values, pltpu.HBM),
        pltpu.with_memory_space_constraint(up_values, pltpu.HBM),
        gate_scales,
        up_scales,
    )


def rows_of(counts_ref, expert):
    first = jnp.int32(0)
    live = jnp.int32(0)
    for other in range(counts_ref.shape[1]):
        count = counts_ref[0, other]
        first = first + jnp.where(other < expert, count, 0)
        live = jnp.where(other == expert, count, live)
    return first, live


def choosers(chip_ref, counts_ref, places, part, row_total):
    row = lax.broadcasted_iota(jnp.int32, (part, row_total), 1)
    slot = lax.broadcasted_iota(jnp.int32, (part, row_total), 0)
    hits = []
    for mask, half in places:
        first, live = rows_of(counts_ref, chip_ref[0] ^ mask)
        here = slot + half * part
        hits.append(((row == first + here) & (here < live)).astype(jnp.float32))
    return jnp.concatenate(hits, 0).astype(jnp.bfloat16)


def pack_kernel(places, chip_ref, counts_ref, tokens_ref, *out_refs):
    part = out_refs[0].shape[0]
    chosen = jnp.dot(
        choosers(chip_ref, counts_ref, places, part, tokens_ref.shape[0]),
        tokens_ref[...],
        preferred_element_type=jnp.float32,
    )
    for place, out_ref in enumerate(out_refs):
        out_ref[...] = chosen[place * part : (place + 1) * part].astype(jnp.bfloat16)


def packed_rows(tokens, counts, chip, places, part):
    row_total, feat_cols = tokens.shape
    smem = pl.BlockSpec(memory_space=pltpu.SMEM)
    vmem = pl.BlockSpec(memory_space=pltpu.VMEM)
    block = jax.ShapeDtypeStruct((part, feat_cols), jnp.bfloat16)
    return pl.pallas_call(
        lambda *refs: pack_kernel(places, *refs),
        out_shape=(block,) * len(places),
        in_specs=[smem, smem, vmem],
        out_specs=(vmem,) * len(places),
        cost_estimate=pl.CostEstimate(
            flops=2 * len(places) * part * row_total * feat_cols,
            bytes_accessed=2 * (row_total + len(places) * part) * feat_cols,
            transcendentals=0,
        ),
        name="pack_rows",
    )(chip[None], counts, tokens)


def combine_kernel(places, chip_ref, counts_ref, *refs):
    piece_refs, out_ref = refs[:-1], refs[-1]
    part = piece_refs[0].shape[0]
    out_ref[...] = lax.dot_general(
        choosers(chip_ref, counts_ref, places, part, out_ref.shape[0]),
        jnp.concatenate([piece_ref[...] for piece_ref in piece_refs], 0),
        (((0,), (0,)), ((), ())),
        preferred_element_type=jnp.float32,
    ).astype(jnp.bfloat16)


def combined_rows(pieces, counts, chip, places, row_total):
    part, feat_cols = pieces[0].shape
    smem = pl.BlockSpec(memory_space=pltpu.SMEM)
    vmem = pl.BlockSpec(memory_space=pltpu.VMEM)
    return pl.pallas_call(
        lambda *refs: combine_kernel(places, *refs),
        out_shape=jax.ShapeDtypeStruct((row_total, feat_cols), jnp.bfloat16),
        in_specs=[smem, smem] + [vmem] * len(pieces),
        out_specs=vmem,
        cost_estimate=pl.CostEstimate(
            flops=2 * len(pieces) * part * row_total * feat_cols,
            bytes_accessed=2 * (row_total + len(pieces) * part) * feat_cols,
            transcendentals=0,
        ),
        name="combine_rows",
    )(chip[None], counts, *pieces)


def weight_kernel(count, *refs):
    input_refs, grad_refs = refs[:count], refs[count : 2 * count]
    gate_ref, up_ref, held = refs[2 * count :]
    half_units = gate_ref.shape[2]

    @pl.when(pl.program_id(0) == 0)
    def _():
        place = 0
        for grad_ref in grad_refs:
            held[place : place + grad_ref.shape[0], :] = grad_ref[...]
            place += grad_ref.shape[0]

    inputs = jnp.concatenate([input_ref[...] for input_ref in input_refs], 0)
    for out_ref, offset in ((gate_ref, 0), (up_ref, half_units)):
        out_ref[0] = lax.dot_general(
            inputs,
            held[:, offset : offset + half_units],
            (((0,), (0,)), ((), ())),
            preferred_element_type=jnp.float32,
        ).astype(jnp.bfloat16)


def weight_grads(inputs, grads):
    count = len(inputs)
    rows = sum(value.shape[0] for value in inputs)
    feat_cols = inputs[0].shape[1]
    units = grads[0].shape[1]
    tile = 256 if feat_cols % 256 == 0 else feat_cols
    out = jax.ShapeDtypeStruct((1, feat_cols, units // 2), jnp.bfloat16)
    out_spec = pl.BlockSpec((1, tile, units // 2), lambda i: (0, i, 0))
    return pl.pallas_call(
        lambda *refs: weight_kernel(count, *refs),
        out_shape=(out, out),
        grid=(feat_cols // tile,),
        in_specs=[pl.BlockSpec((value.shape[0], tile), lambda i: (0, i)) for value in inputs]
        + [pl.BlockSpec(value.shape, lambda i: (0, 0)) for value in grads],
        out_specs=(out_spec, out_spec),
        scratch_shapes=[pltpu.VMEM((rows, units), jnp.bfloat16)],
        compiler_params=pltpu.CompilerParams(vmem_limit_bytes=32 * 2**20),
        cost_estimate=pl.CostEstimate(
            flops=2 * rows * feat_cols * units,
            bytes_accessed=2 * (rows * (feat_cols + units) + feat_cols * units),
            transcendentals=0,
        ),
        name="weight_grads",
    )(*inputs, *grads)


def earlier(value, *needed):
    return lax.optimization_barrier((value,) + needed)[0]


def add_rounded(first, second):
    return (first.astype(jnp.float32) + second.astype(jnp.float32)).astype(jnp.bfloat16)


class Chain:
    def __init__(self, chip, size):
        self.chip = chip
        self.size = size
        self.index = lax.axis_index("fsdp")
        self.partial = None
        self.came = None
        self.whole = None

    def before(self, steps):
        return lax.rem(self.index + self.size - steps, self.size)

    def block(self, owner):
        return pick(self.partial, owner ^ self.chip)

    def send(self, value):
        ring = [(source, (source + 1) % self.size) for source in range(self.size)]
        self.came = lax.ppermute(value, "fsdp", ring)

    def place(self, value, owner):
        self.whole = lax.dynamic_update_index_in_dim(self.whole, value, owner ^ self.chip, 0)


def on_device(tokens, counts, gate_values, up_values, gate_scales, up_scales, grad_hidden):
    row_total, feat_cols = tokens.shape
    experts = counts.shape[1]
    capacity = min(4 * row_total // experts, row_total // 2)
    part = capacity // 2
    n_fsdp = lax.axis_size("fsdp")
    chips = lax.axis_size("expert") // 2
    half_units = gate_values.shape[2]
    parity = lax.axis_index("expert") % 2
    chip = lax.axis_index("expert") // 2
    index = lax.axis_index("fsdp")
    masks = range(chips)
    places = [(mask, half) for half in range(2) for mask in masks]

    packed = packed_rows(tokens, counts, chip, places, part)
    weights = scaled_weights(
        gate_values, up_values, gate_scales, up_scales, index * feat_cols
    )
    cots = grad_hidden[0].reshape(2, 2, part, half_units)
    chains = [Chain(chip, n_fsdp) for _ in range(4)]
    inputs = [None] * 4
    hiddens = [None] * 4
    token = None

    def ordered(value):
        return value if token is None else earlier(value, token)

    def project(group):
        chains[group].partial = (
            jnp.dot(inputs[group], weights, preferred_element_type=jnp.float32)
            .astype(jnp.bfloat16)
            .reshape(chips, part, 2 * half_units)
        )

    def begin(group):
        nonlocal token
        chain = chains[group]
        token = ordered(chain.block(chain.before(1)))
        chain.send(token)

    def reduce(group, step):
        nonlocal token
        chain = chains[group]
        token = add_rounded(chain.block(chain.before(step + 1)), ordered(chain.came))
        chain.send(token)

    def activate(group):
        nonlocal token
        chain = chains[group]
        half, side = divmod(group, 2)
        pre = chain.block(index).astype(jnp.float32) + ordered(chain.came).astype(jnp.float32)
        gate_pre = pre[:, :half_units]
        up_pre = pre[:, half_units:]
        cot = pick(cots, parity ^ (1 - side))[half].astype(jnp.float32)
        sigmoid_gate = jax.nn.sigmoid(gate_pre)
        hiddens[group] = (gate_pre * sigmoid_gate * up_pre).astype(jnp.bfloat16)
        grad_gate_pre = cot * up_pre * sigmoid_gate * (1.0 + gate_pre * (1.0 - sigmoid_gate))
        grad_up_pre = cot * gate_pre * sigmoid_gate
        token = jnp.concatenate(
            [grad_gate_pre.astype(jnp.bfloat16), grad_up_pre.astype(jnp.bfloat16)], 1
        )
        chain.send(token)
        chain.whole = jnp.zeros((chips, part, 2 * half_units), jnp.bfloat16)
        chain.place(token, index)

    def gather(group, step):
        nonlocal token
        chain = chains[group]
        token = ordered(chain.came)
        chain.place(token, chain.before(step))
        if step < n_fsdp - 1:
            chain.send(token)

    def back(group):
        return lax.dot_general(
            chains[group].whole.reshape(chips * part, 2 * half_units),
            weights,
            (((1,), (1,)), ((), ())),
            preferred_element_type=jnp.float32,
        ).astype(jnp.bfloat16)

    def give_back(half):
        taken = swap(back(2 * half), "expert", 1)
        kept = back(2 * half + 1)
        pieces = []
        for mask in masks:
            rows = slice(mask * part, (mask + 1) * part)
            both = add_rounded(kept[rows], taken[rows])
            pieces.append(swap(both, "expert", 2 * mask) if mask else both)
        return pieces

    arrived = [swap(packed[mask], "expert", 2 * mask + 1) for mask in masks]
    weights, *arrived = lax.optimization_barrier((weights, *arrived))
    inputs[0] = jnp.concatenate(arrived, 0)
    inputs[1] = swap(inputs[0], "expert", 1)
    for group in (0, 1):
        project(group)
        begin(group)
    arrived = []
    for step in range(1, n_fsdp - 1):
        for group in (0, 1):
            reduce(group, step)
            if step == 1:
                for mask in masks:
                    if mask % 2 == group:
                        rows = ordered(packed[chips + mask])
                        arrived.append((mask, swap(rows, "expert", 2 * mask + 1)))
    inputs[2] = jnp.concatenate([rows for _, rows in sorted(arrived, key=lambda x: x[0])], 0)
    inputs[3] = swap(inputs[2], "expert", 1)
    for group in (2, 3):
        project(group)
        begin(group)
    for step in range(n_fsdp):
        for group in (0, 1):
            activate(group) if step == 0 else gather(group, step)
        for group in (2, 3):
            if step < n_fsdp - 2:
                reduce(group, step + 1)
            elif step == n_fsdp - 2:
                activate(group)
            else:
                gather(group, 1)
    for group in (0, 1):
        chains[group].whole = ordered(chains[group].whole)
    pieces = give_back(0)
    for step in range(2, n_fsdp):
        for group in (2, 3):
            if group == 3 and step == n_fsdp - 1:
                came, *pieces = lax.optimization_barrier((chains[3].came, *pieces))
                chains[3].came = came
            gather(group, step)
    pieces = pieces + give_back(1)

    own, other = ([hiddens[side], hiddens[2 + side]] for side in (1, 0))
    hidden = jnp.where(
        parity == 0, jnp.concatenate(own + other, 0), jnp.concatenate(other + own, 0)
    )
    grad_gate, grad_up = weight_grads(
        inputs, [chain.whole.reshape(chips * part, 2 * half_units) for chain in chains]
    )
    grad_tokens = combined_rows(pieces, counts, chip, places, row_total)
    return (hidden[None], grad_gate, grad_up, grad_tokens)


def solution(mesh):
    in_specs = (
        P("expert", "fsdp"),
        P("expert", None),
        P("expert", "fsdp", None),
        P("expert", "fsdp", None),
        P("expert", None, None),
        P("expert", None, None),
        P("expert", "fsdp", None),
    )
    out_specs = (
        P("expert", "fsdp", None),
        P("expert", "fsdp", None),
        P("expert", "fsdp", None),
        P("expert", "fsdp"),
    )
    return jax.shard_map(
        on_device, mesh=mesh, in_specs=in_specs, out_specs=out_specs, check_vma=False
    )
```

```python
import math

import jax
import jax.numpy as jnp
from jax import lax
from jax.experimental import pallas as pl
from jax.experimental.pallas import tpu as pltpu
from jax.sharding import PartitionSpec as P


def swap(value, axis, mask):
    pairs = [(source, source ^ mask) for source in range(lax.axis_size(axis))]
    return lax.ppermute(value, axis, pairs)


def pick(blocks, index):
    return lax.dynamic_index_in_dim(blocks, index, 0, keepdims=False)


def scale_kernel(
    sub,
    start_ref,
    gate_ref,
    up_ref,
    gate_scale_ref,
    up_scale_ref,
    out_ref,
    gate_held,
    up_held,
    gate_rows,
    up_rows,
    sems,
):
    rows = out_ref.shape[0]
    half_units = gate_held.shape[1]
    step = pl.program_id(0)

    def arrival(which, turn):
        here = pl.ds(pl.multiple_of(turn * rows, rows), rows)
        value_ref, held = ((gate_ref, gate_held), (up_ref, up_held))[which]
        return pltpu.make_async_copy(
            value_ref.at[0, here, :], held.at[here, :], sems.at[which, turn]
        )

    @pl.when(step == 0)
    def _():
        for turn in range(gate_held.shape[0] // rows):
            for which in range(2):
                arrival(which, turn).start()
        shape = (gate_scale_ref.shape[1], half_units)
        spread = (
            lax.broadcasted_iota(jnp.int32, shape, 0)
            == lax.broadcasted_iota(jnp.int32, shape, 1) // 128
        ).astype(jnp.float32)
        for scale_ref, grown in ((gate_scale_ref, gate_rows), (up_scale_ref, up_rows)):
            grown[...] = lax.dot_general(
                scale_ref[0],
                spread,
                (((0,), (0,)), ((), ())),
                precision=lax.Precision.HIGHEST,
                preferred_element_type=jnp.float32,
            )

    for which, held, grown in ((0, gate_held, gate_rows), (1, up_held, up_rows)):
        arrival(which, step).wait()
        for piece in range(rows // sub):
            block = (start_ref[0] + step * rows + piece * sub) // 128
            there = pl.ds(pl.multiple_of(step * rows + piece * sub, sub), sub)
            scaled = held[there, :].astype(jnp.float32) * grown[pl.ds(block, 1), :]
            out_ref[piece * sub : (piece + 1) * sub, which * half_units : (which + 1) * half_units] = (
                scaled.astype(jnp.bfloat16)
            )


def scaled_weights(gate_values, up_values, gate_scales, up_scales, start_row):
    feat_cols, half_units = gate_values.shape[1:]
    sub = math.gcd(feat_cols, 128)
    rows = max(r for r in range(sub, 257, sub) if feat_cols % r == 0)
    gate_scales, up_scales = (jnp.swapaxes(value, 1, 2) for value in (gate_scales, up_scales))
    any_spec = pl.BlockSpec(memory_space=pl.ANY)
    scale_spec = pl.BlockSpec(gate_scales.shape, lambda i, start: (0, 0, 0))
    held = pltpu.VMEM((feat_cols, half_units), jnp.bfloat16)
    grown = pltpu.VMEM((gate_scales.shape[2], half_units), jnp.float32)
    return pl.pallas_call(
        lambda *refs: scale_kernel(sub, *refs),
        out_shape=jax.ShapeDtypeStruct((feat_cols, 2 * half_units), jnp.bfloat16),
        grid_spec=pltpu.PrefetchScalarGridSpec(
            num_scalar_prefetch=1,
            grid=(feat_cols // rows,),
            in_specs=[any_spec, any_spec, scale_spec, scale_spec],
            out_specs=pl.BlockSpec((rows, 2 * half_units), lambda i, start: (i, 0)),
            scratch_shapes=[
                held,
                held,
                grown,
                grown,
                pltpu.SemaphoreType.DMA((2, feat_cols // rows)),
            ],
        ),
        compiler_params=pltpu.CompilerParams(vmem_limit_bytes=16 * 2**20),
        cost_estimate=pl.CostEstimate(
            flops=2 * feat_cols * half_units,
            bytes_accessed=8 * feat_cols * half_units,
            transcendentals=0,
        ),
        name="scale_weights",
    )(
        start_row[None],
        pltpu.with_memory_space_constraint(gate_values, pltpu.HBM),
        pltpu.with_memory_space_constraint(up_values, pltpu.HBM),
        gate_scales,
        up_scales,
    )


def rows_of(counts_ref, expert):
    first = jnp.int32(0)
    live = jnp.int32(0)
    for other in range(counts_ref.shape[1]):
        count = counts_ref[0, other]
        first = first + jnp.where(other < expert, count, 0)
        live = jnp.where(other == expert, count, live)
    return first, live


def pack_kernel(chip_ref, counts_ref, tokens_ref, chooser_ref, *out_refs):
    row_total = tokens_ref.shape[0]
    capacity = out_refs[0].shape[0]
    row = lax.broadcasted_iota(jnp.int32, (capacity, row_total), 1)
    slot = lax.broadcasted_iota(jnp.int32, (capacity, row_total), 0)
    hits = []
    for mask in range(len(out_refs)):
        first, live = rows_of(counts_ref, chip_ref[0] ^ mask)
        hits.append(((row == first + slot) & (slot < live)).astype(jnp.float32))
    chooser = jnp.concatenate(hits, 0).astype(jnp.bfloat16)
    chooser_ref[...] = chooser
    chosen = jnp.dot(chooser, tokens_ref[...], preferred_element_type=jnp.float32)
    for mask, out_ref in enumerate(out_refs):
        out_ref[...] = chosen[mask * capacity : (mask + 1) * capacity].astype(jnp.bfloat16)


def packed_rows(tokens, counts, chip, capacity):
    row_total, feat_cols = tokens.shape
    experts = counts.shape[1]
    smem = pl.BlockSpec(memory_space=pltpu.SMEM)
    vmem = pl.BlockSpec(memory_space=pltpu.VMEM)
    block = jax.ShapeDtypeStruct((capacity, feat_cols), jnp.bfloat16)
    chooser, *packed = pl.pallas_call(
        pack_kernel,
        out_shape=(jax.ShapeDtypeStruct((experts * capacity, row_total), jnp.bfloat16),)
        + (block,) * experts,
        in_specs=[smem, smem, vmem],
        out_specs=(vmem,) * (experts + 1),
        cost_estimate=pl.CostEstimate(
            flops=2 * experts * capacity * row_total * feat_cols,
            bytes_accessed=2 * (row_total + experts * capacity) * feat_cols,
            transcendentals=0,
        ),
        name="pack_rows",
    )(chip[None], counts, tokens)
    return chooser, packed


def weight_kernel(count, *refs):
    input_refs, grad_refs = refs[:count], refs[count : 2 * count]
    gate_ref, up_ref, held = refs[2 * count :]
    half_units = gate_ref.shape[2]

    @pl.when(pl.program_id(0) == 0)
    def _():
        place = 0
        for grad_ref in grad_refs:
            held[place : place + grad_ref.shape[0], :] = grad_ref[...]
            place += grad_ref.shape[0]

    inputs = jnp.concatenate([input_ref[...] for input_ref in input_refs], 0)
    for out_ref, offset in ((gate_ref, 0), (up_ref, half_units)):
        out_ref[0] = lax.dot_general(
            inputs,
            held[:, offset : offset + half_units],
            (((0,), (0,)), ((), ())),
            preferred_element_type=jnp.float32,
        ).astype(jnp.bfloat16)


def weight_grads(inputs, grads):
    count = len(inputs)
    rows = sum(value.shape[0] for value in inputs)
    feat_cols = inputs[0].shape[1]
    units = grads[0].shape[1]
    tile = 256 if feat_cols % 256 == 0 else feat_cols
    out = jax.ShapeDtypeStruct((1, feat_cols, units // 2), jnp.bfloat16)
    out_spec = pl.BlockSpec((1, tile, units // 2), lambda i: (0, i, 0))
    return pl.pallas_call(
        lambda *refs: weight_kernel(count, *refs),
        out_shape=(out, out),
        grid=(feat_cols // tile,),
        in_specs=[pl.BlockSpec((value.shape[0], tile), lambda i: (0, i)) for value in inputs]
        + [pl.BlockSpec(value.shape, lambda i: (0, 0)) for value in grads],
        out_specs=(out_spec, out_spec),
        scratch_shapes=[pltpu.VMEM((rows, units), jnp.bfloat16)],
        compiler_params=pltpu.CompilerParams(vmem_limit_bytes=16 * 2**20),
        cost_estimate=pl.CostEstimate(
            flops=2 * rows * feat_cols * units,
            bytes_accessed=2 * (rows * (feat_cols + units) + feat_cols * units),
            transcendentals=0,
        ),
        name="weight_grads",
    )(*inputs, *grads)


def earlier(value, *needed):
    return lax.optimization_barrier((value,) + needed)[0]


def add_rounded(first, second):
    return (first.astype(jnp.float32) + second.astype(jnp.float32)).astype(jnp.bfloat16)


class Chain:
    def __init__(self, chip, size):
        self.chip = chip
        self.size = size
        self.index = lax.axis_index("fsdp")
        self.partial = None
        self.came = None
        self.whole = None

    def before(self, steps):
        return lax.rem(self.index + self.size - steps, self.size)

    def block(self, owner):
        return pick(self.partial, owner ^ self.chip)

    def send(self, value):
        ring = [(source, (source + 1) % self.size) for source in range(self.size)]
        self.came = lax.ppermute(value, "fsdp", ring)

    def place(self, value, owner):
        self.whole = lax.dynamic_update_index_in_dim(self.whole, value, owner ^ self.chip, 0)


def on_device(tokens, counts, gate_values, up_values, gate_scales, up_scales, grad_hidden):
    row_total, feat_cols = tokens.shape
    experts = counts.shape[1]
    capacity = min(4 * row_total // experts, row_total // 2)
    n_fsdp = lax.axis_size("fsdp")
    chips = lax.axis_size("expert") // 2
    half_units = gate_values.shape[2]
    parity = lax.axis_index("expert") % 2
    chip = lax.axis_index("expert") // 2
    index = lax.axis_index("fsdp")
    masks = range(chips)

    chooser, packed = packed_rows(tokens, counts, chip, capacity)
    weights = scaled_weights(
        gate_values, up_values, gate_scales, up_scales, index * feat_cols
    )
    cots = grad_hidden[0].reshape(2, capacity, half_units)
    chains = [Chain(chip, n_fsdp) for _ in range(2)]
    hiddens = [None, None]
    token = None

    def ordered(value):
        return value if token is None else earlier(value, token)

    def begin(group):
        nonlocal token
        chain = chains[group]
        chain.partial = (
            jnp.dot(inputs[group], weights, preferred_element_type=jnp.float32)
            .astype(jnp.bfloat16)
            .reshape(chips, capacity, 2 * half_units)
        )
        token = ordered(chain.block(chain.before(1)))
        chain.send(token)

    def reduce(group, step):
        nonlocal token
        chain = chains[group]
        token = add_rounded(chain.block(chain.before(step + 1)), ordered(chain.came))
        chain.send(token)

    def activate(group):
        nonlocal token
        chain = chains[group]
        pre = chain.block(index).astype(jnp.float32) + ordered(chain.came).astype(jnp.float32)
        gate_pre = pre[:, :half_units]
        up_pre = pre[:, half_units:]
        cot = pick(cots, parity ^ (1 - group)).astype(jnp.float32)
        sigmoid_gate = jax.nn.sigmoid(gate_pre)
        hiddens[group] = (gate_pre * sigmoid_gate * up_pre).astype(jnp.bfloat16)
        grad_gate_pre = cot * up_pre * sigmoid_gate * (1.0 + gate_pre * (1.0 - sigmoid_gate))
        grad_up_pre = cot * gate_pre * sigmoid_gate
        token = jnp.concatenate(
            [grad_gate_pre.astype(jnp.bfloat16), grad_up_pre.astype(jnp.bfloat16)], 1
        )
        chain.send(token)
        chain.whole = jnp.zeros((chips, capacity, 2 * half_units), jnp.bfloat16)
        chain.place(token, index)

    def gather(group, step):
        nonlocal token
        chain = chains[group]
        token = ordered(chain.came)
        chain.place(token, chain.before(step))
        if step < n_fsdp - 1:
            chain.send(token)

    def back(whole):
        return lax.dot_general(
            whole, weights, (((1,), (1,)), ((), ())), preferred_element_type=jnp.float32
        ).astype(jnp.bfloat16)

    arrived = [swap(packed[mask], "expert", 2 * mask + 1) for mask in masks]
    weights, *arrived = lax.optimization_barrier((weights, *arrived))
    other = jnp.concatenate(arrived, 0)
    inputs = [other, swap(other, "expert", 1)]
    for group in range(2):
        begin(group)
    for step in range(1, n_fsdp - 1):
        for group in range(2):
            reduce(group, step)
    for group in range(2):
        activate(group)
    for step in range(1, n_fsdp):
        for group in range(2):
            gather(group, step)
    wholes = [chain.whole.reshape(chips * capacity, 2 * half_units) for chain in chains]

    taken = swap(back(wholes[0]), "expert", 1)
    kept = back(earlier(wholes[1], taken))
    pieces = []
    for mask in masks:
        rows = slice(mask * capacity, (mask + 1) * capacity)
        both = add_rounded(kept[rows], taken[rows])
        pieces.append(swap(both, "expert", 2 * mask) if mask else both)

    hidden = jnp.where(
        parity == 0, jnp.concatenate([hiddens[1], hiddens[0]], 0), jnp.concatenate(hiddens, 0)
    )
    grad_gate, grad_up = weight_grads(inputs, wholes)
    grad_tokens = lax.dot_general(
        chooser,
        jnp.concatenate(pieces, 0),
        (((0,), (0,)), ((), ())),
        preferred_element_type=jnp.float32,
    ).astype(jnp.bfloat16)
    return (hidden[None], grad_gate, grad_up, grad_tokens)


def solution(mesh):
    in_specs = (
        P("expert", "fsdp"),
        P("expert", None),
        P("expert", "fsdp", None),
        P("expert", "fsdp", None),
        P("expert", None, None),
        P("expert", None, None),
        P("expert", "fsdp", None),
    )
    out_specs = (
        P("expert", "fsdp", None),
        P("expert", "fsdp", None),
        P("expert", "fsdp", None),
        P("expert", "fsdp"),
    )
    return jax.shard_map(
        on_device, mesh=mesh, in_specs=in_specs, out_specs=out_specs, check_vma=False
    )
```

```python
import math

import jax
import jax.numpy as jnp
from jax import lax
from jax.experimental import pallas as pl
from jax.experimental.pallas import tpu as pltpu
from jax.sharding import PartitionSpec as P


def swap(value, axis, mask):
    pairs = [(source, source ^ mask) for source in range(lax.axis_size(axis))]
    return lax.ppermute(value, axis, pairs)


def pick(blocks, index):
    return lax.dynamic_index_in_dim(blocks, index, 0, keepdims=False)


def scale_kernel(
    sub,
    start_ref,
    gate_ref,
    up_ref,
    gate_scale_ref,
    up_scale_ref,
    out_ref,
    gate_held,
    up_held,
    gate_rows,
    up_rows,
    sems,
):
    rows = out_ref.shape[0]
    half_units = gate_held.shape[1]
    step = pl.program_id(0)

    def arrival(which, turn):
        here = pl.ds(pl.multiple_of(turn * rows, rows), rows)
        value_ref, held = ((gate_ref, gate_held), (up_ref, up_held))[which]
        return pltpu.make_async_copy(
            value_ref.at[0, here, :], held.at[here, :], sems.at[which, turn]
        )

    @pl.when(step == 0)
    def _():
        for turn in range(gate_held.shape[0] // rows):
            for which in range(2):
                arrival(which, turn).start()
        shape = (gate_scale_ref.shape[1], half_units)
        spread = (
            lax.broadcasted_iota(jnp.int32, shape, 0)
            == lax.broadcasted_iota(jnp.int32, shape, 1) // 128
        ).astype(jnp.float32)
        for scale_ref, grown in ((gate_scale_ref, gate_rows), (up_scale_ref, up_rows)):
            grown[...] = lax.dot_general(
                scale_ref[0],
                spread,
                (((0,), (0,)), ((), ())),
                precision=lax.Precision.HIGHEST,
                preferred_element_type=jnp.float32,
            )

    for which, held, grown in ((0, gate_held, gate_rows), (1, up_held, up_rows)):
        arrival(which, step).wait()
        for piece in range(rows // sub):
            block = (start_ref[0] + step * rows + piece * sub) // 128
            there = pl.ds(pl.multiple_of(step * rows + piece * sub, sub), sub)
            scaled = held[there, :].astype(jnp.float32) * grown[pl.ds(block, 1), :]
            out_ref[piece * sub : (piece + 1) * sub, which * half_units : (which + 1) * half_units] = (
                scaled.astype(jnp.bfloat16)
            )


def scaled_weights(gate_values, up_values, gate_scales, up_scales, start_row):
    feat_cols, half_units = gate_values.shape[1:]
    sub = math.gcd(feat_cols, 128)
    rows = max(r for r in range(sub, 257, sub) if feat_cols % r == 0)
    gate_scales, up_scales = (jnp.swapaxes(value, 1, 2) for value in (gate_scales, up_scales))
    any_spec = pl.BlockSpec(memory_space=pl.ANY)
    scale_spec = pl.BlockSpec(gate_scales.shape, lambda i, start: (0, 0, 0))
    held = pltpu.VMEM((feat_cols, half_units), jnp.bfloat16)
    grown = pltpu.VMEM((gate_scales.shape[2], half_units), jnp.float32)
    return pl.pallas_call(
        lambda *refs: scale_kernel(sub, *refs),
        out_shape=jax.ShapeDtypeStruct((feat_cols, 2 * half_units), jnp.bfloat16),
        grid_spec=pltpu.PrefetchScalarGridSpec(
            num_scalar_prefetch=1,
            grid=(feat_cols // rows,),
            in_specs=[any_spec, any_spec, scale_spec, scale_spec],
            out_specs=pl.BlockSpec((rows, 2 * half_units), lambda i, start: (i, 0)),
            scratch_shapes=[
                held,
                held,
                grown,
                grown,
                pltpu.SemaphoreType.DMA((2, feat_cols // rows)),
            ],
        ),
        compiler_params=pltpu.CompilerParams(vmem_limit_bytes=16 * 2**20),
        cost_estimate=pl.CostEstimate(
            flops=2 * feat_cols * half_units,
            bytes_accessed=8 * feat_cols * half_units,
            transcendentals=0,
        ),
        name="scale_weights",
    )(
        start_row[None],
        pltpu.with_memory_space_constraint(gate_values, pltpu.HBM),
        pltpu.with_memory_space_constraint(up_values, pltpu.HBM),
        gate_scales,
        up_scales,
    )


def rows_of(counts_ref, expert):
    first = jnp.int32(0)
    live = jnp.int32(0)
    for other in range(counts_ref.shape[1]):
        count = counts_ref[0, other]
        first = first + jnp.where(other < expert, count, 0)
        live = jnp.where(other == expert, count, live)
    return first, live


def pack_kernel(chip_ref, counts_ref, tokens_ref, chooser_ref, *out_refs):
    row_total = tokens_ref.shape[0]
    capacity = out_refs[0].shape[0]
    row = lax.broadcasted_iota(jnp.int32, (capacity, row_total), 1)
    slot = lax.broadcasted_iota(jnp.int32, (capacity, row_total), 0)
    hits = []
    for mask in range(len(out_refs)):
        first, live = rows_of(counts_ref, chip_ref[0] ^ mask)
        hits.append(((row == first + slot) & (slot < live)).astype(jnp.float32))
    chooser = jnp.concatenate(hits, 0).astype(jnp.bfloat16)
    chooser_ref[...] = chooser
    chosen = jnp.dot(chooser, tokens_ref[...], preferred_element_type=jnp.float32)
    for mask, out_ref in enumerate(out_refs):
        out_ref[...] = chosen[mask * capacity : (mask + 1) * capacity].astype(jnp.bfloat16)


def packed_rows(tokens, counts, chip, capacity):
    row_total, feat_cols = tokens.shape
    experts = counts.shape[1]
    smem = pl.BlockSpec(memory_space=pltpu.SMEM)
    vmem = pl.BlockSpec(memory_space=pltpu.VMEM)
    block = jax.ShapeDtypeStruct((capacity, feat_cols), jnp.bfloat16)
    chooser, *packed = pl.pallas_call(
        pack_kernel,
        out_shape=(jax.ShapeDtypeStruct((experts * capacity, row_total), jnp.bfloat16),)
        + (block,) * experts,
        in_specs=[smem, smem, vmem],
        out_specs=(vmem,) * (experts + 1),
        cost_estimate=pl.CostEstimate(
            flops=2 * experts * capacity * row_total * feat_cols,
            bytes_accessed=2 * (row_total + experts * capacity) * feat_cols,
            transcendentals=0,
        ),
        name="pack_rows",
    )(chip[None], counts, tokens)
    return chooser, packed


def project_kernel(*refs):
    *block_refs, weight_ref, out_ref, held = refs
    capacity = block_refs[0].shape[0]

    @pl.when(pl.program_id(0) == 0)
    def _():
        for place, block_ref in enumerate(block_refs):
            held[place * capacity : (place + 1) * capacity, :] = block_ref[...]

    sums = jnp.dot(held[...], weight_ref[...], preferred_element_type=jnp.float32)
    for place in range(len(block_refs)):
        out_ref[place] = sums[place * capacity : (place + 1) * capacity].astype(jnp.bfloat16)


def projected(blocks, weights):
    count = len(blocks)
    capacity, feat_cols = blocks[0].shape
    units = weights.shape[1]
    tile = math.gcd(units, 512)
    return pl.pallas_call(
        project_kernel,
        out_shape=jax.ShapeDtypeStruct((count, capacity, units), jnp.bfloat16),
        grid=(units // tile,),
        in_specs=[pl.BlockSpec((capacity, feat_cols), lambda i: (0, 0))] * count
        + [pl.BlockSpec((feat_cols, tile), lambda i: (0, i))],
        out_specs=pl.BlockSpec((count, capacity, tile), lambda i: (0, 0, i)),
        scratch_shapes=[pltpu.VMEM((count * capacity, feat_cols), jnp.bfloat16)],
        compiler_params=pltpu.CompilerParams(vmem_limit_bytes=16 * 2**20),
        cost_estimate=pl.CostEstimate(
            flops=2 * count * capacity * feat_cols * units,
            bytes_accessed=2 * (count * capacity * (feat_cols + units) + feat_cols * units),
            transcendentals=0,
        ),
        name="project",
    )(*blocks, pltpu.with_memory_space_constraint(weights, pltpu.VMEM))


def weight_kernel(count, *refs):
    input_refs, grad_refs = refs[:count], refs[count:-3]
    gate_ref, up_ref, held = refs[-3:]
    half_units = gate_ref.shape[2]

    @pl.when(pl.program_id(0) == 0)
    def _():
        place = 0
        for grad_ref in grad_refs:
            held[place : place + grad_ref.shape[0], :] = grad_ref[...]
            place += grad_ref.shape[0]

    inputs = jnp.concatenate([input_ref[...] for input_ref in input_refs], 0)
    for out_ref, offset in ((gate_ref, 0), (up_ref, half_units)):
        out_ref[0] = lax.dot_general(
            inputs,
            held[:, offset : offset + half_units],
            (((0,), (0,)), ((), ())),
            preferred_element_type=jnp.float32,
        ).astype(jnp.bfloat16)


def weight_grads(inputs, grads):
    count = len(inputs)
    rows = sum(value.shape[0] for value in inputs)
    feat_cols = inputs[0].shape[1]
    units = grads[0].shape[1]
    tile = 256 if feat_cols % 256 == 0 else feat_cols
    out = jax.ShapeDtypeStruct((1, feat_cols, units // 2), jnp.bfloat16)
    out_spec = pl.BlockSpec((1, tile, units // 2), lambda i: (0, i, 0))
    return pl.pallas_call(
        lambda *refs: weight_kernel(count, *refs),
        out_shape=(out, out),
        grid=(feat_cols // tile,),
        in_specs=[pl.BlockSpec((value.shape[0], tile), lambda i: (0, i)) for value in inputs]
        + [pl.BlockSpec(value.shape, lambda i: (0, 0)) for value in grads],
        out_specs=(out_spec, out_spec),
        scratch_shapes=[pltpu.VMEM((rows, units), jnp.bfloat16)],
        compiler_params=pltpu.CompilerParams(vmem_limit_bytes=16 * 2**20),
        cost_estimate=pl.CostEstimate(
            flops=2 * rows * feat_cols * units,
            bytes_accessed=2 * (rows * (feat_cols + units) + feat_cols * units),
            transcendentals=0,
        ),
        name="weight_grads",
    )(*inputs, *grads)


def earlier(value, *needed):
    return lax.optimization_barrier((value,) + needed)[0]


def add_rounded(first, second):
    return (first.astype(jnp.float32) + second.astype(jnp.float32)).astype(jnp.bfloat16)


class Chain:
    def __init__(self, chip, size):
        self.chip = chip
        self.size = size
        self.index = lax.axis_index("fsdp")
        self.partial = None
        self.came = None
        self.whole = None

    def before(self, steps):
        return lax.rem(self.index + self.size - steps, self.size)

    def block(self, owner):
        return pick(self.partial, owner ^ self.chip)

    def send(self, value):
        ring = [(source, (source + 1) % self.size) for source in range(self.size)]
        self.came = lax.ppermute(value, "fsdp", ring)

    def place(self, value, owner):
        self.whole = lax.dynamic_update_index_in_dim(self.whole, value, owner ^ self.chip, 0)


def on_device(tokens, counts, gate_values, up_values, gate_scales, up_scales, grad_hidden):
    row_total, feat_cols = tokens.shape
    experts = counts.shape[1]
    capacity = min(4 * row_total // experts, row_total // 2)
    n_fsdp = lax.axis_size("fsdp")
    chips = lax.axis_size("expert") // 2
    half_units = gate_values.shape[2]
    parity = lax.axis_index("expert") % 2
    chip = lax.axis_index("expert") // 2
    index = lax.axis_index("fsdp")
    masks = range(chips)

    chooser, packed = packed_rows(tokens, counts, chip, capacity)
    weights = scaled_weights(
        gate_values, up_values, gate_scales, up_scales, index * feat_cols
    )
    cots = grad_hidden[0].reshape(2, capacity, half_units)
    chains = [Chain(chip, n_fsdp) for _ in range(2)]
    hiddens = [None, None]
    token = None

    def ordered(value):
        return value if token is None else earlier(value, token)

    def begin(group):
        nonlocal token
        chain = chains[group]
        chain.partial = projected(inputs[group], weights)
        token = ordered(chain.block(chain.before(1)))
        chain.send(token)

    def reduce(group, step):
        nonlocal token
        chain = chains[group]
        token = add_rounded(chain.block(chain.before(step + 1)), ordered(chain.came))
        chain.send(token)

    def activate(group):
        nonlocal token
        chain = chains[group]
        pre = chain.block(index).astype(jnp.float32) + ordered(chain.came).astype(jnp.float32)
        gate_pre = pre[:, :half_units]
        up_pre = pre[:, half_units:]
        cot = pick(cots, parity ^ (1 - group)).astype(jnp.float32)
        sigmoid_gate = jax.nn.sigmoid(gate_pre)
        hiddens[group] = (gate_pre * sigmoid_gate * up_pre).astype(jnp.bfloat16)
        grad_gate_pre = cot * up_pre * sigmoid_gate * (1.0 + gate_pre * (1.0 - sigmoid_gate))
        grad_up_pre = cot * gate_pre * sigmoid_gate
        token = jnp.concatenate(
            [grad_gate_pre.astype(jnp.bfloat16), grad_up_pre.astype(jnp.bfloat16)], 1
        )
        chain.send(token)
        chain.whole = jnp.zeros((chips, capacity, 2 * half_units), jnp.bfloat16)
        chain.place(token, index)

    def gather(group, step):
        nonlocal token
        chain = chains[group]
        token = ordered(chain.came)
        chain.place(token, chain.before(step))
        if step < n_fsdp - 1:
            chain.send(token)

    def back(whole):
        return lax.dot_general(
            whole, weights, (((1,), (1,)), ((), ())), preferred_element_type=jnp.float32
        ).astype(jnp.bfloat16)

    arrived = [swap(packed[mask], "expert", 2 * mask + 1) for mask in masks]
    inputs = [arrived, [swap(rows, "expert", 1) for rows in arrived]]
    for group in range(2):
        begin(group)
    for step in range(1, n_fsdp - 1):
        for group in range(2):
            reduce(group, step)
    for group in range(2):
        activate(group)
    for step in range(1, n_fsdp):
        for group in range(2):
            gather(group, step)
    wholes = [chain.whole.reshape(chips * capacity, 2 * half_units) for chain in chains]

    taken = swap(back(wholes[0]), "expert", 1)
    kept = back(earlier(wholes[1], taken))
    pieces = []
    for mask in masks:
        rows = slice(mask * capacity, (mask + 1) * capacity)
        both = add_rounded(kept[rows], taken[rows])
        pieces.append(swap(both, "expert", 2 * mask) if mask else both)

    hidden = jnp.where(
        parity == 0, jnp.concatenate([hiddens[1], hiddens[0]], 0), jnp.concatenate(hiddens, 0)
    )
    grad_gate, grad_up = weight_grads(inputs[0] + inputs[1], wholes)
    grad_tokens = lax.dot_general(
        chooser,
        jnp.concatenate(pieces, 0),
        (((0,), (0,)), ((), ())),
        preferred_element_type=jnp.float32,
    ).astype(jnp.bfloat16)
    return (hidden[None], grad_gate, grad_up, grad_tokens)


def solution(mesh):
    in_specs = (
        P("expert", "fsdp"),
        P("expert", None),
        P("expert", "fsdp", None),
        P("expert", "fsdp", None),
        P("expert", None, None),
        P("expert", None, None),
        P("expert", "fsdp", None),
    )
    out_specs = (
        P("expert", "fsdp", None),
        P("expert", "fsdp", None),
        P("expert", "fsdp", None),
        P("expert", "fsdp"),
    )
    return jax.shard_map(
        on_device, mesh=mesh, in_specs=in_specs, out_specs=out_specs, check_vma=False
    )
```

```python
import math

import jax
import jax.numpy as jnp
from jax import lax
from jax.experimental import pallas as pl
from jax.experimental.pallas import tpu as pltpu
from jax.sharding import PartitionSpec as P


def swap(value, axis, mask):
    pairs = [(source, source ^ mask) for source in range(lax.axis_size(axis))]
    return lax.ppermute(value, axis, pairs)


def pick(blocks, index):
    return lax.dynamic_index_in_dim(blocks, index, 0, keepdims=False)


def scale_kernel(
    sub,
    start_ref,
    gate_ref,
    up_ref,
    gate_scale_ref,
    up_scale_ref,
    out_ref,
    gate_held,
    up_held,
    gate_rows,
    up_rows,
    sems,
):
    rows = out_ref.shape[0]
    half_units = gate_held.shape[1]
    step = pl.program_id(0)

    def arrival(which, turn):
        here = pl.ds(pl.multiple_of(turn * rows, rows), rows)
        value_ref, held = ((gate_ref, gate_held), (up_ref, up_held))[which]
        return pltpu.make_async_copy(
            value_ref.at[0, here, :], held.at[here, :], sems.at[which, turn]
        )

    @pl.when(step == 0)
    def _():
        for turn in range(gate_held.shape[0] // rows):
            for which in range(2):
                arrival(which, turn).start()
        shape = (gate_scale_ref.shape[1], half_units)
        spread = (
            lax.broadcasted_iota(jnp.int32, shape, 0)
            == lax.broadcasted_iota(jnp.int32, shape, 1) // 128
        ).astype(jnp.float32)
        for scale_ref, grown in ((gate_scale_ref, gate_rows), (up_scale_ref, up_rows)):
            grown[...] = lax.dot_general(
                scale_ref[0],
                spread,
                (((0,), (0,)), ((), ())),
                precision=lax.Precision.HIGHEST,
                preferred_element_type=jnp.float32,
            )

    for which, held, grown in ((0, gate_held, gate_rows), (1, up_held, up_rows)):
        arrival(which, step).wait()
        for piece in range(rows // sub):
            block = (start_ref[0] + step * rows + piece * sub) // 128
            there = pl.ds(pl.multiple_of(step * rows + piece * sub, sub), sub)
            scaled = held[there, :].astype(jnp.float32) * grown[pl.ds(block, 1), :]
            out_ref[piece * sub : (piece + 1) * sub, which * half_units : (which + 1) * half_units] = (
                scaled.astype(jnp.bfloat16)
            )


def scaled_weights(gate_values, up_values, gate_scales, up_scales, start_row):
    feat_cols, half_units = gate_values.shape[1:]
    sub = math.gcd(feat_cols, 128)
    rows = max(r for r in range(sub, 257, sub) if feat_cols % r == 0)
    gate_scales, up_scales = (jnp.swapaxes(value, 1, 2) for value in (gate_scales, up_scales))
    any_spec = pl.BlockSpec(memory_space=pl.ANY)
    scale_spec = pl.BlockSpec(gate_scales.shape, lambda i, start: (0, 0, 0))
    held = pltpu.VMEM((feat_cols, half_units), jnp.bfloat16)
    grown = pltpu.VMEM((gate_scales.shape[2], half_units), jnp.float32)
    return pl.pallas_call(
        lambda *refs: scale_kernel(sub, *refs),
        out_shape=jax.ShapeDtypeStruct((feat_cols, 2 * half_units), jnp.bfloat16),
        grid_spec=pltpu.PrefetchScalarGridSpec(
            num_scalar_prefetch=1,
            grid=(feat_cols // rows,),
            in_specs=[any_spec, any_spec, scale_spec, scale_spec],
            out_specs=pl.BlockSpec((rows, 2 * half_units), lambda i, start: (i, 0)),
            scratch_shapes=[
                held,
                held,
                grown,
                grown,
                pltpu.SemaphoreType.DMA((2, feat_cols // rows)),
            ],
        ),
        compiler_params=pltpu.CompilerParams(vmem_limit_bytes=16 * 2**20),
        cost_estimate=pl.CostEstimate(
            flops=2 * feat_cols * half_units,
            bytes_accessed=8 * feat_cols * half_units,
            transcendentals=0,
        ),
        name="scale_weights",
    )(
        start_row[None],
        pltpu.with_memory_space_constraint(gate_values, pltpu.HBM),
        pltpu.with_memory_space_constraint(up_values, pltpu.HBM),
        gate_scales,
        up_scales,
    )


def rows_of(counts_ref, expert):
    first = jnp.int32(0)
    live = jnp.int32(0)
    for other in range(counts_ref.shape[1]):
        count = counts_ref[0, other]
        first = first + jnp.where(other < expert, count, 0)
        live = jnp.where(other == expert, count, live)
    return first, live


def pack_kernel(chip_ref, counts_ref, tokens_ref, chooser_ref, *out_refs):
    row_total = tokens_ref.shape[0]
    capacity = out_refs[0].shape[0]
    row = lax.broadcasted_iota(jnp.int32, (capacity, row_total), 1)
    slot = lax.broadcasted_iota(jnp.int32, (capacity, row_total), 0)
    hits = []
    for mask in range(len(out_refs)):
        first, live = rows_of(counts_ref, chip_ref[0] ^ mask)
        hits.append(((row == first + slot) & (slot < live)).astype(jnp.float32))
    chooser = jnp.concatenate(hits, 0).astype(jnp.bfloat16)
    chooser_ref[...] = chooser
    chosen = jnp.dot(chooser, tokens_ref[...], preferred_element_type=jnp.float32)
    for mask, out_ref in enumerate(out_refs):
        out_ref[...] = chosen[mask * capacity : (mask + 1) * capacity].astype(jnp.bfloat16)


def packed_rows(tokens, counts, chip, capacity):
    row_total, feat_cols = tokens.shape
    experts = counts.shape[1]
    smem = pl.BlockSpec(memory_space=pltpu.SMEM)
    vmem = pl.BlockSpec(memory_space=pltpu.VMEM)
    block = jax.ShapeDtypeStruct((capacity, feat_cols), jnp.bfloat16)
    chooser, *packed = pl.pallas_call(
        pack_kernel,
        out_shape=(jax.ShapeDtypeStruct((experts * capacity, row_total), jnp.bfloat16),)
        + (block,) * experts,
        in_specs=[smem, smem, vmem],
        out_specs=(vmem,) * (experts + 1),
        cost_estimate=pl.CostEstimate(
            flops=2 * experts * capacity * row_total * feat_cols,
            bytes_accessed=2 * (row_total + experts * capacity) * feat_cols,
            transcendentals=0,
        ),
        name="pack_rows",
    )(chip[None], counts, tokens)
    return chooser, packed


def project_kernel(*refs):
    *block_refs, weight_ref, out_ref, held = refs
    capacity = block_refs[0].shape[0]

    @pl.when(pl.program_id(0) == 0)
    def _():
        for place, block_ref in enumerate(block_refs):
            held[place * capacity : (place + 1) * capacity, :] = block_ref[...]

    sums = jnp.dot(held[...], weight_ref[...], preferred_element_type=jnp.float32)
    for place in range(len(block_refs)):
        out_ref[place] = sums[place * capacity : (place + 1) * capacity].astype(jnp.bfloat16)


def projected(blocks, weights):
    count = len(blocks)
    capacity, feat_cols = blocks[0].shape
    units = weights.shape[1]
    tile = math.gcd(units, 512)
    return pl.pallas_call(
        project_kernel,
        out_shape=jax.ShapeDtypeStruct((count, capacity, units), jnp.bfloat16),
        grid=(units // tile,),
        in_specs=[pl.BlockSpec((capacity, feat_cols), lambda i: (0, 0))] * count
        + [pl.BlockSpec((feat_cols, tile), lambda i: (0, i))],
        out_specs=pl.BlockSpec((count, capacity, tile), lambda i: (0, 0, i)),
        scratch_shapes=[pltpu.VMEM((count * capacity, feat_cols), jnp.bfloat16)],
        compiler_params=pltpu.CompilerParams(vmem_limit_bytes=16 * 2**20),
        cost_estimate=pl.CostEstimate(
            flops=2 * count * capacity * feat_cols * units,
            bytes_accessed=2 * (count * capacity * (feat_cols + units) + feat_cols * units),
            transcendentals=0,
        ),
        name="project",
    )(*blocks, pltpu.with_memory_space_constraint(weights, pltpu.VMEM))


def weight_kernel(count, *refs):
    input_refs, grad_refs = refs[:count], refs[count:-3]
    gate_ref, up_ref, held = refs[-3:]
    half_units = gate_ref.shape[2]

    @pl.when(pl.program_id(0) == 0)
    def _():
        place = 0
        for grad_ref in grad_refs:
            held[place : place + grad_ref.shape[0], :] = grad_ref[...]
            place += grad_ref.shape[0]

    inputs = jnp.concatenate([input_ref[...] for input_ref in input_refs], 0)
    for out_ref, offset in ((gate_ref, 0), (up_ref, half_units)):
        out_ref[0] = lax.dot_general(
            inputs,
            held[:, offset : offset + half_units],
            (((0,), (0,)), ((), ())),
            preferred_element_type=jnp.float32,
        ).astype(jnp.bfloat16)


def weight_grads(inputs, grads):
    count = len(inputs)
    rows = sum(value.shape[0] for value in inputs)
    feat_cols = inputs[0].shape[1]
    units = grads[0].shape[1]
    tile = 256 if feat_cols % 256 == 0 else feat_cols
    out = jax.ShapeDtypeStruct((1, feat_cols, units // 2), jnp.bfloat16)
    out_spec = pl.BlockSpec((1, tile, units // 2), lambda i: (0, i, 0))
    return pl.pallas_call(
        lambda *refs: weight_kernel(count, *refs),
        out_shape=(out, out),
        grid=(feat_cols // tile,),
        in_specs=[pl.BlockSpec((value.shape[0], tile), lambda i: (0, i)) for value in inputs]
        + [pl.BlockSpec(value.shape, lambda i: (0, 0)) for value in grads],
        out_specs=(out_spec, out_spec),
        scratch_shapes=[pltpu.VMEM((rows, units), jnp.bfloat16)],
        compiler_params=pltpu.CompilerParams(vmem_limit_bytes=16 * 2**20),
        cost_estimate=pl.CostEstimate(
            flops=2 * rows * feat_cols * units,
            bytes_accessed=2 * (rows * (feat_cols + units) + feat_cols * units),
            transcendentals=0,
        ),
        name="weight_grads",
    )(*inputs, *grads)


def earlier(value, *needed):
    return lax.optimization_barrier((value,) + needed)[0]


def add_rounded(first, second):
    return (first.astype(jnp.float32) + second.astype(jnp.float32)).astype(jnp.bfloat16)


class Chain:
    def __init__(self, chip, size):
        self.chip = chip
        self.size = size
        self.index = lax.axis_index("fsdp")
        self.reach = {1: size // 2, -1: size - 1 - size // 2}
        self.partial = None
        self.whole = None
        self.came = {}

    def owner(self, steps):
        return lax.rem(self.index + self.size + steps, self.size)

    def block(self, steps):
        return pick(self.partial, self.owner(steps) ^ self.chip)

    def send(self, way, value):
        ring = [(source, (source + way) % self.size) for source in range(self.size)]
        self.came[way] = lax.ppermute(value, "fsdp", ring)

    def place(self, value, steps):
        self.whole = lax.dynamic_update_index_in_dim(
            self.whole, value, self.owner(steps) ^ self.chip, 0
        )


def on_device(tokens, counts, gate_values, up_values, gate_scales, up_scales, grad_hidden):
    row_total, feat_cols = tokens.shape
    experts = counts.shape[1]
    capacity = min(4 * row_total // experts, row_total // 2)
    n_fsdp = lax.axis_size("fsdp")
    chips = lax.axis_size("expert") // 2
    half_units = gate_values.shape[2]
    parity = lax.axis_index("expert") % 2
    chip = lax.axis_index("expert") // 2
    index = lax.axis_index("fsdp")
    masks = range(chips)

    chooser, packed = packed_rows(tokens, counts, chip, capacity)
    weights = scaled_weights(
        gate_values, up_values, gate_scales, up_scales, index * feat_cols
    )
    cots = grad_hidden[0].reshape(2, capacity, half_units)
    chains = [Chain(chip, n_fsdp) for _ in range(2)]
    hiddens = [None, None]
    token = None

    def ordered(value):
        return value if token is None else earlier(value, token)

    def begin(group):
        nonlocal token
        chain = chains[group]
        chain.partial = projected(inputs[group], weights)
        for way, reach in chain.reach.items():
            if reach:
                token = ordered(chain.block(way * reach))
                chain.send(way, token)

    def reduce(group, way, step):
        nonlocal token
        chain = chains[group]
        token = add_rounded(
            chain.block(way * (chain.reach[way] - step)), ordered(chain.came[way])
        )
        chain.send(way, token)

    def activate(group):
        nonlocal token
        chain = chains[group]
        pre = chain.block(0).astype(jnp.float32)
        for came in chain.came.values():
            pre = pre + ordered(came).astype(jnp.float32)
        gate_pre = pre[:, :half_units]
        up_pre = pre[:, half_units:]
        cot = pick(cots, parity ^ (1 - group)).astype(jnp.float32)
        sigmoid_gate = jax.nn.sigmoid(gate_pre)
        hiddens[group] = (gate_pre * sigmoid_gate * up_pre).astype(jnp.bfloat16)
        grad_gate_pre = cot * up_pre * sigmoid_gate * (1.0 + gate_pre * (1.0 - sigmoid_gate))
        grad_up_pre = cot * gate_pre * sigmoid_gate
        token = jnp.concatenate(
            [grad_gate_pre.astype(jnp.bfloat16), grad_up_pre.astype(jnp.bfloat16)], 1
        )
        for way, reach in chain.reach.items():
            if reach:
                chain.send(way, token)
        chain.whole = jnp.zeros((chips, capacity, 2 * half_units), jnp.bfloat16)
        chain.place(token, 0)

    def gather(group, way, step):
        nonlocal token
        chain = chains[group]
        token = ordered(chain.came[way])
        chain.place(token, -way * step)
        if step < chain.reach[way]:
            chain.send(way, token)

    def back(whole):
        return lax.dot_general(
            whole, weights, (((1,), (1,)), ((), ())), preferred_element_type=jnp.float32
        ).astype(jnp.bfloat16)

    arrived = [swap(packed[mask], "expert", 2 * mask + 1) for mask in masks]
    inputs = [arrived, [swap(rows, "expert", 1) for rows in arrived]]
    for group in range(2):
        begin(group)
    steps = range(1, n_fsdp)
    for step in steps:
        for group in range(2):
            for way, reach in chains[group].reach.items():
                if step < reach:
                    reduce(group, way, step)
    for group in range(2):
        activate(group)
    for step in steps:
        for group in range(2):
            for way, reach in chains[group].reach.items():
                if step <= reach:
                    gather(group, way, step)
    wholes = [chain.whole.reshape(chips * capacity, 2 * half_units) for chain in chains]

    taken = swap(back(wholes[0]), "expert", 1)
    kept = back(earlier(wholes[1], taken))
    pieces = []
    for mask in masks:
        rows = slice(mask * capacity, (mask + 1) * capacity)
        both = add_rounded(kept[rows], taken[rows])
        pieces.append(swap(both, "expert", 2 * mask) if mask else both)

    hidden = jnp.where(
        parity == 0, jnp.concatenate([hiddens[1], hiddens[0]], 0), jnp.concatenate(hiddens, 0)
    )
    grad_gate, grad_up = weight_grads(inputs[0] + inputs[1], wholes)
    grad_tokens = lax.dot_general(
        chooser,
        jnp.concatenate(pieces, 0),
        (((0,), (0,)), ((), ())),
        preferred_element_type=jnp.float32,
    ).astype(jnp.bfloat16)
    return (hidden[None], grad_gate, grad_up, grad_tokens)


def solution(mesh):
    in_specs = (
        P("expert", "fsdp"),
        P("expert", None),
        P("expert", "fsdp", None),
        P("expert", "fsdp", None),
        P("expert", None, None),
        P("expert", None, None),
        P("expert", "fsdp", None),
    )
    out_specs = (
        P("expert", "fsdp", None),
        P("expert", "fsdp", None),
        P("expert", "fsdp", None),
        P("expert", "fsdp"),
    )
    return jax.shard_map(
        on_device, mesh=mesh, in_specs=in_specs, out_specs=out_specs, check_vma=False
    )
```

```python
import math

import jax
import jax.numpy as jnp
from jax import lax
from jax.experimental import pallas as pl
from jax.experimental.pallas import tpu as pltpu
from jax.sharding import PartitionSpec as P


def swap(value, axis, mask):
    pairs = [(source, source ^ mask) for source in range(lax.axis_size(axis))]
    return lax.ppermute(value, axis, pairs)


def pick(blocks, index):
    return lax.dynamic_index_in_dim(blocks, index, 0, keepdims=False)


def scale_kernel(
    sub,
    start_ref,
    gate_ref,
    up_ref,
    gate_scale_ref,
    up_scale_ref,
    out_ref,
    gate_held,
    up_held,
    gate_rows,
    up_rows,
    sems,
):
    rows = out_ref.shape[0]
    half_units = gate_held.shape[1]
    step = pl.program_id(0)

    def arrival(which, turn):
        here = pl.ds(pl.multiple_of(turn * rows, rows), rows)
        value_ref, held = ((gate_ref, gate_held), (up_ref, up_held))[which]
        return pltpu.make_async_copy(
            value_ref.at[0, here, :], held.at[here, :], sems.at[which, turn]
        )

    @pl.when(step == 0)
    def _():
        for turn in range(gate_held.shape[0] // rows):
            for which in range(2):
                arrival(which, turn).start()
        shape = (gate_scale_ref.shape[1], half_units)
        spread = (
            lax.broadcasted_iota(jnp.int32, shape, 0)
            == lax.broadcasted_iota(jnp.int32, shape, 1) // 128
        ).astype(jnp.float32)
        for scale_ref, grown in ((gate_scale_ref, gate_rows), (up_scale_ref, up_rows)):
            grown[...] = lax.dot_general(
                scale_ref[0],
                spread,
                (((0,), (0,)), ((), ())),
                precision=lax.Precision.HIGHEST,
                preferred_element_type=jnp.float32,
            )

    for which, held, grown in ((0, gate_held, gate_rows), (1, up_held, up_rows)):
        arrival(which, step).wait()
        for piece in range(rows // sub):
            block = (start_ref[0] + step * rows + piece * sub) // 128
            there = pl.ds(pl.multiple_of(step * rows + piece * sub, sub), sub)
            scaled = held[there, :].astype(jnp.float32) * grown[pl.ds(block, 1), :]
            out_ref[piece * sub : (piece + 1) * sub, which * half_units : (which + 1) * half_units] = (
                scaled.astype(jnp.bfloat16)
            )


def scaled_weights(gate_values, up_values, gate_scales, up_scales, start_row):
    feat_cols, half_units = gate_values.shape[1:]
    sub = math.gcd(feat_cols, 128)
    rows = max(r for r in range(sub, 257, sub) if feat_cols % r == 0)
    gate_scales, up_scales = (jnp.swapaxes(value, 1, 2) for value in (gate_scales, up_scales))
    any_spec = pl.BlockSpec(memory_space=pl.ANY)
    scale_spec = pl.BlockSpec(gate_scales.shape, lambda i, start: (0, 0, 0))
    held = pltpu.VMEM((feat_cols, half_units), jnp.bfloat16)
    grown = pltpu.VMEM((gate_scales.shape[2], half_units), jnp.float32)
    return pl.pallas_call(
        lambda *refs: scale_kernel(sub, *refs),
        out_shape=jax.ShapeDtypeStruct((feat_cols, 2 * half_units), jnp.bfloat16),
        grid_spec=pltpu.PrefetchScalarGridSpec(
            num_scalar_prefetch=1,
            grid=(feat_cols // rows,),
            in_specs=[any_spec, any_spec, scale_spec, scale_spec],
            out_specs=pl.BlockSpec((rows, 2 * half_units), lambda i, start: (i, 0)),
            scratch_shapes=[
                held,
                held,
                grown,
                grown,
                pltpu.SemaphoreType.DMA((2, feat_cols // rows)),
            ],
        ),
        compiler_params=pltpu.CompilerParams(vmem_limit_bytes=16 * 2**20),
        cost_estimate=pl.CostEstimate(flops=rows, bytes_accessed=rows, transcendentals=0),
        name="scale_weights",
    )(
        start_row[None],
        pltpu.with_memory_space_constraint(gate_values, pltpu.HBM),
        pltpu.with_memory_space_constraint(up_values, pltpu.HBM),
        gate_scales,
        up_scales,
    )


def rows_of(counts_ref, expert):
    first = jnp.int32(0)
    live = jnp.int32(0)
    for other in range(counts_ref.shape[1]):
        count = counts_ref[0, other]
        first = first + jnp.where(other < expert, count, 0)
        live = jnp.where(other == expert, count, live)
    return first, live


def pack_kernel(places, chip_ref, counts_ref, tokens_ref, chooser_ref, *out_refs):
    row_total = tokens_ref.shape[0]
    part = out_refs[0].shape[0]
    row = lax.broadcasted_iota(jnp.int32, (part, row_total), 1)
    slot = lax.broadcasted_iota(jnp.int32, (part, row_total), 0)
    hits = []
    for half, mask in places:
        first, live = rows_of(counts_ref, chip_ref[0] ^ mask)
        here = slot + half * part
        hits.append(((row == first + here) & (here < live)).astype(jnp.float32))
    chooser = jnp.concatenate(hits, 0).astype(jnp.bfloat16)
    chooser_ref[...] = chooser
    chosen = jnp.dot(chooser, tokens_ref[...], preferred_element_type=jnp.float32)
    for place, out_ref in enumerate(out_refs):
        out_ref[...] = chosen[place * part : (place + 1) * part].astype(jnp.bfloat16)


def packed_rows(tokens, counts, chip, places, part):
    row_total, feat_cols = tokens.shape
    count = len(places)
    smem = pl.BlockSpec(memory_space=pltpu.SMEM)
    vmem = pl.BlockSpec(memory_space=pltpu.VMEM)
    block = jax.ShapeDtypeStruct((part, feat_cols), jnp.bfloat16)
    chooser, *packed = pl.pallas_call(
        lambda *refs: pack_kernel(places, *refs),
        out_shape=(jax.ShapeDtypeStruct((count * part, row_total), jnp.bfloat16),)
        + (block,) * count,
        in_specs=[smem, smem, vmem],
        out_specs=(vmem,) * (count + 1),
        cost_estimate=pl.CostEstimate(
            flops=2 * count * part * row_total * feat_cols,
            bytes_accessed=2 * (row_total + count * part) * feat_cols,
            transcendentals=0,
        ),
        name="pack_rows",
    )(chip[None], counts, tokens)
    return chooser, dict(zip(places, packed))


def project_kernel(*refs):
    *block_refs, weight_ref, out_ref, held = refs
    part = block_refs[0].shape[0]
    capacity = out_ref.shape[1]

    @pl.when(pl.program_id(0) == 0)
    def _():
        for place, block_ref in enumerate(block_refs):
            held[place * part : (place + 1) * part, :] = block_ref[...]

    sums = jnp.dot(held[...], weight_ref[...], preferred_element_type=jnp.float32)
    for owner in range(out_ref.shape[0]):
        out_ref[owner] = sums[owner * capacity : (owner + 1) * capacity].astype(jnp.bfloat16)


def projected(blocks, owners, weights):
    part, feat_cols = blocks[0].shape
    rows = len(blocks) * part
    units = weights.shape[1]
    tile = math.gcd(units, 512)
    return pl.pallas_call(
        project_kernel,
        out_shape=jax.ShapeDtypeStruct((owners, rows // owners, units), jnp.bfloat16),
        grid=(units // tile,),
        in_specs=[pl.BlockSpec((part, feat_cols), lambda i: (0, 0))] * len(blocks)
        + [pl.BlockSpec((feat_cols, tile), lambda i: (0, i))],
        out_specs=pl.BlockSpec((owners, rows // owners, tile), lambda i: (0, 0, i)),
        scratch_shapes=[pltpu.VMEM((rows, feat_cols), jnp.bfloat16)],
        compiler_params=pltpu.CompilerParams(vmem_limit_bytes=16 * 2**20),
        cost_estimate=pl.CostEstimate(flops=rows, bytes_accessed=rows, transcendentals=0),
        name="project",
    )(*blocks, pltpu.with_memory_space_constraint(weights, pltpu.VMEM))


def weight_kernel(count, *refs):
    input_refs, grad_refs = refs[:count], refs[count:-3]
    gate_ref, up_ref, held = refs[-3:]
    half_units = gate_ref.shape[2]

    @pl.when(pl.program_id(0) == 0)
    def _():
        place = 0
        for grad_ref in grad_refs:
            held[place : place + grad_ref.shape[0], :] = grad_ref[...]
            place += grad_ref.shape[0]

    inputs = jnp.concatenate([input_ref[...] for input_ref in input_refs], 0)
    for out_ref, offset in ((gate_ref, 0), (up_ref, half_units)):
        out_ref[0] = lax.dot_general(
            inputs,
            held[:, offset : offset + half_units],
            (((0,), (0,)), ((), ())),
            preferred_element_type=jnp.float32,
        ).astype(jnp.bfloat16)


def weight_grads(inputs, grads):
    count = len(inputs)
    rows = sum(value.shape[0] for value in inputs)
    feat_cols = inputs[0].shape[1]
    units = grads[0].shape[1]
    tile = 256 if feat_cols % 256 == 0 else feat_cols
    out = jax.ShapeDtypeStruct((1, feat_cols, units // 2), jnp.bfloat16)
    out_spec = pl.BlockSpec((1, tile, units // 2), lambda i: (0, i, 0))
    return pl.pallas_call(
        lambda *refs: weight_kernel(count, *refs),
        out_shape=(out, out),
        grid=(feat_cols // tile,),
        in_specs=[pl.BlockSpec((value.shape[0], tile), lambda i: (0, i)) for value in inputs]
        + [pl.BlockSpec(value.shape, lambda i: (0, 0)) for value in grads],
        out_specs=(out_spec, out_spec),
        scratch_shapes=[pltpu.VMEM((rows, units), jnp.bfloat16)],
        compiler_params=pltpu.CompilerParams(vmem_limit_bytes=16 * 2**20),
        cost_estimate=pl.CostEstimate(
            flops=2 * rows * feat_cols * units,
            bytes_accessed=2 * (rows * (feat_cols + units) + feat_cols * units),
            transcendentals=0,
        ),
        name="weight_grads",
    )(*inputs, *grads)


def earlier(value, *needed):
    return lax.optimization_barrier((value,) + needed)[0]


def add_rounded(first, second):
    return (first.astype(jnp.float32) + second.astype(jnp.float32)).astype(jnp.bfloat16)


class Chain:
    def __init__(self, chip, size):
        self.chip = chip
        self.size = size
        self.index = lax.axis_index("fsdp")
        self.reach = {1: size // 2, -1: size - 1 - size // 2}
        self.partial = None
        self.whole = None
        self.came = {}

    def owner(self, steps):
        return lax.rem(self.index + self.size + steps, self.size)

    def block(self, steps):
        return pick(self.partial, self.owner(steps) ^ self.chip)

    def send(self, way, value):
        ring = [(source, (source + way) % self.size) for source in range(self.size)]
        self.came[way] = lax.ppermute(value, "fsdp", ring)

    def place(self, value, steps):
        self.whole = lax.dynamic_update_index_in_dim(
            self.whole, value, self.owner(steps) ^ self.chip, 0
        )


def on_device(tokens, counts, gate_values, up_values, gate_scales, up_scales, grad_hidden):
    row_total, feat_cols = tokens.shape
    experts = counts.shape[1]
    capacity = min(4 * row_total // experts, row_total // 2)
    part = capacity // 2
    n_fsdp = lax.axis_size("fsdp")
    chips = lax.axis_size("expert") // 2
    half_units = gate_values.shape[2]
    parity = lax.axis_index("expert") % 2
    chip = lax.axis_index("expert") // 2
    index = lax.axis_index("fsdp")
    masks = range(chips)
    halves = range(2)
    places = [(half, mask) for half in halves for mask in masks]

    chooser, packed = packed_rows(tokens, counts, chip, places, part)
    weights = scaled_weights(
        gate_values, up_values, gate_scales, up_scales, index * feat_cols
    )
    cots = grad_hidden[0].reshape(2, 2, part, half_units)
    chains = [Chain(chip, n_fsdp) for _ in halves]
    hiddens = [None, None]
    token = None

    def ordered(value):
        return value if token is None else earlier(value, token)

    def arrive(half, *needed):
        rows = {0: (swap(packed[half, 0], "expert", 1), packed[half, 0])}
        for mask in masks[1:]:
            value = packed[half, mask]
            if half:
                value = earlier(value, inputs[0][-2])
            value = swap(value, "expert", 2 * mask + 1)
            rows[mask] = [earlier(value, *needed) if needed else value]
        for mask in masks[1:]:
            value = rows[mask][0]
            if mask > 2:
                value = earlier(value, rows[mask - 2][1])
            rows[mask].append(swap(value, "expert", 1))
        return [value for mask in masks for value in rows[mask]]

    def begin(half):
        nonlocal token
        chain = chains[half]
        chain.partial = projected(inputs[half], chips, weights)
        for way, reach in chain.reach.items():
            if reach:
                token = ordered(chain.block(way * reach))
                chain.send(way, token)

    def reduce(half, way, step):
        nonlocal token
        chain = chains[half]
        token = add_rounded(
            chain.block(way * (chain.reach[way] - step)), ordered(chain.came[way])
        )
        chain.send(way, token)

    def activate(half):
        nonlocal token
        chain = chains[half]
        pre = chain.block(0).astype(jnp.float32)
        for came in chain.came.values():
            pre = pre + ordered(came).astype(jnp.float32)
        gate_pre = pre[:, :half_units]
        up_pre = pre[:, half_units:]
        cot = jnp.concatenate([pick(cots, 1 - parity)[half], pick(cots, parity)[half]], 0)
        cot = cot.astype(jnp.float32)
        sigmoid_gate = jax.nn.sigmoid(gate_pre)
        hiddens[half] = (gate_pre * sigmoid_gate * up_pre).astype(jnp.bfloat16)
        grad_gate_pre = cot * up_pre * sigmoid_gate * (1.0 + gate_pre * (1.0 - sigmoid_gate))
        grad_up_pre = cot * gate_pre * sigmoid_gate
        token = jnp.concatenate(
            [grad_gate_pre.astype(jnp.bfloat16), grad_up_pre.astype(jnp.bfloat16)], 1
        )
        for way, reach in chain.reach.items():
            if reach:
                chain.send(way, token)
        chain.whole = jnp.zeros((chips, capacity, 2 * half_units), jnp.bfloat16)
        chain.place(token, 0)

    def gather(half, step):
        nonlocal token
        chain = chains[half]
        for way, reach in chain.reach.items():
            if step <= reach:
                token = ordered(chain.came[way])
                chain.place(token, -way * step)
                if step < reach:
                    chain.send(way, token)

    def give_back(half):
        back = lax.dot_general(
            chains[half].whole.reshape(chips * capacity, 2 * half_units),
            weights,
            (((1,), (1,)), ((), ())),
            preferred_element_type=jnp.float32,
        ).astype(jnp.bfloat16)
        back = back.reshape(chips, 2, part, feat_cols)
        taken = swap(back[:, 0], "expert", 1)
        sums = add_rounded(back[:, 1], taken)
        pieces = [swap(sums[mask], "expert", 2 * mask) if mask else sums[0] for mask in masks]
        return sums, pieces

    def reduce_all(half):
        chain = chains[half]
        for step in range(1, chain.reach[1]):
            for way, reach in chain.reach.items():
                if step < reach:
                    reduce(half, way, step)

    inputs = []
    inputs.append(arrive(0, weights))
    begin(0)
    reduce_all(0)
    inputs.append(arrive(1, token))
    begin(1)
    activate(0)
    reduce_all(1)
    reach = chains[0].reach[1]
    for step in range(1, reach):
        gather(0, step)
    activate(1)
    gather(0, reach)
    _, pieces = give_back(0)
    for step in range(1, reach):
        gather(1, step)
    chains[1].came[1], *pieces = lax.optimization_barrier((chains[1].came[1], *pieces))
    gather(1, reach)
    sums, late = give_back(1)
    pieces += late

    own, other = (
        jnp.concatenate([rows[side * part : (side + 1) * part] for rows in hiddens], 0)
        for side in (1, 0)
    )
    hidden = jnp.where(
        parity == 0, jnp.concatenate([own, other], 0), jnp.concatenate([other, own], 0)
    )
    grad_gate, grad_up = weight_grads(
        inputs[0] + inputs[1],
        [
            earlier(chain.whole, sums).reshape(chips * capacity, 2 * half_units)
            for chain in chains
        ],
    )
    grad_tokens = lax.dot_general(
        chooser,
        jnp.concatenate(pieces, 0),
        (((0,), (0,)), ((), ())),
        preferred_element_type=jnp.float32,
    ).astype(jnp.bfloat16)
    return (hidden[None], grad_gate, grad_up, grad_tokens)


def solution(mesh):
    in_specs = (
        P("expert", "fsdp"),
        P("expert", None),
        P("expert", "fsdp", None),
        P("expert", "fsdp", None),
        P("expert", None, None),
        P("expert", None, None),
        P("expert", "fsdp", None),
    )
    out_specs = (
        P("expert", "fsdp", None),
        P("expert", "fsdp", None),
        P("expert", "fsdp", None),
        P("expert", "fsdp"),
    )
    return jax.shard_map(
        on_device, mesh=mesh, in_specs=in_specs, out_specs=out_specs, check_vma=False
    )
```

```python
import math

import jax
import jax.numpy as jnp
from jax import lax
from jax.experimental import pallas as pl
from jax.experimental.pallas import tpu as pltpu
from jax.sharding import PartitionSpec as P


def swap(value, axis, mask):
    pairs = [(source, source ^ mask) for source in range(lax.axis_size(axis))]
    return lax.ppermute(value, axis, pairs)


def pick(blocks, index):
    return lax.dynamic_index_in_dim(blocks, index, 0, keepdims=False)


def scale_kernel(
    sub,
    start_ref,
    gate_ref,
    up_ref,
    gate_scale_ref,
    up_scale_ref,
    out_ref,
    gate_held,
    up_held,
    gate_rows,
    up_rows,
    sems,
):
    rows = out_ref.shape[0]
    half_units = gate_held.shape[1]
    step = pl.program_id(0)

    def arrival(which, turn):
        here = pl.ds(pl.multiple_of(turn * rows, rows), rows)
        value_ref, held = ((gate_ref, gate_held), (up_ref, up_held))[which]
        return pltpu.make_async_copy(
            value_ref.at[0, here, :], held.at[here, :], sems.at[which, turn]
        )

    @pl.when(step == 0)
    def _():
        for turn in range(gate_held.shape[0] // rows):
            for which in range(2):
                arrival(which, turn).start()
        shape = (gate_scale_ref.shape[1], half_units)
        spread = (
            lax.broadcasted_iota(jnp.int32, shape, 0)
            == lax.broadcasted_iota(jnp.int32, shape, 1) // 128
        ).astype(jnp.float32)
        for scale_ref, grown in ((gate_scale_ref, gate_rows), (up_scale_ref, up_rows)):
            grown[...] = lax.dot_general(
                scale_ref[0],
                spread,
                (((0,), (0,)), ((), ())),
                precision=lax.Precision.HIGHEST,
                preferred_element_type=jnp.float32,
            )

    for which, held, grown in ((0, gate_held, gate_rows), (1, up_held, up_rows)):
        arrival(which, step).wait()
        for piece in range(rows // sub):
            block = (start_ref[0] + step * rows + piece * sub) // 128
            there = pl.ds(pl.multiple_of(step * rows + piece * sub, sub), sub)
            scaled = held[there, :].astype(jnp.float32) * grown[pl.ds(block, 1), :]
            out_ref[piece * sub : (piece + 1) * sub, which * half_units : (which + 1) * half_units] = (
                scaled.astype(jnp.bfloat16)
            )


def scaled_weights(gate_values, up_values, gate_scales, up_scales, start_row):
    feat_cols, half_units = gate_values.shape[1:]
    sub = math.gcd(feat_cols, 128)
    rows = max(r for r in range(sub, 257, sub) if feat_cols % r == 0)
    gate_scales, up_scales = (jnp.swapaxes(value, 1, 2) for value in (gate_scales, up_scales))
    any_spec = pl.BlockSpec(memory_space=pl.ANY)
    scale_spec = pl.BlockSpec(gate_scales.shape, lambda i, start: (0, 0, 0))
    held = pltpu.VMEM((feat_cols, half_units), jnp.bfloat16)
    grown = pltpu.VMEM((gate_scales.shape[2], half_units), jnp.float32)
    return pl.pallas_call(
        lambda *refs: scale_kernel(sub, *refs),
        out_shape=jax.ShapeDtypeStruct((feat_cols, 2 * half_units), jnp.bfloat16),
        grid_spec=pltpu.PrefetchScalarGridSpec(
            num_scalar_prefetch=1,
            grid=(feat_cols // rows,),
            in_specs=[any_spec, any_spec, scale_spec, scale_spec],
            out_specs=pl.BlockSpec((rows, 2 * half_units), lambda i, start: (i, 0)),
            scratch_shapes=[
                held,
                held,
                grown,
                grown,
                pltpu.SemaphoreType.DMA((2, feat_cols // rows)),
            ],
        ),
        compiler_params=pltpu.CompilerParams(vmem_limit_bytes=16 * 2**20),
        cost_estimate=pl.CostEstimate(
            flops=2 * feat_cols * half_units,
            bytes_accessed=8 * feat_cols * half_units,
            transcendentals=0,
        ),
        name="scale_weights",
    )(
        start_row[None],
        pltpu.with_memory_space_constraint(gate_values, pltpu.HBM),
        pltpu.with_memory_space_constraint(up_values, pltpu.HBM),
        gate_scales,
        up_scales,
    )


def rows_of(counts_ref, expert):
    first = jnp.int32(0)
    live = jnp.int32(0)
    for other in range(counts_ref.shape[1]):
        count = counts_ref[0, other]
        first = first + jnp.where(other < expert, count, 0)
        live = jnp.where(other == expert, count, live)
    return first, live


def pack_kernel(chip_ref, counts_ref, tokens_ref, chooser_ref, *out_refs):
    row_total = tokens_ref.shape[0]
    capacity = out_refs[0].shape[0]
    row = lax.broadcasted_iota(jnp.int32, (capacity, row_total), 1)
    slot = lax.broadcasted_iota(jnp.int32, (capacity, row_total), 0)
    hits = []
    for mask in range(len(out_refs)):
        first, live = rows_of(counts_ref, chip_ref[0] ^ mask)
        hits.append(((row == first + slot) & (slot < live)).astype(jnp.float32))
    chooser = jnp.concatenate(hits, 0).astype(jnp.bfloat16)
    chooser_ref[...] = chooser
    chosen = jnp.dot(chooser, tokens_ref[...], preferred_element_type=jnp.float32)
    for mask, out_ref in enumerate(out_refs):
        out_ref[...] = chosen[mask * capacity : (mask + 1) * capacity].astype(jnp.bfloat16)


def packed_rows(tokens, counts, chip, capacity):
    row_total, feat_cols = tokens.shape
    experts = counts.shape[1]
    smem = pl.BlockSpec(memory_space=pltpu.SMEM)
    vmem = pl.BlockSpec(memory_space=pltpu.VMEM)
    block = jax.ShapeDtypeStruct((capacity, feat_cols), jnp.bfloat16)
    chooser, *packed = pl.pallas_call(
        pack_kernel,
        out_shape=(jax.ShapeDtypeStruct((experts * capacity, row_total), jnp.bfloat16),)
        + (block,) * experts,
        in_specs=[smem, smem, vmem],
        out_specs=(vmem,) * (experts + 1),
        cost_estimate=pl.CostEstimate(
            flops=2 * experts * capacity * row_total * feat_cols,
            bytes_accessed=2 * (row_total + experts * capacity) * feat_cols,
            transcendentals=0,
        ),
        name="pack_rows",
    )(chip[None], counts, tokens)
    return chooser, packed


def project_kernel(*refs):
    *block_refs, weight_ref, out_ref, held = refs
    capacity = block_refs[0].shape[0]

    @pl.when(pl.program_id(0) == 0)
    def _():
        for place, block_ref in enumerate(block_refs):
            held[place * capacity : (place + 1) * capacity, :] = block_ref[...]

    sums = jnp.dot(held[...], weight_ref[...], preferred_element_type=jnp.float32)
    for place in range(len(block_refs)):
        out_ref[place] = sums[place * capacity : (place + 1) * capacity].astype(jnp.bfloat16)


def projected(blocks, weights):
    count = len(blocks)
    capacity, feat_cols = blocks[0].shape
    units = weights.shape[1]
    tile = math.gcd(units, 512)
    return pl.pallas_call(
        project_kernel,
        out_shape=jax.ShapeDtypeStruct((count, capacity, units), jnp.bfloat16),
        grid=(units // tile,),
        in_specs=[pl.BlockSpec((capacity, feat_cols), lambda i: (0, 0))] * count
        + [pl.BlockSpec((feat_cols, tile), lambda i: (0, i))],
        out_specs=pl.BlockSpec((count, capacity, tile), lambda i: (0, 0, i)),
        scratch_shapes=[pltpu.VMEM((count * capacity, feat_cols), jnp.bfloat16)],
        compiler_params=pltpu.CompilerParams(vmem_limit_bytes=16 * 2**20),
        cost_estimate=pl.CostEstimate(
            flops=2 * count * capacity * feat_cols * units,
            bytes_accessed=2 * (count * capacity * (feat_cols + units) + feat_cols * units),
            transcendentals=0,
        ),
        name="project",
    )(*blocks, pltpu.with_memory_space_constraint(weights, pltpu.VMEM))


def weight_kernel(count, *refs):
    input_refs, grad_refs = refs[:count], refs[count:-3]
    gate_ref, up_ref, held = refs[-3:]
    half_units = gate_ref.shape[2]

    @pl.when(pl.program_id(0) == 0)
    def _():
        place = 0
        for grad_ref in grad_refs:
            held[place : place + grad_ref.shape[0], :] = grad_ref[...]
            place += grad_ref.shape[0]

    inputs = jnp.concatenate([input_ref[...] for input_ref in input_refs], 0)
    for out_ref, offset in ((gate_ref, 0), (up_ref, half_units)):
        out_ref[0] = lax.dot_general(
            inputs,
            held[:, offset : offset + half_units],
            (((0,), (0,)), ((), ())),
            preferred_element_type=jnp.float32,
        ).astype(jnp.bfloat16)


def weight_grads(inputs, grads):
    count = len(inputs)
    rows = sum(value.shape[0] for value in inputs)
    feat_cols = inputs[0].shape[1]
    units = grads[0].shape[1]
    tile = 256 if feat_cols % 256 == 0 else feat_cols
    out = jax.ShapeDtypeStruct((1, feat_cols, units // 2), jnp.bfloat16)
    out_spec = pl.BlockSpec((1, tile, units // 2), lambda i: (0, i, 0))
    return pl.pallas_call(
        lambda *refs: weight_kernel(count, *refs),
        out_shape=(out, out),
        grid=(feat_cols // tile,),
        in_specs=[pl.BlockSpec((value.shape[0], tile), lambda i: (0, i)) for value in inputs]
        + [pl.BlockSpec(value.shape, lambda i: (0, 0)) for value in grads],
        out_specs=(out_spec, out_spec),
        scratch_shapes=[pltpu.VMEM((rows, units), jnp.bfloat16)],
        compiler_params=pltpu.CompilerParams(vmem_limit_bytes=16 * 2**20),
        cost_estimate=pl.CostEstimate(
            flops=2 * rows * feat_cols * units,
            bytes_accessed=2 * (rows * (feat_cols + units) + feat_cols * units),
            transcendentals=0,
        ),
        name="weight_grads",
    )(*inputs, *grads)


def earlier(value, *needed):
    return lax.optimization_barrier((value,) + needed)[0]


def add_rounded(first, second):
    return (first.astype(jnp.float32) + second.astype(jnp.float32)).astype(jnp.bfloat16)


class Chain:
    def __init__(self, chip, size):
        self.chip = chip
        self.size = size
        self.index = lax.axis_index("fsdp")
        self.reach = {1: size // 2, -1: size - 1 - size // 2}
        self.partials = []
        self.whole = None
        self.came = {}

    def owner(self, steps):
        return lax.rem(self.index + self.size + steps, self.size)

    def block(self, steps):
        near, far = self.partials
        place = self.owner(steps) ^ self.chip
        count = near.shape[0]
        return jnp.where(
            place < count,
            pick(near, jnp.minimum(place, count - 1)),
            pick(far, jnp.maximum(place - count, 0)),
        )

    def send(self, way, value):
        ring = [(source, (source + way) % self.size) for source in range(self.size)]
        self.came[way] = lax.ppermute(value, "fsdp", ring)

    def place(self, value, steps):
        self.whole = lax.dynamic_update_index_in_dim(
            self.whole, value, self.owner(steps) ^ self.chip, 0
        )


def on_device(tokens, counts, gate_values, up_values, gate_scales, up_scales, grad_hidden):
    row_total, feat_cols = tokens.shape
    experts = counts.shape[1]
    capacity = min(4 * row_total // experts, row_total // 2)
    n_fsdp = lax.axis_size("fsdp")
    chips = lax.axis_size("expert") // 2
    half_units = gate_values.shape[2]
    parity = lax.axis_index("expert") % 2
    chip = lax.axis_index("expert") // 2
    index = lax.axis_index("fsdp")
    masks = range(chips)

    chooser, packed = packed_rows(tokens, counts, chip, capacity)
    weights = scaled_weights(
        gate_values, up_values, gate_scales, up_scales, index * feat_cols
    )
    cots = grad_hidden[0].reshape(2, capacity, half_units)
    chains = [Chain(chip, n_fsdp) for _ in range(2)]
    hiddens = [None, None]
    token = None

    def ordered(value):
        return value if token is None else earlier(value, token)

    def begin(group):
        nonlocal token
        chain = chains[group]
        chain.partials.append(projected(inputs[group][chips // 2 :], weights))
        for way, reach in chain.reach.items():
            if reach:
                token = ordered(chain.block(way * reach))
                chain.send(way, token)

    def reduce(group, way, step):
        nonlocal token
        chain = chains[group]
        token = add_rounded(
            chain.block(way * (chain.reach[way] - step)), ordered(chain.came[way])
        )
        chain.send(way, token)

    def activate(group):
        nonlocal token
        chain = chains[group]
        pre = chain.block(0).astype(jnp.float32)
        for came in chain.came.values():
            pre = pre + ordered(came).astype(jnp.float32)
        gate_pre = pre[:, :half_units]
        up_pre = pre[:, half_units:]
        cot = pick(cots, parity ^ (1 - group)).astype(jnp.float32)
        sigmoid_gate = jax.nn.sigmoid(gate_pre)
        hiddens[group] = (gate_pre * sigmoid_gate * up_pre).astype(jnp.bfloat16)
        grad_gate_pre = cot * up_pre * sigmoid_gate * (1.0 + gate_pre * (1.0 - sigmoid_gate))
        grad_up_pre = cot * gate_pre * sigmoid_gate
        token = jnp.concatenate(
            [grad_gate_pre.astype(jnp.bfloat16), grad_up_pre.astype(jnp.bfloat16)], 1
        )
        for way, reach in chain.reach.items():
            if reach:
                chain.send(way, token)
        chain.whole = jnp.zeros((chips, capacity, 2 * half_units), jnp.bfloat16)
        chain.place(token, 0)

    def gather(group, way, step):
        nonlocal token
        chain = chains[group]
        token = ordered(chain.came[way])
        chain.place(token, -way * step)
        if step < chain.reach[way]:
            chain.send(way, token)

    def back(whole):
        return lax.dot_general(
            whole, weights, (((1,), (1,)), ((), ())), preferred_element_type=jnp.float32
        ).astype(jnp.bfloat16)

    inputs = [[], []]
    for mask in masks:
        rows = swap(packed[mask], "expert", 2 * mask + 1)
        if mask == chips // 2:
            for group in range(2):
                chains[group].partials.append(projected(inputs[group], weights))
        if mask >= chips // 2:
            rows = earlier(rows, *(chain.partials[0] for chain in chains))
        inputs[0].append(rows)
        inputs[1].append(swap(rows, "expert", 1) if mask else packed[0])
    for group in range(2):
        begin(group)
    steps = range(1, n_fsdp)
    for step in steps:
        for group in range(2):
            for way, reach in chains[group].reach.items():
                if step < reach:
                    reduce(group, way, step)
    for group in range(2):
        activate(group)
    for step in steps:
        for group in range(2):
            for way, reach in chains[group].reach.items():
                if step <= reach:
                    gather(group, way, step)
    wholes = [chain.whole.reshape(chips * capacity, 2 * half_units) for chain in chains]

    taken = swap(back(wholes[0]), "expert", 1)
    kept = back(earlier(wholes[1], taken))
    pieces = []
    for mask in masks:
        rows = slice(mask * capacity, (mask + 1) * capacity)
        both = add_rounded(kept[rows], taken[rows])
        pieces.append(swap(both, "expert", 2 * mask) if mask else both)

    hidden = jnp.where(
        parity == 0, jnp.concatenate([hiddens[1], hiddens[0]], 0), jnp.concatenate(hiddens, 0)
    )
    grad_gate, grad_up = weight_grads(inputs[0] + inputs[1], wholes)
    grad_tokens = lax.dot_general(
        chooser,
        jnp.concatenate(pieces, 0),
        (((0,), (0,)), ((), ())),
        preferred_element_type=jnp.float32,
    ).astype(jnp.bfloat16)
    return (hidden[None], grad_gate, grad_up, grad_tokens)


def solution(mesh):
    in_specs = (
        P("expert", "fsdp"),
        P("expert", None),
        P("expert", "fsdp", None),
        P("expert", "fsdp", None),
        P("expert", None, None),
        P("expert", None, None),
        P("expert", "fsdp", None),
    )
    out_specs = (
        P("expert", "fsdp", None),
        P("expert", "fsdp", None),
        P("expert", "fsdp", None),
        P("expert", "fsdp"),
    )
    return jax.shard_map(
        on_device, mesh=mesh, in_specs=in_specs, out_specs=out_specs, check_vma=False
    )
```

```python
import math

import jax
import jax.numpy as jnp
from jax import lax
from jax.experimental import pallas as pl
from jax.experimental.pallas import tpu as pltpu
from jax.sharding import PartitionSpec as P


def swap(value, axis, mask):
    pairs = [(source, source ^ mask) for source in range(lax.axis_size(axis))]
    return lax.ppermute(value, axis, pairs)


def pick(blocks, index):
    return lax.dynamic_index_in_dim(blocks, index, 0, keepdims=False)


def scale_kernel(
    sub,
    start_ref,
    gate_ref,
    up_ref,
    gate_scale_ref,
    up_scale_ref,
    out_ref,
    gate_held,
    up_held,
    gate_rows,
    up_rows,
    sems,
):
    rows = out_ref.shape[0]
    half_units = gate_held.shape[1]
    step = pl.program_id(0)

    def arrival(which, turn):
        here = pl.ds(pl.multiple_of(turn * rows, rows), rows)
        value_ref, held = ((gate_ref, gate_held), (up_ref, up_held))[which]
        return pltpu.make_async_copy(
            value_ref.at[0, here, :], held.at[here, :], sems.at[which, turn]
        )

    @pl.when(step == 0)
    def _():
        for turn in range(gate_held.shape[0] // rows):
            for which in range(2):
                arrival(which, turn).start()
        shape = (gate_scale_ref.shape[1], half_units)
        spread = (
            lax.broadcasted_iota(jnp.int32, shape, 0)
            == lax.broadcasted_iota(jnp.int32, shape, 1) // 128
        ).astype(jnp.float32)
        for scale_ref, grown in ((gate_scale_ref, gate_rows), (up_scale_ref, up_rows)):
            grown[...] = lax.dot_general(
                scale_ref[0],
                spread,
                (((0,), (0,)), ((), ())),
                precision=lax.Precision.HIGHEST,
                preferred_element_type=jnp.float32,
            )

    for which, held, grown in ((0, gate_held, gate_rows), (1, up_held, up_rows)):
        arrival(which, step).wait()
        for piece in range(rows // sub):
            block = (start_ref[0] + step * rows + piece * sub) // 128
            there = pl.ds(pl.multiple_of(step * rows + piece * sub, sub), sub)
            scaled = held[there, :].astype(jnp.float32) * grown[pl.ds(block, 1), :]
            out_ref[piece * sub : (piece + 1) * sub, which * half_units : (which + 1) * half_units] = (
                scaled.astype(jnp.bfloat16)
            )


def scaled_weights(gate_values, up_values, gate_scales, up_scales, start_row):
    feat_cols, half_units = gate_values.shape[1:]
    sub = math.gcd(feat_cols, 128)
    rows = max(r for r in range(sub, 257, sub) if feat_cols % r == 0)
    gate_scales, up_scales = (jnp.swapaxes(value, 1, 2) for value in (gate_scales, up_scales))
    any_spec = pl.BlockSpec(memory_space=pl.ANY)
    scale_spec = pl.BlockSpec(gate_scales.shape, lambda i, start: (0, 0, 0))
    held = pltpu.VMEM((feat_cols, half_units), jnp.bfloat16)
    grown = pltpu.VMEM((gate_scales.shape[2], half_units), jnp.float32)
    return pl.pallas_call(
        lambda *refs: scale_kernel(sub, *refs),
        out_shape=jax.ShapeDtypeStruct((feat_cols, 2 * half_units), jnp.bfloat16),
        grid_spec=pltpu.PrefetchScalarGridSpec(
            num_scalar_prefetch=1,
            grid=(feat_cols // rows,),
            in_specs=[any_spec, any_spec, scale_spec, scale_spec],
            out_specs=pl.BlockSpec((rows, 2 * half_units), lambda i, start: (i, 0)),
            scratch_shapes=[
                held,
                held,
                grown,
                grown,
                pltpu.SemaphoreType.DMA((2, feat_cols // rows)),
            ],
        ),
        compiler_params=pltpu.CompilerParams(vmem_limit_bytes=16 * 2**20),
        cost_estimate=pl.CostEstimate(
            flops=2 * feat_cols * half_units,
            bytes_accessed=8 * feat_cols * half_units,
            transcendentals=0,
        ),
        name="scale_weights",
    )(
        start_row[None],
        pltpu.with_memory_space_constraint(gate_values, pltpu.HBM),
        pltpu.with_memory_space_constraint(up_values, pltpu.HBM),
        gate_scales,
        up_scales,
    )


def rows_of(counts_ref, expert):
    first = jnp.int32(0)
    live = jnp.int32(0)
    for other in range(counts_ref.shape[1]):
        count = counts_ref[0, other]
        first = first + jnp.where(other < expert, count, 0)
        live = jnp.where(other == expert, count, live)
    return first, live


def pack_kernel(chip_ref, counts_ref, tokens_ref, chooser_ref, *out_refs):
    row_total = tokens_ref.shape[0]
    capacity = out_refs[0].shape[0]
    row = lax.broadcasted_iota(jnp.int32, (capacity, row_total), 1)
    slot = lax.broadcasted_iota(jnp.int32, (capacity, row_total), 0)
    hits = []
    for mask in range(len(out_refs)):
        first, live = rows_of(counts_ref, chip_ref[0] ^ mask)
        hits.append(((row == first + slot) & (slot < live)).astype(jnp.float32))
    chooser = jnp.concatenate(hits, 0).astype(jnp.bfloat16)
    chooser_ref[...] = chooser
    chosen = jnp.dot(chooser, tokens_ref[...], preferred_element_type=jnp.float32)
    for mask, out_ref in enumerate(out_refs):
        out_ref[...] = chosen[mask * capacity : (mask + 1) * capacity].astype(jnp.bfloat16)


def packed_rows(tokens, counts, chip, capacity):
    row_total, feat_cols = tokens.shape
    experts = counts.shape[1]
    smem = pl.BlockSpec(memory_space=pltpu.SMEM)
    vmem = pl.BlockSpec(memory_space=pltpu.VMEM)
    block = jax.ShapeDtypeStruct((capacity, feat_cols), jnp.bfloat16)
    chooser, *packed = pl.pallas_call(
        pack_kernel,
        out_shape=(jax.ShapeDtypeStruct((experts * capacity, row_total), jnp.bfloat16),)
        + (block,) * experts,
        in_specs=[smem, smem, vmem],
        out_specs=(vmem,) * (experts + 1),
        cost_estimate=pl.CostEstimate(
            flops=2 * experts * capacity * row_total * feat_cols,
            bytes_accessed=2 * (row_total + experts * capacity) * feat_cols,
            transcendentals=0,
        ),
        name="pack_rows",
    )(chip[None], counts, tokens)
    return chooser, packed


def project_kernel(*refs):
    *block_refs, weight_ref, out_ref, held = refs
    capacity = block_refs[0].shape[0]

    @pl.when(pl.program_id(0) == 0)
    def _():
        for place, block_ref in enumerate(block_refs):
            held[place * capacity : (place + 1) * capacity, :] = block_ref[...]

    sums = jnp.dot(held[...], weight_ref[...], preferred_element_type=jnp.float32)
    for place in range(len(block_refs)):
        out_ref[place] = sums[place * capacity : (place + 1) * capacity].astype(jnp.bfloat16)


def projected(blocks, weights):
    count = len(blocks)
    capacity, feat_cols = blocks[0].shape
    units = weights.shape[1]
    tile = math.gcd(units, 512)
    return pl.pallas_call(
        project_kernel,
        out_shape=jax.ShapeDtypeStruct((count, capacity, units), jnp.bfloat16),
        grid=(units // tile,),
        in_specs=[pl.BlockSpec((capacity, feat_cols), lambda i: (0, 0))] * count
        + [pl.BlockSpec((feat_cols, tile), lambda i: (0, i))],
        out_specs=pl.BlockSpec((count, capacity, tile), lambda i: (0, 0, i)),
        scratch_shapes=[pltpu.VMEM((count * capacity, feat_cols), jnp.bfloat16)],
        compiler_params=pltpu.CompilerParams(vmem_limit_bytes=16 * 2**20),
        cost_estimate=pl.CostEstimate(
            flops=2 * count * capacity * feat_cols * units,
            bytes_accessed=2 * (count * capacity * (feat_cols + units) + feat_cols * units),
            transcendentals=0,
        ),
        name="project",
    )(*blocks, pltpu.with_memory_space_constraint(weights, pltpu.VMEM))


def weight_kernel(count, *refs):
    input_refs, grad_refs = refs[:count], refs[count:-3]
    gate_ref, up_ref, held = refs[-3:]
    half_units = gate_ref.shape[2]

    @pl.when(pl.program_id(0) == 0)
    def _():
        place = 0
        for grad_ref in grad_refs:
            held[place : place + grad_ref.shape[0], :] = grad_ref[...]
            place += grad_ref.shape[0]

    inputs = jnp.concatenate([input_ref[...] for input_ref in input_refs], 0)
    for out_ref, offset in ((gate_ref, 0), (up_ref, half_units)):
        out_ref[0] = lax.dot_general(
            inputs,
            held[:, offset : offset + half_units],
            (((0,), (0,)), ((), ())),
            preferred_element_type=jnp.float32,
        ).astype(jnp.bfloat16)


def weight_grads(inputs, grads):
    count = len(inputs)
    rows = sum(value.shape[0] for value in inputs)
    feat_cols = inputs[0].shape[1]
    units = grads[0].shape[1]
    tile = 256 if feat_cols % 256 == 0 else feat_cols
    out = jax.ShapeDtypeStruct((1, feat_cols, units // 2), jnp.bfloat16)
    out_spec = pl.BlockSpec((1, tile, units // 2), lambda i: (0, i, 0))
    return pl.pallas_call(
        lambda *refs: weight_kernel(count, *refs),
        out_shape=(out, out),
        grid=(feat_cols // tile,),
        in_specs=[pl.BlockSpec((value.shape[0], tile), lambda i: (0, i)) for value in inputs]
        + [pl.BlockSpec(value.shape, lambda i: (0, 0)) for value in grads],
        out_specs=(out_spec, out_spec),
        scratch_shapes=[pltpu.VMEM((rows, units), jnp.bfloat16)],
        compiler_params=pltpu.CompilerParams(vmem_limit_bytes=16 * 2**20),
        cost_estimate=pl.CostEstimate(
            flops=2 * rows * feat_cols * units,
            bytes_accessed=2 * (rows * (feat_cols + units) + feat_cols * units),
            transcendentals=0,
        ),
        name="weight_grads",
    )(*inputs, *grads)


def earlier(value, *needed):
    return lax.optimization_barrier((value,) + needed)[0]


def add_rounded(first, second):
    return (first.astype(jnp.float32) + second.astype(jnp.float32)).astype(jnp.bfloat16)


class Chain:
    def __init__(self, chip, size):
        self.chip = chip
        self.size = size
        self.index = lax.axis_index("fsdp")
        self.reach = {1: size // 2, -1: size - 1 - size // 2}
        self.partials = []
        self.whole = None
        self.came = {}

    def owner(self, steps):
        return lax.rem(self.index + self.size + steps, self.size)

    def block(self, steps):
        near, far = self.partials
        place = self.owner(steps) ^ self.chip
        count = near.shape[0]
        return jnp.where(
            place < count,
            pick(near, jnp.minimum(place, count - 1)),
            pick(far, jnp.maximum(place - count, 0)),
        )

    def send(self, way, value):
        ring = [(source, (source + way) % self.size) for source in range(self.size)]
        self.came[way] = lax.ppermute(value, "fsdp", ring)

    def place(self, value, steps):
        self.whole = lax.dynamic_update_index_in_dim(
            self.whole, value, self.owner(steps) ^ self.chip, 0
        )


def on_device(tokens, counts, gate_values, up_values, gate_scales, up_scales, grad_hidden):
    row_total, feat_cols = tokens.shape
    experts = counts.shape[1]
    capacity = min(4 * row_total // experts, row_total // 2)
    n_fsdp = lax.axis_size("fsdp")
    chips = lax.axis_size("expert") // 2
    half_units = gate_values.shape[2]
    parity = lax.axis_index("expert") % 2
    chip = lax.axis_index("expert") // 2
    index = lax.axis_index("fsdp")
    masks = range(chips)

    chooser, packed = packed_rows(tokens, counts, chip, capacity)
    weights = scaled_weights(
        gate_values, up_values, gate_scales, up_scales, index * feat_cols
    )
    cots = grad_hidden[0].reshape(2, capacity, half_units)
    chains = [Chain(chip, n_fsdp) for _ in range(2)]
    hiddens = [None, None]
    token = None

    def ordered(value):
        return value if token is None else earlier(value, token)

    def begin(group):
        nonlocal token
        chain = chains[group]
        chain.partials.append(projected(inputs[group][chips // 2 :], weights))
        for way, reach in chain.reach.items():
            if reach:
                token = ordered(chain.block(way * reach))
                chain.send(way, token)

    def reduce(group, way, step):
        nonlocal token
        chain = chains[group]
        token = add_rounded(
            chain.block(way * (chain.reach[way] - step)), ordered(chain.came[way])
        )
        chain.send(way, token)

    def activate(group):
        nonlocal token
        chain = chains[group]
        pre = chain.block(0).astype(jnp.float32)
        for came in chain.came.values():
            pre = pre + ordered(came).astype(jnp.float32)
        gate_pre = pre[:, :half_units]
        up_pre = pre[:, half_units:]
        cot = pick(cots, parity ^ (1 - group)).astype(jnp.float32)
        sigmoid_gate = jax.nn.sigmoid(gate_pre)
        hiddens[group] = (gate_pre * sigmoid_gate * up_pre).astype(jnp.bfloat16)
        grad_gate_pre = cot * up_pre * sigmoid_gate * (1.0 + gate_pre * (1.0 - sigmoid_gate))
        grad_up_pre = cot * gate_pre * sigmoid_gate
        token = jnp.concatenate(
            [grad_gate_pre.astype(jnp.bfloat16), grad_up_pre.astype(jnp.bfloat16)], 1
        )
        for way, reach in chain.reach.items():
            if reach:
                chain.send(way, token)
        chain.whole = jnp.zeros((chips, capacity, 2 * half_units), jnp.bfloat16)
        chain.place(token, 0)

    def gather(group, way, step):
        nonlocal token
        chain = chains[group]
        token = ordered(chain.came[way])
        chain.place(token, -way * step)
        if step < chain.reach[way]:
            chain.send(way, token)

    def back(whole):
        return lax.dot_general(
            whole, weights, (((1,), (1,)), ((), ())), preferred_element_type=jnp.float32
        ).astype(jnp.bfloat16)

    inputs = [[], []]
    for mask in masks:
        rows = swap(packed[mask], "expert", 2 * mask + 1)
        if mask == chips // 2:
            for group in range(2):
                chains[group].partials.append(projected(inputs[group], weights))
        if mask >= chips // 2:
            rows = earlier(rows, *(chain.partials[0] for chain in chains))
        else:
            rows = earlier(rows, weights)
        inputs[0].append(rows)
        inputs[1].append(swap(rows, "expert", 1) if mask else packed[0])
    for group in range(2):
        begin(group)
    steps = range(1, n_fsdp)
    for step in steps:
        for group in range(2):
            for way, reach in chains[group].reach.items():
                if step < reach:
                    reduce(group, way, step)
    for group in range(2):
        activate(group)
    for step in steps:
        for group in range(2):
            for way, reach in chains[group].reach.items():
                if step <= reach:
                    gather(group, way, step)
    wholes = [chain.whole.reshape(chips * capacity, 2 * half_units) for chain in chains]

    taken = swap(back(wholes[0]), "expert", 1)
    kept = back(earlier(wholes[1], taken))
    pieces = []
    for mask in masks:
        rows = slice(mask * capacity, (mask + 1) * capacity)
        both = add_rounded(kept[rows], taken[rows])
        pieces.append(swap(both, "expert", 2 * mask) if mask else both)

    hidden = jnp.where(
        parity == 0, jnp.concatenate([hiddens[1], hiddens[0]], 0), jnp.concatenate(hiddens, 0)
    )
    grad_gate, grad_up = weight_grads(inputs[0] + inputs[1], wholes)
    grad_tokens = lax.dot_general(
        chooser,
        jnp.concatenate(pieces, 0),
        (((0,), (0,)), ((), ())),
        preferred_element_type=jnp.float32,
    ).astype(jnp.bfloat16)
    return (hidden[None], grad_gate, grad_up, grad_tokens)


def solution(mesh):
    in_specs = (
        P("expert", "fsdp"),
        P("expert", None),
        P("expert", "fsdp", None),
        P("expert", "fsdp", None),
        P("expert", None, None),
        P("expert", None, None),
        P("expert", "fsdp", None),
    )
    out_specs = (
        P("expert", "fsdp", None),
        P("expert", "fsdp", None),
        P("expert", "fsdp", None),
        P("expert", "fsdp"),
    )
    return jax.shard_map(
        on_device, mesh=mesh, in_specs=in_specs, out_specs=out_specs, check_vma=False
    )
```

```python
import math

import jax
import jax.numpy as jnp
from jax import lax
from jax.experimental import pallas as pl
from jax.experimental.pallas import tpu as pltpu
from jax.sharding import PartitionSpec as P


def swap(value, axis, mask):
    pairs = [(source, source ^ mask) for source in range(lax.axis_size(axis))]
    return lax.ppermute(value, axis, pairs)


def pick(blocks, index):
    return lax.dynamic_index_in_dim(blocks, index, 0, keepdims=False)


def scale_kernel(
    sub,
    start_ref,
    gate_ref,
    up_ref,
    gate_scale_ref,
    up_scale_ref,
    out_ref,
    gate_held,
    up_held,
    gate_rows,
    up_rows,
    sems,
):
    rows = out_ref.shape[0]
    half_units = gate_held.shape[1]
    step = pl.program_id(0)

    def arrival(which, turn):
        here = pl.ds(pl.multiple_of(turn * rows, rows), rows)
        value_ref, held = ((gate_ref, gate_held), (up_ref, up_held))[which]
        return pltpu.make_async_copy(
            value_ref.at[0, here, :], held.at[here, :], sems.at[which, turn]
        )

    @pl.when(step == 0)
    def _():
        for turn in range(gate_held.shape[0] // rows):
            for which in range(2):
                arrival(which, turn).start()
        shape = (gate_scale_ref.shape[1], half_units)
        spread = (
            lax.broadcasted_iota(jnp.int32, shape, 0)
            == lax.broadcasted_iota(jnp.int32, shape, 1) // 128
        ).astype(jnp.float32)
        for scale_ref, grown in ((gate_scale_ref, gate_rows), (up_scale_ref, up_rows)):
            grown[...] = lax.dot_general(
                scale_ref[0],
                spread,
                (((0,), (0,)), ((), ())),
                precision=lax.Precision.HIGHEST,
                preferred_element_type=jnp.float32,
            )

    for which, held, grown in ((0, gate_held, gate_rows), (1, up_held, up_rows)):
        arrival(which, step).wait()
        for piece in range(rows // sub):
            block = (start_ref[0] + step * rows + piece * sub) // 128
            there = pl.ds(pl.multiple_of(step * rows + piece * sub, sub), sub)
            scaled = held[there, :].astype(jnp.float32) * grown[pl.ds(block, 1), :]
            out_ref[piece * sub : (piece + 1) * sub, which * half_units : (which + 1) * half_units] = (
                scaled.astype(jnp.bfloat16)
            )


def scaled_weights(gate_values, up_values, gate_scales, up_scales, start_row):
    feat_cols, half_units = gate_values.shape[1:]
    sub = math.gcd(feat_cols, 128)
    rows = max(r for r in range(sub, 257, sub) if feat_cols % r == 0)
    gate_scales, up_scales = (jnp.swapaxes(value, 1, 2) for value in (gate_scales, up_scales))
    any_spec = pl.BlockSpec(memory_space=pl.ANY)
    scale_spec = pl.BlockSpec(gate_scales.shape, lambda i, start: (0, 0, 0))
    held = pltpu.VMEM((feat_cols, half_units), jnp.bfloat16)
    grown = pltpu.VMEM((gate_scales.shape[2], half_units), jnp.float32)
    return pl.pallas_call(
        lambda *refs: scale_kernel(sub, *refs),
        out_shape=jax.ShapeDtypeStruct((feat_cols, 2 * half_units), jnp.bfloat16),
        grid_spec=pltpu.PrefetchScalarGridSpec(
            num_scalar_prefetch=1,
            grid=(feat_cols // rows,),
            in_specs=[any_spec, any_spec, scale_spec, scale_spec],
            out_specs=pl.BlockSpec((rows, 2 * half_units), lambda i, start: (i, 0)),
            scratch_shapes=[
                held,
                held,
                grown,
                grown,
                pltpu.SemaphoreType.DMA((2, feat_cols // rows)),
            ],
        ),
        compiler_params=pltpu.CompilerParams(vmem_limit_bytes=16 * 2**20),
        cost_estimate=pl.CostEstimate(
            flops=2 * feat_cols * half_units,
            bytes_accessed=8 * feat_cols * half_units,
            transcendentals=0,
        ),
        name="scale_weights",
    )(
        start_row[None],
        pltpu.with_memory_space_constraint(gate_values, pltpu.HBM),
        pltpu.with_memory_space_constraint(up_values, pltpu.HBM),
        gate_scales,
        up_scales,
    )


def rows_of(counts_ref, expert):
    first = jnp.int32(0)
    live = jnp.int32(0)
    for other in range(counts_ref.shape[1]):
        count = counts_ref[0, other]
        first = first + jnp.where(other < expert, count, 0)
        live = jnp.where(other == expert, count, live)
    return first, live


def pack_kernel(chip_ref, counts_ref, tokens_ref, chooser_ref, *out_refs):
    row_total = tokens_ref.shape[0]
    capacity = out_refs[0].shape[0]
    row = lax.broadcasted_iota(jnp.int32, (capacity, row_total), 1)
    slot = lax.broadcasted_iota(jnp.int32, (capacity, row_total), 0)
    hits = []
    for mask in range(len(out_refs)):
        first, live = rows_of(counts_ref, chip_ref[0] ^ mask)
        hits.append(((row == first + slot) & (slot < live)).astype(jnp.float32))
    chooser = jnp.concatenate(hits, 0).astype(jnp.bfloat16)
    chooser_ref[...] = chooser
    chosen = jnp.dot(chooser, tokens_ref[...], preferred_element_type=jnp.float32)
    for mask, out_ref in enumerate(out_refs):
        out_ref[...] = chosen[mask * capacity : (mask + 1) * capacity].astype(jnp.bfloat16)


def packed_rows(tokens, counts, chip, capacity):
    row_total, feat_cols = tokens.shape
    experts = counts.shape[1]
    smem = pl.BlockSpec(memory_space=pltpu.SMEM)
    vmem = pl.BlockSpec(memory_space=pltpu.VMEM)
    block = jax.ShapeDtypeStruct((capacity, feat_cols), jnp.bfloat16)
    chooser, *packed = pl.pallas_call(
        pack_kernel,
        out_shape=(jax.ShapeDtypeStruct((experts * capacity, row_total), jnp.bfloat16),)
        + (block,) * experts,
        in_specs=[smem, smem, vmem],
        out_specs=(vmem,) * (experts + 1),
        cost_estimate=pl.CostEstimate(
            flops=2 * experts * capacity * row_total * feat_cols,
            bytes_accessed=2 * (row_total + experts * capacity) * feat_cols,
            transcendentals=0,
        ),
        name="pack_rows",
    )(chip[None], counts, tokens)
    return chooser, packed


def project_kernel(*refs):
    *block_refs, weight_ref, out_ref, held = refs
    capacity = block_refs[0].shape[0]

    @pl.when(pl.program_id(0) == 0)
    def _():
        for place, block_ref in enumerate(block_refs):
            held[place * capacity : (place + 1) * capacity, :] = block_ref[...]

    sums = jnp.dot(held[...], weight_ref[...], preferred_element_type=jnp.float32)
    for place in range(len(block_refs)):
        out_ref[place] = sums[place * capacity : (place + 1) * capacity].astype(jnp.bfloat16)


def projected(blocks, weights):
    count = len(blocks)
    capacity, feat_cols = blocks[0].shape
    units = weights.shape[1]
    tile = math.gcd(units, 512)
    return pl.pallas_call(
        project_kernel,
        out_shape=jax.ShapeDtypeStruct((count, capacity, units), jnp.bfloat16),
        grid=(units // tile,),
        in_specs=[pl.BlockSpec((capacity, feat_cols), lambda i: (0, 0))] * count
        + [pl.BlockSpec((feat_cols, tile), lambda i: (0, i))],
        out_specs=pl.BlockSpec((count, capacity, tile), lambda i: (0, 0, i)),
        scratch_shapes=[pltpu.VMEM((count * capacity, feat_cols), jnp.bfloat16)],
        compiler_params=pltpu.CompilerParams(vmem_limit_bytes=16 * 2**20),
        cost_estimate=pl.CostEstimate(
            flops=2 * count * capacity * feat_cols * units,
            bytes_accessed=2 * (count * capacity * (feat_cols + units) + feat_cols * units),
            transcendentals=0,
        ),
        name="project",
    )(*blocks, pltpu.with_memory_space_constraint(weights, pltpu.VMEM))


def weight_kernel(count, *refs):
    input_refs, grad_refs = refs[:count], refs[count:-3]
    gate_ref, up_ref, held = refs[-3:]
    half_units = gate_ref.shape[2]

    @pl.when(pl.program_id(0) == 0)
    def _():
        place = 0
        for grad_ref in grad_refs:
            held[place : place + grad_ref.shape[0], :] = grad_ref[...]
            place += grad_ref.shape[0]

    inputs = jnp.concatenate([input_ref[...] for input_ref in input_refs], 0)
    for out_ref, offset in ((gate_ref, 0), (up_ref, half_units)):
        out_ref[0] = lax.dot_general(
            inputs,
            held[:, offset : offset + half_units],
            (((0,), (0,)), ((), ())),
            preferred_element_type=jnp.float32,
        ).astype(jnp.bfloat16)


def weight_grads(inputs, grads):
    count = len(inputs)
    rows = sum(value.shape[0] for value in inputs)
    feat_cols = inputs[0].shape[1]
    units = grads[0].shape[1]
    tile = 256 if feat_cols % 256 == 0 else feat_cols
    out = jax.ShapeDtypeStruct((1, feat_cols, units // 2), jnp.bfloat16)
    out_spec = pl.BlockSpec((1, tile, units // 2), lambda i: (0, i, 0))
    return pl.pallas_call(
        lambda *refs: weight_kernel(count, *refs),
        out_shape=(out, out),
        grid=(feat_cols // tile,),
        in_specs=[pl.BlockSpec((value.shape[0], tile), lambda i: (0, i)) for value in inputs]
        + [pl.BlockSpec(value.shape, lambda i: (0, 0)) for value in grads],
        out_specs=(out_spec, out_spec),
        scratch_shapes=[pltpu.VMEM((rows, units), jnp.bfloat16)],
        compiler_params=pltpu.CompilerParams(vmem_limit_bytes=16 * 2**20),
        cost_estimate=pl.CostEstimate(
            flops=2 * rows * feat_cols * units,
            bytes_accessed=2 * (rows * (feat_cols + units) + feat_cols * units),
            transcendentals=0,
        ),
        name="weight_grads",
    )(*inputs, *grads)


def earlier(value, *needed):
    return lax.optimization_barrier((value,) + needed)[0]


def add_rounded(first, second):
    return (first.astype(jnp.float32) + second.astype(jnp.float32)).astype(jnp.bfloat16)


class Chain:
    def __init__(self, chip, size):
        self.chip = chip
        self.size = size
        self.index = lax.axis_index("fsdp")
        self.reach = {1: size // 2, -1: size - 1 - size // 2}
        self.partial = None
        self.whole = None
        self.came = {}

    def owner(self, steps):
        return lax.rem(self.index + self.size + steps, self.size)

    def block(self, steps):
        return pick(self.partial, self.owner(steps) ^ self.chip)

    def send(self, way, value):
        ring = [(source, (source + way) % self.size) for source in range(self.size)]
        self.came[way] = lax.ppermute(value, "fsdp", ring)

    def place(self, value, steps):
        self.whole = lax.dynamic_update_index_in_dim(
            self.whole, value, self.owner(steps) ^ self.chip, 0
        )


def on_device(tokens, counts, gate_values, up_values, gate_scales, up_scales, grad_hidden):
    row_total, feat_cols = tokens.shape
    experts = counts.shape[1]
    capacity = min(4 * row_total // experts, row_total // 2)
    n_fsdp = lax.axis_size("fsdp")
    chips = lax.axis_size("expert") // 2
    half_units = gate_values.shape[2]
    parity = lax.axis_index("expert") % 2
    chip = lax.axis_index("expert") // 2
    index = lax.axis_index("fsdp")
    masks = range(chips)

    chooser, packed = packed_rows(tokens, counts, chip, capacity)
    weights = scaled_weights(
        gate_values, up_values, gate_scales, up_scales, index * feat_cols
    )
    cots = grad_hidden[0].reshape(2, capacity, half_units)
    chains = [Chain(chip, n_fsdp) for _ in range(2)]
    hiddens = [None, None]
    token = None

    def ordered(value):
        return value if token is None else earlier(value, token)

    def begin(group):
        nonlocal token
        chain = chains[group]
        chain.partial = projected(inputs[group], weights)
        for way, reach in chain.reach.items():
            if reach:
                token = ordered(chain.block(way * reach))
                chain.send(way, token)

    def reduce(group, way, step):
        nonlocal token
        chain = chains[group]
        token = add_rounded(
            chain.block(way * (chain.reach[way] - step)), ordered(chain.came[way])
        )
        chain.send(way, token)

    def activate(group):
        nonlocal token
        chain = chains[group]
        pre = chain.block(0).astype(jnp.float32)
        for came in chain.came.values():
            pre = pre + ordered(came).astype(jnp.float32)
        gate_pre = pre[:, :half_units]
        up_pre = pre[:, half_units:]
        cot = pick(cots, parity ^ (1 - group)).astype(jnp.float32)
        sigmoid_gate = jax.nn.sigmoid(gate_pre)
        hiddens[group] = (gate_pre * sigmoid_gate * up_pre).astype(jnp.bfloat16)
        grad_gate_pre = cot * up_pre * sigmoid_gate * (1.0 + gate_pre * (1.0 - sigmoid_gate))
        grad_up_pre = cot * gate_pre * sigmoid_gate
        token = jnp.concatenate(
            [grad_gate_pre.astype(jnp.bfloat16), grad_up_pre.astype(jnp.bfloat16)], 1
        )
        for way, reach in chain.reach.items():
            if reach:
                chain.send(way, token)
        chain.whole = jnp.zeros((chips, capacity, 2 * half_units), jnp.bfloat16)
        chain.place(token, 0)

    def gather(group, way, step):
        nonlocal token
        chain = chains[group]
        token = ordered(chain.came[way])
        chain.place(token, -way * step)
        if step < chain.reach[way]:
            chain.send(way, token)

    def back(whole, columns):
        return lax.dot_general(
            whole,
            weights[columns],
            (((1,), (1,)), ((), ())),
            preferred_element_type=jnp.float32,
        ).astype(jnp.bfloat16)

    arrived = {mask: swap(packed[mask], "expert", 2 * mask + 1) for mask in reversed(masks)}
    inputs = [
        [arrived[mask] for mask in masks],
        [swap(arrived[mask], "expert", 1) if mask else packed[0] for mask in masks],
    ]
    for group in range(2):
        begin(group)
    steps = range(1, n_fsdp)
    for step in steps:
        for group in range(2):
            for way, reach in chains[group].reach.items():
                if step < reach:
                    reduce(group, way, step)
    for group in range(2):
        activate(group)
    for step in steps:
        for group in range(2):
            for way, reach in chains[group].reach.items():
                if step <= reach:
                    gather(group, way, step)
    wholes = [chain.whole.reshape(chips * capacity, 2 * half_units) for chain in chains]

    taken = swap(back(wholes[0], slice(None)), "expert", 1)
    returned = []
    sums = wholes[1]
    for start in (0, feat_cols // 2):
        columns = slice(start, start + feat_cols // 2)
        sums = add_rounded(back(earlier(wholes[1], sums), columns), taken[:, columns])
        pieces = {}
        for mask in reversed(masks):
            rows = sums[mask * capacity : (mask + 1) * capacity]
            pieces[mask] = swap(rows, "expert", 2 * mask) if mask else rows
        returned.append([pieces[mask] for mask in masks])

    hidden = jnp.where(
        parity == 0, jnp.concatenate([hiddens[1], hiddens[0]], 0), jnp.concatenate(hiddens, 0)
    )
    grad_gate, grad_up = weight_grads(inputs[0] + inputs[1], wholes)
    grad_tokens = jnp.concatenate(
        [
            lax.dot_general(
                chooser,
                jnp.concatenate(pieces, 0),
                (((0,), (0,)), ((), ())),
                preferred_element_type=jnp.float32,
            ).astype(jnp.bfloat16)
            for pieces in returned
        ],
        1,
    )
    return (hidden[None], grad_gate, grad_up, grad_tokens)


def solution(mesh):
    in_specs = (
        P("expert", "fsdp"),
        P("expert", None),
        P("expert", "fsdp", None),
        P("expert", "fsdp", None),
        P("expert", None, None),
        P("expert", None, None),
        P("expert", "fsdp", None),
    )
    out_specs = (
        P("expert", "fsdp", None),
        P("expert", "fsdp", None),
        P("expert", "fsdp", None),
        P("expert", "fsdp"),
    )
    return jax.shard_map(
        on_device, mesh=mesh, in_specs=in_specs, out_specs=out_specs, check_vma=False
    )
```

```python
import math

import jax
import jax.numpy as jnp
from jax import lax
from jax.experimental import pallas as pl
from jax.experimental.pallas import tpu as pltpu
from jax.sharding import PartitionSpec as P


def swap(value, axis, mask):
    pairs = [(source, source ^ mask) for source in range(lax.axis_size(axis))]
    return lax.ppermute(value, axis, pairs)


def pick(blocks, index):
    return lax.dynamic_index_in_dim(blocks, index, 0, keepdims=False)


def scale_kernel(
    sub,
    start_ref,
    gate_ref,
    up_ref,
    gate_scale_ref,
    up_scale_ref,
    out_ref,
    gate_held,
    up_held,
    gate_rows,
    up_rows,
    sems,
):
    rows = out_ref.shape[0]
    half_units = gate_held.shape[1]
    step = pl.program_id(0)

    def arrival(which, turn):
        here = pl.ds(pl.multiple_of(turn * rows, rows), rows)
        value_ref, held = ((gate_ref, gate_held), (up_ref, up_held))[which]
        return pltpu.make_async_copy(
            value_ref.at[0, here, :], held.at[here, :], sems.at[which, turn]
        )

    @pl.when(step == 0)
    def _():
        for turn in range(gate_held.shape[0] // rows):
            for which in range(2):
                arrival(which, turn).start()
        shape = (gate_scale_ref.shape[1], half_units)
        spread = (
            lax.broadcasted_iota(jnp.int32, shape, 0)
            == lax.broadcasted_iota(jnp.int32, shape, 1) // 128
        ).astype(jnp.float32)
        for scale_ref, grown in ((gate_scale_ref, gate_rows), (up_scale_ref, up_rows)):
            grown[...] = lax.dot_general(
                scale_ref[0],
                spread,
                (((0,), (0,)), ((), ())),
                precision=lax.Precision.HIGHEST,
                preferred_element_type=jnp.float32,
            )

    for which, held, grown in ((0, gate_held, gate_rows), (1, up_held, up_rows)):
        arrival(which, step).wait()
        for piece in range(rows // sub):
            block = (start_ref[0] + step * rows + piece * sub) // 128
            there = pl.ds(pl.multiple_of(step * rows + piece * sub, sub), sub)
            scaled = held[there, :].astype(jnp.float32) * grown[pl.ds(block, 1), :]
            out_ref[piece * sub : (piece + 1) * sub, which * half_units : (which + 1) * half_units] = (
                scaled.astype(jnp.bfloat16)
            )


def scaled_weights(gate_values, up_values, gate_scales, up_scales, start_row):
    feat_cols, half_units = gate_values.shape[1:]
    sub = math.gcd(feat_cols, 128)
    rows = max(r for r in range(sub, 257, sub) if feat_cols % r == 0)
    gate_scales, up_scales = (jnp.swapaxes(value, 1, 2) for value in (gate_scales, up_scales))
    any_spec = pl.BlockSpec(memory_space=pl.ANY)
    scale_spec = pl.BlockSpec(gate_scales.shape, lambda i, start: (0, 0, 0))
    held = pltpu.VMEM((feat_cols, half_units), jnp.bfloat16)
    grown = pltpu.VMEM((gate_scales.shape[2], half_units), jnp.float32)
    return pl.pallas_call(
        lambda *refs: scale_kernel(sub, *refs),
        out_shape=jax.ShapeDtypeStruct((feat_cols, 2 * half_units), jnp.bfloat16),
        grid_spec=pltpu.PrefetchScalarGridSpec(
            num_scalar_prefetch=1,
            grid=(feat_cols // rows,),
            in_specs=[any_spec, any_spec, scale_spec, scale_spec],
            out_specs=pl.BlockSpec((rows, 2 * half_units), lambda i, start: (i, 0)),
            scratch_shapes=[
                held,
                held,
                grown,
                grown,
                pltpu.SemaphoreType.DMA((2, feat_cols // rows)),
            ],
        ),
        compiler_params=pltpu.CompilerParams(vmem_limit_bytes=16 * 2**20),
        cost_estimate=pl.CostEstimate(
            flops=2 * feat_cols * half_units,
            bytes_accessed=8 * feat_cols * half_units,
            transcendentals=0,
        ),
        name="scale_weights",
    )(
        start_row[None],
        pltpu.with_memory_space_constraint(gate_values, pltpu.HBM),
        pltpu.with_memory_space_constraint(up_values, pltpu.HBM),
        gate_scales,
        up_scales,
    )


def rows_of(counts_ref, expert):
    first = jnp.int32(0)
    live = jnp.int32(0)
    for other in range(counts_ref.shape[1]):
        count = counts_ref[0, other]
        first = first + jnp.where(other < expert, count, 0)
        live = jnp.where(other == expert, count, live)
    return first, live


def pack_kernel(chip_ref, counts_ref, tokens_ref, chooser_ref, *out_refs):
    row_total = tokens_ref.shape[0]
    capacity = out_refs[0].shape[0]
    row = lax.broadcasted_iota(jnp.int32, (capacity, row_total), 1)
    slot = lax.broadcasted_iota(jnp.int32, (capacity, row_total), 0)
    hits = []
    for mask in range(len(out_refs)):
        first, live = rows_of(counts_ref, chip_ref[0] ^ mask)
        hits.append(((row == first + slot) & (slot < live)).astype(jnp.float32))
    chooser = jnp.concatenate(hits, 0).astype(jnp.bfloat16)
    chooser_ref[...] = chooser
    chosen = jnp.dot(chooser, tokens_ref[...], preferred_element_type=jnp.float32)
    for mask, out_ref in enumerate(out_refs):
        out_ref[...] = chosen[mask * capacity : (mask + 1) * capacity].astype(jnp.bfloat16)


def packed_rows(tokens, counts, chip, capacity):
    row_total, feat_cols = tokens.shape
    experts = counts.shape[1]
    smem = pl.BlockSpec(memory_space=pltpu.SMEM)
    vmem = pl.BlockSpec(memory_space=pltpu.VMEM)
    block = jax.ShapeDtypeStruct((capacity, feat_cols), jnp.bfloat16)
    chooser, *packed = pl.pallas_call(
        pack_kernel,
        out_shape=(jax.ShapeDtypeStruct((experts * capacity, row_total), jnp.bfloat16),)
        + (block,) * experts,
        in_specs=[smem, smem, vmem],
        out_specs=(vmem,) * (experts + 1),
        cost_estimate=pl.CostEstimate(
            flops=2 * experts * capacity * row_total * feat_cols,
            bytes_accessed=2 * (row_total + experts * capacity) * feat_cols,
            transcendentals=0,
        ),
        name="pack_rows",
    )(chip[None], counts, tokens)
    return chooser, packed


def project_kernel(*refs):
    *block_refs, weight_ref, out_ref, held = refs
    capacity = block_refs[0].shape[0]

    @pl.when(pl.program_id(0) == 0)
    def _():
        for place, block_ref in enumerate(block_refs):
            held[place * capacity : (place + 1) * capacity, :] = block_ref[...]

    sums = jnp.dot(held[...], weight_ref[...], preferred_element_type=jnp.float32)
    for place in range(len(block_refs)):
        out_ref[place] = sums[place * capacity : (place + 1) * capacity].astype(jnp.bfloat16)


def projected(blocks, weights):
    count = len(blocks)
    capacity, feat_cols = blocks[0].shape
    units = weights.shape[1]
    tile = math.gcd(units, 1024)
    return pl.pallas_call(
        project_kernel,
        out_shape=jax.ShapeDtypeStruct((count, capacity, units), jnp.bfloat16),
        grid=(units // tile,),
        in_specs=[pl.BlockSpec((capacity, feat_cols), lambda i: (0, 0))] * count
        + [pl.BlockSpec((feat_cols, tile), lambda i: (0, i))],
        out_specs=pl.BlockSpec((count, capacity, tile), lambda i: (0, 0, i)),
        scratch_shapes=[pltpu.VMEM((count * capacity, feat_cols), jnp.bfloat16)],
        compiler_params=pltpu.CompilerParams(vmem_limit_bytes=24 * 2**20),
        cost_estimate=pl.CostEstimate(
            flops=2 * count * capacity * feat_cols * units,
            bytes_accessed=2 * (count * capacity * (feat_cols + units) + feat_cols * units),
            transcendentals=0,
        ),
        name="project",
    )(*blocks, pltpu.with_memory_space_constraint(weights, pltpu.VMEM))


def weight_kernel(count, *refs):
    input_refs, grad_refs = refs[:count], refs[count:-3]
    gate_ref, up_ref, held = refs[-3:]
    half_units = gate_ref.shape[2]

    @pl.when(pl.program_id(0) == 0)
    def _():
        place = 0
        for grad_ref in grad_refs:
            held[place : place + grad_ref.shape[0], :] = grad_ref[...]
            place += grad_ref.shape[0]

    inputs = jnp.concatenate([input_ref[...] for input_ref in input_refs], 0)
    for out_ref, offset in ((gate_ref, 0), (up_ref, half_units)):
        out_ref[0] = lax.dot_general(
            inputs,
            held[:, offset : offset + half_units],
            (((0,), (0,)), ((), ())),
            preferred_element_type=jnp.float32,
        ).astype(jnp.bfloat16)


def weight_grads(inputs, grads):
    count = len(inputs)
    rows = sum(value.shape[0] for value in inputs)
    feat_cols = inputs[0].shape[1]
    units = grads[0].shape[1]
    tile = 256 if feat_cols % 256 == 0 else feat_cols
    out = jax.ShapeDtypeStruct((1, feat_cols, units // 2), jnp.bfloat16)
    out_spec = pl.BlockSpec((1, tile, units // 2), lambda i: (0, i, 0))
    return pl.pallas_call(
        lambda *refs: weight_kernel(count, *refs),
        out_shape=(out, out),
        grid=(feat_cols // tile,),
        in_specs=[pl.BlockSpec((value.shape[0], tile), lambda i: (0, i)) for value in inputs]
        + [pl.BlockSpec(value.shape, lambda i: (0, 0)) for value in grads],
        out_specs=(out_spec, out_spec),
        scratch_shapes=[pltpu.VMEM((rows, units), jnp.bfloat16)],
        compiler_params=pltpu.CompilerParams(vmem_limit_bytes=16 * 2**20),
        cost_estimate=pl.CostEstimate(
            flops=2 * rows * feat_cols * units,
            bytes_accessed=2 * (rows * (feat_cols + units) + feat_cols * units),
            transcendentals=0,
        ),
        name="weight_grads",
    )(*inputs, *grads)


def earlier(value, *needed):
    return lax.optimization_barrier((value,) + needed)[0]


def add_rounded(first, second):
    return (first.astype(jnp.float32) + second.astype(jnp.float32)).astype(jnp.bfloat16)


class Chain:
    def __init__(self, chip, size):
        self.chip = chip
        self.size = size
        self.index = lax.axis_index("fsdp")
        self.reach = {1: size // 2, -1: size - 1 - size // 2}
        self.partial = None
        self.whole = None
        self.came = {}

    def owner(self, steps):
        return lax.rem(self.index + self.size + steps, self.size)

    def block(self, steps):
        return pick(self.partial, self.owner(steps) ^ self.chip)

    def send(self, way, value):
        ring = [(source, (source + way) % self.size) for source in range(self.size)]
        self.came[way] = lax.ppermute(value, "fsdp", ring)

    def place(self, value, steps):
        self.whole = lax.dynamic_update_index_in_dim(
            self.whole, value, self.owner(steps) ^ self.chip, 0
        )


def on_device(tokens, counts, gate_values, up_values, gate_scales, up_scales, grad_hidden):
    row_total, feat_cols = tokens.shape
    experts = counts.shape[1]
    capacity = min(4 * row_total // experts, row_total // 2)
    n_fsdp = lax.axis_size("fsdp")
    chips = lax.axis_size("expert") // 2
    half_units = gate_values.shape[2]
    parity = lax.axis_index("expert") % 2
    chip = lax.axis_index("expert") // 2
    index = lax.axis_index("fsdp")
    masks = range(chips)

    chooser, packed = packed_rows(tokens, counts, chip, capacity)
    weights = scaled_weights(
        gate_values, up_values, gate_scales, up_scales, index * feat_cols
    )
    cots = grad_hidden[0].reshape(2, capacity, half_units)
    chains = [Chain(chip, n_fsdp) for _ in range(2)]
    hiddens = [None, None]
    token = None

    def ordered(value):
        return value if token is None else earlier(value, token)

    def begin(group):
        nonlocal token
        chain = chains[group]
        chain.partial = projected(inputs[group], weights)
        for way, reach in chain.reach.items():
            if reach:
                token = ordered(chain.block(way * reach))
                chain.send(way, token)

    def reduce(group, way, step):
        nonlocal token
        chain = chains[group]
        token = add_rounded(
            chain.block(way * (chain.reach[way] - step)), ordered(chain.came[way])
        )
        chain.send(way, token)

    def activate(group):
        nonlocal token
        chain = chains[group]
        pre = chain.block(0).astype(jnp.float32)
        for came in chain.came.values():
            pre = pre + ordered(came).astype(jnp.float32)
        gate_pre = pre[:, :half_units]
        up_pre = pre[:, half_units:]
        cot = pick(cots, parity ^ (1 - group)).astype(jnp.float32)
        sigmoid_gate = jax.nn.sigmoid(gate_pre)
        hiddens[group] = (gate_pre * sigmoid_gate * up_pre).astype(jnp.bfloat16)
        grad_gate_pre = cot * up_pre * sigmoid_gate * (1.0 + gate_pre * (1.0 - sigmoid_gate))
        grad_up_pre = cot * gate_pre * sigmoid_gate
        token = jnp.concatenate(
            [grad_gate_pre.astype(jnp.bfloat16), grad_up_pre.astype(jnp.bfloat16)], 1
        )
        for way, reach in chain.reach.items():
            if reach:
                chain.send(way, token)
        chain.whole = jnp.zeros((chips, capacity, 2 * half_units), jnp.bfloat16)
        chain.place(token, 0)

    def gather(group, way, step):
        nonlocal token
        chain = chains[group]
        token = ordered(chain.came[way])
        chain.place(token, -way * step)
        if step < chain.reach[way]:
            chain.send(way, token)

    def back(whole):
        return lax.dot_general(
            whole, weights, (((1,), (1,)), ((), ())), preferred_element_type=jnp.float32
        ).astype(jnp.bfloat16)

    arrived = {mask: swap(packed[mask], "expert", 2 * mask + 1) for mask in reversed(masks)}
    inputs = [
        [arrived[mask] for mask in masks],
        [swap(arrived[mask], "expert", 1) if mask else packed[0] for mask in masks],
    ]
    for group in range(2):
        begin(group)
    steps = range(1, n_fsdp)
    for step in steps:
        for group in range(2):
            for way, reach in chains[group].reach.items():
                if step < reach:
                    reduce(group, way, step)
    for group in range(2):
        activate(group)
    for step in steps:
        for group in range(2):
            for way, reach in chains[group].reach.items():
                if step <= reach:
                    gather(group, way, step)
    wholes = [chain.whole.reshape(chips * capacity, 2 * half_units) for chain in chains]

    taken = swap(back(wholes[0]), "expert", 1)
    kept = back(earlier(wholes[1], taken))
    pieces = []
    for mask in masks:
        rows = slice(mask * capacity, (mask + 1) * capacity)
        both = add_rounded(kept[rows], taken[rows])
        pieces.append(swap(both, "expert", 2 * mask) if mask else both)

    hidden = jnp.where(
        parity == 0, jnp.concatenate([hiddens[1], hiddens[0]], 0), jnp.concatenate(hiddens, 0)
    )
    grad_gate, grad_up = weight_grads(inputs[0] + inputs[1], wholes)
    grad_tokens = lax.dot_general(
        chooser,
        jnp.concatenate(pieces, 0),
        (((0,), (0,)), ((), ())),
        preferred_element_type=jnp.float32,
    ).astype(jnp.bfloat16)
    return (hidden[None], grad_gate, grad_up, grad_tokens)


def solution(mesh):
    in_specs = (
        P("expert", "fsdp"),
        P("expert", None),
        P("expert", "fsdp", None),
        P("expert", "fsdp", None),
        P("expert", None, None),
        P("expert", None, None),
        P("expert", "fsdp", None),
    )
    out_specs = (
        P("expert", "fsdp", None),
        P("expert", "fsdp", None),
        P("expert", "fsdp", None),
        P("expert", "fsdp"),
    )
    return jax.shard_map(
        on_device, mesh=mesh, in_specs=in_specs, out_specs=out_specs, check_vma=False
    )
```

```python
import math

import jax
import jax.numpy as jnp
from jax import lax
from jax.experimental import pallas as pl
from jax.experimental.pallas import tpu as pltpu
from jax.sharding import PartitionSpec as P


def swap(value, axis, mask):
    pairs = [(source, source ^ mask) for source in range(lax.axis_size(axis))]
    return lax.ppermute(value, axis, pairs)


def pick(blocks, index):
    return lax.dynamic_index_in_dim(blocks, index, 0, keepdims=False)


def scale_kernel(
    sub,
    start_ref,
    gate_ref,
    up_ref,
    gate_scale_ref,
    up_scale_ref,
    out_ref,
    gate_held,
    up_held,
    gate_rows,
    up_rows,
    sems,
):
    rows = out_ref.shape[0]
    half_units = gate_held.shape[1]
    step = pl.program_id(0)

    def arrival(which, turn):
        here = pl.ds(pl.multiple_of(turn * rows, rows), rows)
        value_ref, held = ((gate_ref, gate_held), (up_ref, up_held))[which]
        return pltpu.make_async_copy(
            value_ref.at[0, here, :], held.at[here, :], sems.at[which, turn]
        )

    @pl.when(step == 0)
    def _():
        for turn in range(gate_held.shape[0] // rows):
            for which in range(2):
                arrival(which, turn).start()
        shape = (gate_scale_ref.shape[1], half_units)
        spread = (
            lax.broadcasted_iota(jnp.int32, shape, 0)
            == lax.broadcasted_iota(jnp.int32, shape, 1) // 128
        ).astype(jnp.float32)
        for scale_ref, grown in ((gate_scale_ref, gate_rows), (up_scale_ref, up_rows)):
            grown[...] = lax.dot_general(
                scale_ref[0],
                spread,
                (((0,), (0,)), ((), ())),
                precision=lax.Precision.HIGHEST,
                preferred_element_type=jnp.float32,
            )

    for which, held, grown in ((0, gate_held, gate_rows), (1, up_held, up_rows)):
        arrival(which, step).wait()
        for piece in range(rows // sub):
            block = (start_ref[0] + step * rows + piece * sub) // 128
            there = pl.ds(pl.multiple_of(step * rows + piece * sub, sub), sub)
            scaled = held[there, :].astype(jnp.float32) * grown[pl.ds(block, 1), :]
            out_ref[piece * sub : (piece + 1) * sub, which * half_units : (which + 1) * half_units] = (
                scaled.astype(jnp.bfloat16)
            )


def scaled_weights(gate_values, up_values, gate_scales, up_scales, start_row):
    feat_cols, half_units = gate_values.shape[1:]
    sub = math.gcd(feat_cols, 128)
    rows = max(r for r in range(sub, 257, sub) if feat_cols % r == 0)
    gate_scales, up_scales = (jnp.swapaxes(value, 1, 2) for value in (gate_scales, up_scales))
    any_spec = pl.BlockSpec(memory_space=pl.ANY)
    scale_spec = pl.BlockSpec(gate_scales.shape, lambda i, start: (0, 0, 0))
    held = pltpu.VMEM((feat_cols, half_units), jnp.bfloat16)
    grown = pltpu.VMEM((gate_scales.shape[2], half_units), jnp.float32)
    return pl.pallas_call(
        lambda *refs: scale_kernel(sub, *refs),
        out_shape=jax.ShapeDtypeStruct((feat_cols, 2 * half_units), jnp.bfloat16),
        grid_spec=pltpu.PrefetchScalarGridSpec(
            num_scalar_prefetch=1,
            grid=(feat_cols // rows,),
            in_specs=[any_spec, any_spec, scale_spec, scale_spec],
            out_specs=pl.BlockSpec((rows, 2 * half_units), lambda i, start: (i, 0)),
            scratch_shapes=[
                held,
                held,
                grown,
                grown,
                pltpu.SemaphoreType.DMA((2, feat_cols // rows)),
            ],
        ),
        compiler_params=pltpu.CompilerParams(vmem_limit_bytes=16 * 2**20),
        cost_estimate=pl.CostEstimate(
            flops=2 * feat_cols * half_units,
            bytes_accessed=8 * feat_cols * half_units,
            transcendentals=0,
        ),
        name="scale_weights",
    )(
        start_row[None],
        pltpu.with_memory_space_constraint(gate_values, pltpu.HBM),
        pltpu.with_memory_space_constraint(up_values, pltpu.HBM),
        gate_scales,
        up_scales,
    )


def rows_of(counts_ref, expert):
    first = jnp.int32(0)
    live = jnp.int32(0)
    for other in range(counts_ref.shape[1]):
        count = counts_ref[0, other]
        first = first + jnp.where(other < expert, count, 0)
        live = jnp.where(other == expert, count, live)
    return first, live


def pack_kernel(chip_ref, counts_ref, tokens_ref, chooser_ref, *out_refs):
    row_total = tokens_ref.shape[0]
    capacity = out_refs[0].shape[0]
    row = lax.broadcasted_iota(jnp.int32, (capacity, row_total), 1)
    slot = lax.broadcasted_iota(jnp.int32, (capacity, row_total), 0)
    hits = []
    for mask in range(len(out_refs)):
        first, live = rows_of(counts_ref, chip_ref[0] ^ mask)
        hits.append(((row == first + slot) & (slot < live)).astype(jnp.float32))
    chooser = jnp.concatenate(hits, 0).astype(jnp.bfloat16)
    chooser_ref[...] = chooser
    chosen = jnp.dot(chooser, tokens_ref[...], preferred_element_type=jnp.float32)
    for mask, out_ref in enumerate(out_refs):
        out_ref[...] = chosen[mask * capacity : (mask + 1) * capacity].astype(jnp.bfloat16)


def packed_rows(tokens, counts, chip, capacity):
    row_total, feat_cols = tokens.shape
    experts = counts.shape[1]
    smem = pl.BlockSpec(memory_space=pltpu.SMEM)
    vmem = pl.BlockSpec(memory_space=pltpu.VMEM)
    block = jax.ShapeDtypeStruct((capacity, feat_cols), jnp.bfloat16)
    chooser, *packed = pl.pallas_call(
        pack_kernel,
        out_shape=(jax.ShapeDtypeStruct((experts * capacity, row_total), jnp.bfloat16),)
        + (block,) * experts,
        in_specs=[smem, smem, vmem],
        out_specs=(vmem,) * (experts + 1),
        cost_estimate=pl.CostEstimate(
            flops=2 * experts * capacity * row_total * feat_cols,
            bytes_accessed=2 * (row_total + experts * capacity) * feat_cols,
            transcendentals=0,
        ),
        name="pack_rows",
    )(chip[None], counts, tokens)
    return chooser, packed


def project_kernel(*refs):
    *block_refs, weight_ref, out_ref, held = refs
    part = block_refs[0].shape[0]
    capacity = out_ref.shape[1]

    @pl.when(pl.program_id(0) == 0)
    def _():
        for place, block_ref in enumerate(block_refs):
            held[place * part : (place + 1) * part, :] = block_ref[...]

    sums = jnp.dot(held[...], weight_ref[...], preferred_element_type=jnp.float32)
    for owner in range(out_ref.shape[0]):
        out_ref[owner] = sums[owner * capacity : (owner + 1) * capacity].astype(jnp.bfloat16)


def projected(blocks, half, owners, weights):
    capacity, feat_cols = blocks[0].shape
    part = capacity // 2
    rows = len(blocks) * part
    units = weights.shape[1]
    tile = math.gcd(units, 1024)
    return pl.pallas_call(
        project_kernel,
        out_shape=jax.ShapeDtypeStruct((owners, rows // owners, units), jnp.bfloat16),
        grid=(units // tile,),
        in_specs=[pl.BlockSpec((part, feat_cols), lambda i: (half, 0))] * len(blocks)
        + [pl.BlockSpec((feat_cols, tile), lambda i: (0, i))],
        out_specs=pl.BlockSpec((owners, rows // owners, tile), lambda i: (0, 0, i)),
        scratch_shapes=[pltpu.VMEM((rows, feat_cols), jnp.bfloat16)],
        compiler_params=pltpu.CompilerParams(vmem_limit_bytes=24 * 2**20),
        cost_estimate=pl.CostEstimate(
            flops=2 * rows * feat_cols * units,
            bytes_accessed=2 * (rows * (feat_cols + units) + feat_cols * units),
            transcendentals=0,
        ),
        name="project",
    )(*blocks, pltpu.with_memory_space_constraint(weights, pltpu.VMEM))


def weight_kernel(count, *refs):
    block_refs, grad_ref, before_refs = refs[:count], refs[count], refs[count + 1 : -2]
    half_units = refs[-1].shape[2]
    inputs = jnp.concatenate([block_ref[...] for block_ref in block_refs], 0)
    for place, out_ref in enumerate(refs[-2:]):
        sums = lax.dot_general(
            inputs,
            grad_ref[:, place * half_units : (place + 1) * half_units],
            (((0,), (0,)), ((), ())),
            preferred_element_type=jnp.float32,
        )
        if before_refs:
            sums = sums + before_refs[place][0].astype(jnp.float32)
        out_ref[0] = sums.astype(jnp.bfloat16)


def weight_grads(blocks, half, grads, before=()):
    count = len(blocks)
    rows, units = grads.shape
    capacity, feat_cols = blocks[0].shape
    tile = 256 if feat_cols % 256 == 0 else feat_cols
    out = jax.ShapeDtypeStruct((1, feat_cols, units // 2), jnp.bfloat16)
    out_spec = pl.BlockSpec((1, tile, units // 2), lambda i: (0, i, 0))
    return pl.pallas_call(
        lambda *refs: weight_kernel(count, *refs),
        out_shape=(out, out),
        grid=(feat_cols // tile,),
        in_specs=[pl.BlockSpec((capacity // 2, tile), lambda i: (half, i))] * count
        + [pl.BlockSpec((rows, units), lambda i: (0, 0))]
        + [out_spec] * len(before),
        out_specs=(out_spec, out_spec),
        compiler_params=pltpu.CompilerParams(vmem_limit_bytes=16 * 2**20),
        cost_estimate=pl.CostEstimate(
            flops=2 * rows * feat_cols * units,
            bytes_accessed=2 * (rows * (feat_cols + units) + feat_cols * units),
            transcendentals=0,
        ),
        name="weight_grads",
    )(*blocks, grads, *before)


def earlier(value, *needed):
    return lax.optimization_barrier((value,) + needed)[0]


def add_rounded(first, second):
    return (first.astype(jnp.float32) + second.astype(jnp.float32)).astype(jnp.bfloat16)


class Chain:
    def __init__(self, chip, size):
        self.chip = chip
        self.size = size
        self.index = lax.axis_index("fsdp")
        self.reach = {1: size // 2, -1: size - 1 - size // 2}
        self.partial = None
        self.whole = None
        self.came = {}

    def owner(self, steps):
        return lax.rem(self.index + self.size + steps, self.size)

    def block(self, steps):
        return pick(self.partial, self.owner(steps) ^ self.chip)

    def send(self, way, value):
        ring = [(source, (source + way) % self.size) for source in range(self.size)]
        self.came[way] = lax.ppermute(value, "fsdp", ring)

    def place(self, value, steps):
        self.whole = lax.dynamic_update_index_in_dim(
            self.whole, value, self.owner(steps) ^ self.chip, 0
        )


def on_device(tokens, counts, gate_values, up_values, gate_scales, up_scales, grad_hidden):
    row_total, feat_cols = tokens.shape
    experts = counts.shape[1]
    capacity = min(4 * row_total // experts, row_total // 2)
    part = capacity // 2
    n_fsdp = lax.axis_size("fsdp")
    chips = lax.axis_size("expert") // 2
    half_units = gate_values.shape[2]
    parity = lax.axis_index("expert") % 2
    chip = lax.axis_index("expert") // 2
    index = lax.axis_index("fsdp")
    masks = range(chips)

    chooser, packed = packed_rows(tokens, counts, chip, capacity)
    weights = scaled_weights(
        gate_values, up_values, gate_scales, up_scales, index * feat_cols
    )
    cots = grad_hidden[0].reshape(2, 2, part, half_units)
    chains = [Chain(chip, n_fsdp) for _ in range(2)]
    hiddens = [None, None]
    token = None

    def ordered(value):
        return value if token is None else earlier(value, token)

    def begin(half):
        nonlocal token
        chain = chains[half]
        chain.partial = projected(inputs, half, chips, weights)
        for way, reach in chain.reach.items():
            if reach:
                token = ordered(chain.block(way * reach))
                chain.send(way, token)

    def reduce(half, way, step):
        nonlocal token
        chain = chains[half]
        token = add_rounded(
            chain.block(way * (chain.reach[way] - step)), ordered(chain.came[way])
        )
        chain.send(way, token)

    def activate(half):
        nonlocal token
        chain = chains[half]
        pre = chain.block(0).astype(jnp.float32)
        for came in chain.came.values():
            pre = pre + ordered(came).astype(jnp.float32)
        gate_pre = pre[:, :half_units]
        up_pre = pre[:, half_units:]
        cot = jnp.concatenate([pick(cots, 1 - parity)[half], pick(cots, parity)[half]], 0)
        cot = cot.astype(jnp.float32)
        sigmoid_gate = jax.nn.sigmoid(gate_pre)
        hiddens[half] = (gate_pre * sigmoid_gate * up_pre).astype(jnp.bfloat16)
        grad_gate_pre = cot * up_pre * sigmoid_gate * (1.0 + gate_pre * (1.0 - sigmoid_gate))
        grad_up_pre = cot * gate_pre * sigmoid_gate
        token = jnp.concatenate(
            [grad_gate_pre.astype(jnp.bfloat16), grad_up_pre.astype(jnp.bfloat16)], 1
        )
        for way, reach in chain.reach.items():
            if reach:
                chain.send(way, token)
        chain.whole = jnp.zeros((chips, capacity, 2 * half_units), jnp.bfloat16)
        chain.place(token, 0)

    def gather(half, step):
        nonlocal token
        chain = chains[half]
        for way, reach in chain.reach.items():
            if step <= reach:
                token = ordered(chain.came[way])
                chain.place(token, -way * step)
                if step < reach:
                    chain.send(way, token)

    def give_back(whole):
        back = lax.dot_general(
            whole, weights, (((1,), (1,)), ((), ())), preferred_element_type=jnp.float32
        ).astype(jnp.bfloat16)
        back = back.reshape(chips, 2, part, feat_cols)
        sums = add_rounded(back[:, 1], swap(back[:, 0], "expert", 1))
        return sums, [swap(sums[mask], "expert", 2 * mask) if mask else sums[0] for mask in masks]

    arrived = {mask: swap(packed[mask], "expert", 2 * mask + 1) for mask in reversed(masks)}
    inputs = []
    for mask in masks:
        inputs += [arrived[mask], swap(arrived[mask], "expert", 1) if mask else packed[0]]
    for half in range(2):
        begin(half)
    reach = chains[0].reach[1]
    for step in range(1, reach):
        for half in range(2):
            for way in chains[half].reach:
                if step < chains[half].reach[way]:
                    reduce(half, way, step)
    activate(0)
    for step in range(1, reach):
        gather(0, step)
    activate(1)
    gather(0, reach)
    whole = chains[0].whole.reshape(chips * capacity, 2 * half_units)
    token, low = give_back(whole)
    partly = weight_grads(inputs, 0, whole)
    for step in range(1, reach):
        gather(1, step)
    came, *kept = lax.optimization_barrier((chains[1].came[1], *low, *partly))
    chains[1].came[1], low, partly = came, kept[:chips], kept[chips:]
    gather(1, reach)
    whole = chains[1].whole.reshape(chips * capacity, 2 * half_units)
    sums, high = give_back(whole)

    own, other = (
        jnp.concatenate([rows[side * part : (side + 1) * part] for rows in hiddens], 0)
        for side in (1, 0)
    )
    hidden = jnp.where(
        parity == 0, jnp.concatenate([own, other], 0), jnp.concatenate([other, own], 0)
    )
    grad_gate, grad_up = weight_grads(inputs, 1, earlier(whole, sums), partly)
    grad_tokens = lax.dot_general(
        chooser,
        jnp.concatenate([pieces[mask] for mask in masks for pieces in (low, high)], 0),
        (((0,), (0,)), ((), ())),
        preferred_element_type=jnp.float32,
    ).astype(jnp.bfloat16)
    return (hidden[None], grad_gate, grad_up, grad_tokens)


def solution(mesh):
    in_specs = (
        P("expert", "fsdp"),
        P("expert", None),
        P("expert", "fsdp", None),
        P("expert", "fsdp", None),
        P("expert", None, None),
        P("expert", None, None),
        P("expert", "fsdp", None),
    )
    out_specs = (
        P("expert", "fsdp", None),
        P("expert", "fsdp", None),
        P("expert", "fsdp", None),
        P("expert", "fsdp"),
    )
    return jax.shard_map(
        on_device, mesh=mesh, in_specs=in_specs, out_specs=out_specs, check_vma=False
    )
```

```python
import math

import jax
import jax.numpy as jnp
from jax import lax
from jax.experimental import pallas as pl
from jax.experimental.pallas import tpu as pltpu
from jax.sharding import PartitionSpec as P


def swap(value, axis, mask):
    pairs = [(source, source ^ mask) for source in range(lax.axis_size(axis))]
    return lax.ppermute(value, axis, pairs)


def pick(blocks, index):
    return lax.dynamic_index_in_dim(blocks, index, 0, keepdims=False)


def scale_kernel(
    sub,
    start_ref,
    gate_ref,
    up_ref,
    gate_scale_ref,
    up_scale_ref,
    out_ref,
    gate_held,
    up_held,
    gate_rows,
    up_rows,
    sems,
):
    rows = out_ref.shape[0]
    half_units = gate_held.shape[1]
    step = pl.program_id(0)

    def arrival(which, turn):
        here = pl.ds(pl.multiple_of(turn * rows, rows), rows)
        value_ref, held = ((gate_ref, gate_held), (up_ref, up_held))[which]
        return pltpu.make_async_copy(
            value_ref.at[0, here, :], held.at[here, :], sems.at[which, turn]
        )

    @pl.when(step == 0)
    def _():
        for turn in range(gate_held.shape[0] // rows):
            for which in range(2):
                arrival(which, turn).start()
        shape = (gate_scale_ref.shape[1], half_units)
        spread = (
            lax.broadcasted_iota(jnp.int32, shape, 0)
            == lax.broadcasted_iota(jnp.int32, shape, 1) // 128
        ).astype(jnp.float32)
        for scale_ref, grown in ((gate_scale_ref, gate_rows), (up_scale_ref, up_rows)):
            grown[...] = lax.dot_general(
                scale_ref[0],
                spread,
                (((0,), (0,)), ((), ())),
                precision=lax.Precision.HIGHEST,
                preferred_element_type=jnp.float32,
            )

    for which, held, grown in ((0, gate_held, gate_rows), (1, up_held, up_rows)):
        arrival(which, step).wait()
        for piece in range(rows // sub):
            block = (start_ref[0] + step * rows + piece * sub) // 128
            there = pl.ds(pl.multiple_of(step * rows + piece * sub, sub), sub)
            scaled = held[there, :].astype(jnp.float32) * grown[pl.ds(block, 1), :]
            out_ref[piece * sub : (piece + 1) * sub, which * half_units : (which + 1) * half_units] = (
                scaled.astype(jnp.bfloat16)
            )


def scaled_weights(gate_values, up_values, gate_scales, up_scales, start_row):
    feat_cols, half_units = gate_values.shape[1:]
    sub = math.gcd(feat_cols, 128)
    rows = max(r for r in range(sub, 257, sub) if feat_cols % r == 0)
    gate_scales, up_scales = (jnp.swapaxes(value, 1, 2) for value in (gate_scales, up_scales))
    any_spec = pl.BlockSpec(memory_space=pl.ANY)
    scale_spec = pl.BlockSpec(gate_scales.shape, lambda i, start: (0, 0, 0))
    held = pltpu.VMEM((feat_cols, half_units), jnp.bfloat16)
    grown = pltpu.VMEM((gate_scales.shape[2], half_units), jnp.float32)
    return pl.pallas_call(
        lambda *refs: scale_kernel(sub, *refs),
        out_shape=jax.ShapeDtypeStruct((feat_cols, 2 * half_units), jnp.bfloat16),
        grid_spec=pltpu.PrefetchScalarGridSpec(
            num_scalar_prefetch=1,
            grid=(feat_cols // rows,),
            in_specs=[any_spec, any_spec, scale_spec, scale_spec],
            out_specs=pl.BlockSpec((rows, 2 * half_units), lambda i, start: (i, 0)),
            scratch_shapes=[
                held,
                held,
                grown,
                grown,
                pltpu.SemaphoreType.DMA((2, feat_cols // rows)),
            ],
        ),
        compiler_params=pltpu.CompilerParams(vmem_limit_bytes=16 * 2**20),
        cost_estimate=pl.CostEstimate(
            flops=2 * feat_cols * half_units,
            bytes_accessed=8 * feat_cols * half_units,
            transcendentals=0,
        ),
        name="scale_weights",
    )(
        start_row[None],
        pltpu.with_memory_space_constraint(gate_values, pltpu.HBM),
        pltpu.with_memory_space_constraint(up_values, pltpu.HBM),
        gate_scales,
        up_scales,
    )


def rows_of(counts_ref, expert):
    first = jnp.int32(0)
    live = jnp.int32(0)
    for other in range(counts_ref.shape[1]):
        count = counts_ref[0, other]
        first = first + jnp.where(other < expert, count, 0)
        live = jnp.where(other == expert, count, live)
    return first, live


def pack_kernel(counts_ref, tokens_ref, chooser_ref, *out_refs):
    chip = lax.axis_index("expert") // 2
    row_total = tokens_ref.shape[0]
    capacity = out_refs[0].shape[0]
    row = lax.broadcasted_iota(jnp.int32, (capacity, row_total), 1)
    slot = lax.broadcasted_iota(jnp.int32, (capacity, row_total), 0)
    hits = []
    for mask in range(len(out_refs)):
        first, live = rows_of(counts_ref, chip ^ mask)
        hits.append(((row == first + slot) & (slot < live)).astype(jnp.float32))
    chooser = jnp.concatenate(hits, 0).astype(jnp.bfloat16)
    chooser_ref[...] = chooser
    chosen = jnp.dot(chooser, tokens_ref[...], preferred_element_type=jnp.float32)
    for mask, out_ref in enumerate(out_refs):
        out_ref[...] = chosen[mask * capacity : (mask + 1) * capacity].astype(jnp.bfloat16)


def packed_rows(tokens, counts, capacity):
    row_total, feat_cols = tokens.shape
    experts = counts.shape[1]
    tile = feat_cols // 2 if feat_cols % 256 == 0 else feat_cols
    block = jax.ShapeDtypeStruct((capacity, feat_cols), jnp.bfloat16)
    chooser, *packed = pl.pallas_call(
        pack_kernel,
        out_shape=(jax.ShapeDtypeStruct((experts * capacity, row_total), jnp.bfloat16),)
        + (block,) * experts,
        grid=(feat_cols // tile,),
        in_specs=[
            pl.BlockSpec(memory_space=pltpu.SMEM),
            pl.BlockSpec((row_total, tile), lambda i: (0, i)),
        ],
        out_specs=(pl.BlockSpec((experts * capacity, row_total), lambda i: (0, 0)),)
        + (pl.BlockSpec((capacity, tile), lambda i: (0, i)),) * experts,
        cost_estimate=pl.CostEstimate(
            flops=2 * experts * capacity * row_total * feat_cols,
            bytes_accessed=2 * (row_total + experts * capacity) * feat_cols,
            transcendentals=0,
        ),
        name="pack_rows",
    )(counts, pltpu.with_memory_space_constraint(tokens, pltpu.HBM))
    return chooser, packed


def project_kernel(*refs):
    *block_refs, weight_ref, out_ref, held = refs
    capacity = block_refs[0].shape[0]

    @pl.when(pl.program_id(0) == 0)
    def _():
        for place, block_ref in enumerate(block_refs):
            held[place * capacity : (place + 1) * capacity, :] = block_ref[...]

    sums = jnp.dot(held[...], weight_ref[...], preferred_element_type=jnp.float32)
    for place in range(len(block_refs)):
        out_ref[place] = sums[place * capacity : (place + 1) * capacity].astype(jnp.bfloat16)


def projected(blocks, weights):
    count = len(blocks)
    capacity, feat_cols = blocks[0].shape
    units = weights.shape[1]
    tile = units
    return pl.pallas_call(
        project_kernel,
        out_shape=jax.ShapeDtypeStruct((count, capacity, units), jnp.bfloat16),
        grid=(units // tile,),
        in_specs=[pl.BlockSpec((capacity, feat_cols), lambda i: (0, 0))] * count
        + [pl.BlockSpec((feat_cols, tile), lambda i: (0, i))],
        out_specs=pl.BlockSpec((count, capacity, tile), lambda i: (0, 0, i)),
        scratch_shapes=[pltpu.VMEM((count * capacity, feat_cols), jnp.bfloat16)],
        compiler_params=pltpu.CompilerParams(vmem_limit_bytes=24 * 2**20),
        cost_estimate=pl.CostEstimate(
            flops=2 * count * capacity * feat_cols * units,
            bytes_accessed=2 * (count * capacity * (feat_cols + units) + feat_cols * units),
            transcendentals=0,
        ),
        name="project",
    )(*blocks, pltpu.with_memory_space_constraint(weights, pltpu.VMEM))


def weight_kernel(count, *refs):
    input_refs, grad_refs = refs[:count], refs[count:-3]
    gate_ref, up_ref, held = refs[-3:]
    half_units = gate_ref.shape[2]

    @pl.when(pl.program_id(0) == 0)
    def _():
        place = 0
        for grad_ref in grad_refs:
            held[place : place + grad_ref.shape[0], :] = grad_ref[...]
            place += grad_ref.shape[0]

    inputs = jnp.concatenate([input_ref[...] for input_ref in input_refs], 0)
    for out_ref, offset in ((gate_ref, 0), (up_ref, half_units)):
        out_ref[0] = lax.dot_general(
            inputs,
            held[:, offset : offset + half_units],
            (((0,), (0,)), ((), ())),
            preferred_element_type=jnp.float32,
        ).astype(jnp.bfloat16)


def weight_grads(inputs, grads):
    count = len(inputs)
    rows = sum(value.shape[0] for value in inputs)
    feat_cols = inputs[0].shape[1]
    units = grads[0].shape[1]
    tile = 256 if feat_cols % 256 == 0 else feat_cols
    out = jax.ShapeDtypeStruct((1, feat_cols, units // 2), jnp.bfloat16)
    out_spec = pl.BlockSpec((1, tile, units // 2), lambda i: (0, i, 0))
    return pl.pallas_call(
        lambda *refs: weight_kernel(count, *refs),
        out_shape=(out, out),
        grid=(feat_cols // tile,),
        in_specs=[pl.BlockSpec((value.shape[0], tile), lambda i: (0, i)) for value in inputs]
        + [pl.BlockSpec(value.shape, lambda i: (0, 0)) for value in grads],
        out_specs=(out_spec, out_spec),
        scratch_shapes=[pltpu.VMEM((rows, units), jnp.bfloat16)],
        compiler_params=pltpu.CompilerParams(vmem_limit_bytes=16 * 2**20),
        cost_estimate=pl.CostEstimate(
            flops=2 * rows * feat_cols * units,
            bytes_accessed=2 * (rows * (feat_cols + units) + feat_cols * units),
            transcendentals=0,
        ),
        name="weight_grads",
    )(*inputs, *grads)


def earlier(value, *needed):
    return lax.optimization_barrier((value,) + needed)[0]


def add_rounded(first, second):
    return (first.astype(jnp.float32) + second.astype(jnp.float32)).astype(jnp.bfloat16)


class Chain:
    def __init__(self, chip, size):
        self.chip = chip
        self.size = size
        self.index = lax.axis_index("fsdp")
        self.reach = {1: size // 2, -1: size - 1 - size // 2}
        self.partial = None
        self.whole = None
        self.came = {}

    def owner(self, steps):
        return lax.rem(self.index + self.size + steps, self.size)

    def block(self, steps):
        return pick(self.partial, self.owner(steps) ^ self.chip)

    def send(self, way, value):
        ring = [(source, (source + way) % self.size) for source in range(self.size)]
        self.came[way] = lax.ppermute(value, "fsdp", ring)

    def place(self, value, steps):
        self.whole = lax.dynamic_update_index_in_dim(
            self.whole, value, self.owner(steps) ^ self.chip, 0
        )


def on_device(tokens, counts, gate_values, up_values, gate_scales, up_scales, grad_hidden):
    row_total, feat_cols = tokens.shape
    experts = counts.shape[1]
    capacity = min(4 * row_total // experts, row_total // 2)
    n_fsdp = lax.axis_size("fsdp")
    chips = lax.axis_size("expert") // 2
    half_units = gate_values.shape[2]
    parity = lax.axis_index("expert") % 2
    chip = lax.axis_index("expert") // 2
    index = lax.axis_index("fsdp")
    masks = range(chips)

    chooser, packed = packed_rows(tokens, counts, capacity)
    weights = scaled_weights(
        gate_values, up_values, gate_scales, up_scales, index * feat_cols
    )
    cots = grad_hidden[0].reshape(2, capacity, half_units)
    chains = [Chain(chip, n_fsdp) for _ in range(2)]
    hiddens = [None, None]
    token = None

    def ordered(value):
        return value if token is None else earlier(value, token)

    def begin(group):
        nonlocal token
        chain = chains[group]
        chain.partial = projected(inputs[group], weights)
        for way, reach in chain.reach.items():
            if reach:
                token = ordered(chain.block(way * reach))
                chain.send(way, token)

    def reduce(group, way, step):
        nonlocal token
        chain = chains[group]
        token = add_rounded(
            chain.block(way * (chain.reach[way] - step)), ordered(chain.came[way])
        )
        chain.send(way, token)

    def activate(group):
        nonlocal token
        chain = chains[group]
        pre = chain.block(0).astype(jnp.float32)
        for came in chain.came.values():
            pre = pre + ordered(came).astype(jnp.float32)
        gate_pre = pre[:, :half_units]
        up_pre = pre[:, half_units:]
        cot = pick(cots, parity ^ (1 - group)).astype(jnp.float32)
        sigmoid_gate = jax.nn.sigmoid(gate_pre)
        hiddens[group] = (gate_pre * sigmoid_gate * up_pre).astype(jnp.bfloat16)
        grad_gate_pre = cot * up_pre * sigmoid_gate * (1.0 + gate_pre * (1.0 - sigmoid_gate))
        grad_up_pre = cot * gate_pre * sigmoid_gate
        token = jnp.concatenate(
            [grad_gate_pre.astype(jnp.bfloat16), grad_up_pre.astype(jnp.bfloat16)], 1
        )
        for way, reach in chain.reach.items():
            if reach:
                chain.send(way, token)
        chain.whole = jnp.zeros((chips, capacity, 2 * half_units), jnp.bfloat16)
        chain.place(token, 0)

    def gather(group, way, step):
        nonlocal token
        chain = chains[group]
        token = ordered(chain.came[way])
        chain.place(token, -way * step)
        if step < chain.reach[way]:
            chain.send(way, token)

    def back(whole):
        return lax.dot_general(
            whole, weights, (((1,), (1,)), ((), ())), preferred_element_type=jnp.float32
        ).astype(jnp.bfloat16)

    arrived = {mask: swap(packed[mask], "expert", 2 * mask + 1) for mask in reversed(masks)}
    inputs = [
        [arrived[mask] for mask in masks],
        [swap(arrived[mask], "expert", 1) if mask else packed[0] for mask in masks],
    ]
    for group in range(2):
        begin(group)
    steps = range(1, n_fsdp)
    for step in steps:
        for group in range(2):
            for way, reach in chains[group].reach.items():
                if step < reach:
                    reduce(group, way, step)
    for group in range(2):
        activate(group)
    for step in steps:
        for group in range(2):
            for way, reach in chains[group].reach.items():
                if step <= reach:
                    gather(group, way, step)
    wholes = [chain.whole.reshape(chips * capacity, 2 * half_units) for chain in chains]

    taken = swap(back(wholes[0]), "expert", 1)
    kept = back(earlier(wholes[1], taken))
    pieces = []
    for mask in masks:
        rows = slice(mask * capacity, (mask + 1) * capacity)
        both = add_rounded(kept[rows], taken[rows])
        pieces.append(swap(both, "expert", 2 * mask) if mask else both)

    hidden = jnp.where(
        parity == 0, jnp.concatenate([hiddens[1], hiddens[0]], 0), jnp.concatenate(hiddens, 0)
    )
    grad_gate, grad_up = weight_grads(inputs[0] + inputs[1], wholes)
    grad_tokens = lax.dot_general(
        chooser,
        jnp.concatenate(pieces, 0),
        (((0,), (0,)), ((), ())),
        preferred_element_type=jnp.float32,
    ).astype(jnp.bfloat16)
    return (hidden[None], grad_gate, grad_up, grad_tokens)


def solution(mesh):
    in_specs = (
        P("expert", "fsdp"),
        P("expert", None),
        P("expert", "fsdp", None),
        P("expert", "fsdp", None),
        P("expert", None, None),
        P("expert", None, None),
        P("expert", "fsdp", None),
    )
    out_specs = (
        P("expert", "fsdp", None),
        P("expert", "fsdp", None),
        P("expert", "fsdp", None),
        P("expert", "fsdp"),
    )
    return jax.shard_map(
        on_device, mesh=mesh, in_specs=in_specs, out_specs=out_specs, check_vma=False
    )
```

```python
import math

import jax
import jax.numpy as jnp
from jax import lax
from jax.experimental import pallas as pl
from jax.experimental.pallas import tpu as pltpu
from jax.sharding import PartitionSpec as P


def swap(value, axis, mask):
    pairs = [(source, source ^ mask) for source in range(lax.axis_size(axis))]
    return lax.ppermute(value, axis, pairs)


def pick(blocks, index):
    return lax.dynamic_index_in_dim(blocks, index, 0, keepdims=False)


def scale_kernel(
    sub,
    start_ref,
    gate_ref,
    up_ref,
    gate_scale_ref,
    up_scale_ref,
    out_ref,
    gate_held,
    up_held,
    gate_rows,
    up_rows,
    sems,
):
    rows = out_ref.shape[0]
    half_units = gate_held.shape[1]
    step = pl.program_id(0)

    def arrival(which, turn):
        here = pl.ds(pl.multiple_of(turn * rows, rows), rows)
        value_ref, held = ((gate_ref, gate_held), (up_ref, up_held))[which]
        return pltpu.make_async_copy(
            value_ref.at[0, here, :], held.at[here, :], sems.at[which, turn]
        )

    @pl.when(step == 0)
    def _():
        for turn in range(gate_held.shape[0] // rows):
            for which in range(2):
                arrival(which, turn).start()
        shape = (gate_scale_ref.shape[1], half_units)
        spread = (
            lax.broadcasted_iota(jnp.int32, shape, 0)
            == lax.broadcasted_iota(jnp.int32, shape, 1) // 128
        ).astype(jnp.float32)
        for scale_ref, grown in ((gate_scale_ref, gate_rows), (up_scale_ref, up_rows)):
            grown[...] = lax.dot_general(
                scale_ref[0],
                spread,
                (((0,), (0,)), ((), ())),
                precision=lax.Precision.HIGHEST,
                preferred_element_type=jnp.float32,
            )

    for which, held, grown in ((0, gate_held, gate_rows), (1, up_held, up_rows)):
        arrival(which, step).wait()
        for piece in range(rows // sub):
            block = (start_ref[0] + step * rows + piece * sub) // 128
            there = pl.ds(pl.multiple_of(step * rows + piece * sub, sub), sub)
            scaled = held[there, :].astype(jnp.float32) * grown[pl.ds(block, 1), :]
            out_ref[piece * sub : (piece + 1) * sub, which * half_units : (which + 1) * half_units] = (
                scaled.astype(jnp.bfloat16)
            )


def scaled_weights(gate_values, up_values, gate_scales, up_scales, start_row):
    feat_cols, half_units = gate_values.shape[1:]
    sub = math.gcd(feat_cols, 128)
    rows = max(r for r in range(sub, 257, sub) if feat_cols % r == 0)
    gate_scales, up_scales = (jnp.swapaxes(value, 1, 2) for value in (gate_scales, up_scales))
    any_spec = pl.BlockSpec(memory_space=pl.ANY)
    scale_spec = pl.BlockSpec(gate_scales.shape, lambda i, start: (0, 0, 0))
    held = pltpu.VMEM((feat_cols, half_units), jnp.bfloat16)
    grown = pltpu.VMEM((gate_scales.shape[2], half_units), jnp.float32)
    return pl.pallas_call(
        lambda *refs: scale_kernel(sub, *refs),
        out_shape=jax.ShapeDtypeStruct((feat_cols, 2 * half_units), jnp.bfloat16),
        grid_spec=pltpu.PrefetchScalarGridSpec(
            num_scalar_prefetch=1,
            grid=(feat_cols // rows,),
            in_specs=[any_spec, any_spec, scale_spec, scale_spec],
            out_specs=pl.BlockSpec((rows, 2 * half_units), lambda i, start: (i, 0)),
            scratch_shapes=[
                held,
                held,
                grown,
                grown,
                pltpu.SemaphoreType.DMA((2, feat_cols // rows)),
            ],
        ),
        compiler_params=pltpu.CompilerParams(vmem_limit_bytes=16 * 2**20),
        cost_estimate=pl.CostEstimate(
            flops=2 * feat_cols * half_units,
            bytes_accessed=8 * feat_cols * half_units,
            transcendentals=0,
        ),
        name="scale_weights",
    )(
        start_row[None],
        pltpu.with_memory_space_constraint(gate_values, pltpu.HBM),
        pltpu.with_memory_space_constraint(up_values, pltpu.HBM),
        gate_scales,
        up_scales,
    )


def pack_kernel(counts_ref, tokens_ref, chooser_ref, *out_refs):
    chip = lax.axis_index("expert") // 2
    row_total = tokens_ref.shape[0]
    capacity = out_refs[0].shape[0]
    counts = counts_ref[...].astype(jnp.float32)
    expert = lax.broadcasted_iota(jnp.int32, counts.shape, 1)
    row = lax.broadcasted_iota(jnp.int32, (capacity, row_total), 1).astype(jnp.float32)
    slot = lax.broadcasted_iota(jnp.int32, (capacity, row_total), 0).astype(jnp.float32)
    hits = []
    for mask in range(len(out_refs)):
        first = jnp.sum(jnp.where(expert < (chip ^ mask), counts, 0.0), 1, keepdims=True)
        live = jnp.sum(jnp.where(expert == (chip ^ mask), counts, 0.0), 1, keepdims=True)
        hits.append(((row == first + slot) & (slot < live)).astype(jnp.float32))
    chooser = jnp.concatenate(hits, 0).astype(jnp.bfloat16)
    chooser_ref[...] = chooser
    chosen = jnp.dot(chooser, tokens_ref[...], preferred_element_type=jnp.float32)
    for mask, out_ref in enumerate(out_refs):
        out_ref[...] = chosen[mask * capacity : (mask + 1) * capacity].astype(jnp.bfloat16)


def packed_rows(tokens, counts, capacity):
    row_total, feat_cols = tokens.shape
    experts = counts.shape[1]
    tile = feat_cols // 2 if feat_cols % 256 == 0 else feat_cols
    block = jax.ShapeDtypeStruct((capacity, feat_cols), jnp.bfloat16)
    chooser, *packed = pl.pallas_call(
        pack_kernel,
        out_shape=(jax.ShapeDtypeStruct((experts * capacity, row_total), jnp.bfloat16),)
        + (block,) * experts,
        grid=(feat_cols // tile,),
        in_specs=[
            pl.BlockSpec(counts.shape, lambda i: (0, 0)),
            pl.BlockSpec((row_total, tile), lambda i: (0, i)),
        ],
        out_specs=(pl.BlockSpec((experts * capacity, row_total), lambda i: (0, 0)),)
        + (pl.BlockSpec((capacity, tile), lambda i: (0, i)),) * experts,
        cost_estimate=pl.CostEstimate(
            flops=2 * experts * capacity * row_total * feat_cols,
            bytes_accessed=2 * (row_total + experts * capacity) * feat_cols,
            transcendentals=0,
        ),
        name="pack_rows",
    )(counts, pltpu.with_memory_space_constraint(tokens, pltpu.HBM))
    return chooser, packed


def project_kernel(*refs):
    *block_refs, weight_ref, out_ref, held = refs
    capacity = block_refs[0].shape[0]

    @pl.when(pl.program_id(0) == 0)
    def _():
        for place, block_ref in enumerate(block_refs):
            held[place * capacity : (place + 1) * capacity, :] = block_ref[...]

    sums = jnp.dot(held[...], weight_ref[...], preferred_element_type=jnp.float32)
    for place in range(len(block_refs)):
        out_ref[place] = sums[place * capacity : (place + 1) * capacity].astype(jnp.bfloat16)


def projected(blocks, weights):
    count = len(blocks)
    capacity, feat_cols = blocks[0].shape
    units = weights.shape[1]
    tile = units
    return pl.pallas_call(
        project_kernel,
        out_shape=jax.ShapeDtypeStruct((count, capacity, units), jnp.bfloat16),
        grid=(units // tile,),
        in_specs=[pl.BlockSpec((capacity, feat_cols), lambda i: (0, 0))] * count
        + [pl.BlockSpec((feat_cols, tile), lambda i: (0, i))],
        out_specs=pl.BlockSpec((count, capacity, tile), lambda i: (0, 0, i)),
        scratch_shapes=[pltpu.VMEM((count * capacity, feat_cols), jnp.bfloat16)],
        compiler_params=pltpu.CompilerParams(vmem_limit_bytes=24 * 2**20),
        cost_estimate=pl.CostEstimate(
            flops=2 * count * capacity * feat_cols * units,
            bytes_accessed=2 * (count * capacity * (feat_cols + units) + feat_cols * units),
            transcendentals=0,
        ),
        name="project",
    )(*blocks, pltpu.with_memory_space_constraint(weights, pltpu.VMEM))


def weight_kernel(count, *refs):
    input_refs, grad_refs = refs[:count], refs[count:-3]
    gate_ref, up_ref, held = refs[-3:]
    half_units = gate_ref.shape[2]

    @pl.when(pl.program_id(0) == 0)
    def _():
        place = 0
        for grad_ref in grad_refs:
            held[place : place + grad_ref.shape[0], :] = grad_ref[...]
            place += grad_ref.shape[0]

    inputs = jnp.concatenate([input_ref[...] for input_ref in input_refs], 0)
    for out_ref, offset in ((gate_ref, 0), (up_ref, half_units)):
        out_ref[0] = lax.dot_general(
            inputs,
            held[:, offset : offset + half_units],
            (((0,), (0,)), ((), ())),
            preferred_element_type=jnp.float32,
        ).astype(jnp.bfloat16)


def weight_grads(inputs, grads):
    count = len(inputs)
    rows = sum(value.shape[0] for value in inputs)
    feat_cols = inputs[0].shape[1]
    units = grads[0].shape[1]
    tile = 256 if feat_cols % 256 == 0 else feat_cols
    out = jax.ShapeDtypeStruct((1, feat_cols, units // 2), jnp.bfloat16)
    out_spec = pl.BlockSpec((1, tile, units // 2), lambda i: (0, i, 0))
    return pl.pallas_call(
        lambda *refs: weight_kernel(count, *refs),
        out_shape=(out, out),
        grid=(feat_cols // tile,),
        in_specs=[pl.BlockSpec((value.shape[0], tile), lambda i: (0, i)) for value in inputs]
        + [pl.BlockSpec(value.shape, lambda i: (0, 0)) for value in grads],
        out_specs=(out_spec, out_spec),
        scratch_shapes=[pltpu.VMEM((rows, units), jnp.bfloat16)],
        compiler_params=pltpu.CompilerParams(vmem_limit_bytes=16 * 2**20),
        cost_estimate=pl.CostEstimate(
            flops=2 * rows * feat_cols * units,
            bytes_accessed=2 * (rows * (feat_cols + units) + feat_cols * units),
            transcendentals=0,
        ),
        name="weight_grads",
    )(*inputs, *grads)


def earlier(value, *needed):
    return lax.optimization_barrier((value,) + needed)[0]


def add_rounded(first, second):
    return (first.astype(jnp.float32) + second.astype(jnp.float32)).astype(jnp.bfloat16)


class Chain:
    def __init__(self, chip, size):
        self.chip = chip
        self.size = size
        self.index = lax.axis_index("fsdp")
        self.reach = {1: size // 2, -1: size - 1 - size // 2}
        self.partial = None
        self.whole = None
        self.came = {}

    def owner(self, steps):
        return lax.rem(self.index + self.size + steps, self.size)

    def block(self, steps):
        return pick(self.partial, self.owner(steps) ^ self.chip)

    def send(self, way, value):
        ring = [(source, (source + way) % self.size) for source in range(self.size)]
        self.came[way] = lax.ppermute(value, "fsdp", ring)

    def place(self, value, steps):
        self.whole = lax.dynamic_update_index_in_dim(
            self.whole, value, self.owner(steps) ^ self.chip, 0
        )


def on_device(tokens, counts, gate_values, up_values, gate_scales, up_scales, grad_hidden):
    row_total, feat_cols = tokens.shape
    experts = counts.shape[1]
    capacity = min(4 * row_total // experts, row_total // 2)
    n_fsdp = lax.axis_size("fsdp")
    chips = lax.axis_size("expert") // 2
    half_units = gate_values.shape[2]
    parity = lax.axis_index("expert") % 2
    chip = lax.axis_index("expert") // 2
    index = lax.axis_index("fsdp")
    masks = range(chips)

    chooser, packed = packed_rows(tokens, counts, capacity)
    weights = scaled_weights(
        gate_values, up_values, gate_scales, up_scales, index * feat_cols
    )
    cots = grad_hidden[0].reshape(2, capacity, half_units)
    chains = [Chain(chip, n_fsdp) for _ in range(2)]
    hiddens = [None, None]
    token = None

    def ordered(value):
        return value if token is None else earlier(value, token)

    def begin(group):
        nonlocal token
        chain = chains[group]
        chain.partial = projected(inputs[group], weights)
        for way, reach in chain.reach.items():
            if reach:
                token = ordered(chain.block(way * reach))
                chain.send(way, token)

    def reduce(group, way, step):
        nonlocal token
        chain = chains[group]
        token = add_rounded(
            chain.block(way * (chain.reach[way] - step)), ordered(chain.came[way])
        )
        chain.send(way, token)

    def activate(group):
        nonlocal token
        chain = chains[group]
        pre = chain.block(0).astype(jnp.float32)
        for came in chain.came.values():
            pre = pre + ordered(came).astype(jnp.float32)
        gate_pre = pre[:, :half_units]
        up_pre = pre[:, half_units:]
        cot = pick(cots, parity ^ (1 - group)).astype(jnp.float32)
        sigmoid_gate = jax.nn.sigmoid(gate_pre)
        hiddens[group] = (gate_pre * sigmoid_gate * up_pre).astype(jnp.bfloat16)
        grad_gate_pre = cot * up_pre * sigmoid_gate * (1.0 + gate_pre * (1.0 - sigmoid_gate))
        grad_up_pre = cot * gate_pre * sigmoid_gate
        token = jnp.concatenate(
            [grad_gate_pre.astype(jnp.bfloat16), grad_up_pre.astype(jnp.bfloat16)], 1
        )
        for way, reach in chain.reach.items():
            if reach:
                chain.send(way, token)
        chain.whole = jnp.zeros((chips, capacity, 2 * half_units), jnp.bfloat16)
        chain.place(token, 0)

    def gather(group, way, step):
        nonlocal token
        chain = chains[group]
        token = ordered(chain.came[way])
        chain.place(token, -way * step)
        if step < chain.reach[way]:
            chain.send(way, token)

    def back(whole):
        return lax.dot_general(
            whole, weights, (((1,), (1,)), ((), ())), preferred_element_type=jnp.float32
        ).astype(jnp.bfloat16)

    arrived = {mask: swap(packed[mask], "expert", 2 * mask + 1) for mask in reversed(masks)}
    inputs = [
        [arrived[mask] for mask in masks],
        [swap(arrived[mask], "expert", 1) if mask else packed[0] for mask in masks],
    ]
    for group in range(2):
        begin(group)
    steps = range(1, n_fsdp)
    for step in steps:
        for group in range(2):
            for way, reach in chains[group].reach.items():
                if step < reach:
                    reduce(group, way, step)
    for group in range(2):
        activate(group)
    for step in steps:
        for group in range(2):
            for way, reach in chains[group].reach.items():
                if step <= reach:
                    gather(group, way, step)
    wholes = [chain.whole.reshape(chips * capacity, 2 * half_units) for chain in chains]

    taken = swap(back(wholes[0]), "expert", 1)
    kept = back(earlier(wholes[1], taken))
    pieces = {}
    for mask in reversed(masks):
        rows = slice(mask * capacity, (mask + 1) * capacity)
        both = add_rounded(kept[rows], taken[rows])
        pieces[mask] = swap(both, "expert", 2 * mask) if mask else both

    hidden = jnp.where(
        parity == 0, jnp.concatenate([hiddens[1], hiddens[0]], 0), jnp.concatenate(hiddens, 0)
    )
    grad_gate, grad_up = weight_grads(inputs[0] + inputs[1], wholes)
    grad_tokens = lax.dot_general(
        chooser,
        jnp.concatenate([pieces[mask] for mask in masks], 0),
        (((0,), (0,)), ((), ())),
        preferred_element_type=jnp.float32,
    ).astype(jnp.bfloat16)
    return (hidden[None], grad_gate, grad_up, grad_tokens)


def solution(mesh):
    in_specs = (
        P("expert", "fsdp"),
        P("expert", None),
        P("expert", "fsdp", None),
        P("expert", "fsdp", None),
        P("expert", None, None),
        P("expert", None, None),
        P("expert", "fsdp", None),
    )
    out_specs = (
        P("expert", "fsdp", None),
        P("expert", "fsdp", None),
        P("expert", "fsdp", None),
        P("expert", "fsdp"),
    )
    return jax.shard_map(
        on_device, mesh=mesh, in_specs=in_specs, out_specs=out_specs, check_vma=False
    )
```

```python
import math

import jax
import jax.numpy as jnp
from jax import lax
from jax.experimental import pallas as pl
from jax.experimental.pallas import tpu as pltpu
from jax.sharding import PartitionSpec as P


def swap(value, axis, mask):
    pairs = [(source, source ^ mask) for source in range(lax.axis_size(axis))]
    return lax.ppermute(value, axis, pairs)


def pick(blocks, index):
    return lax.dynamic_index_in_dim(blocks, index, 0, keepdims=False)


def scale_kernel(
    sub,
    start_ref,
    gate_ref,
    up_ref,
    gate_scale_ref,
    up_scale_ref,
    out_ref,
    gate_held,
    up_held,
    gate_rows,
    up_rows,
    sems,
):
    rows = out_ref.shape[0]
    half_units = gate_held.shape[1]
    step = pl.program_id(0)

    def arrival(which, turn):
        here = pl.ds(pl.multiple_of(turn * rows, rows), rows)
        value_ref, held = ((gate_ref, gate_held), (up_ref, up_held))[which]
        return pltpu.make_async_copy(
            value_ref.at[0, here, :], held.at[here, :], sems.at[which, turn]
        )

    @pl.when(step == 0)
    def _():
        for turn in range(gate_held.shape[0] // rows):
            for which in range(2):
                arrival(which, turn).start()
        shape = (gate_scale_ref.shape[1], half_units)
        spread = (
            lax.broadcasted_iota(jnp.int32, shape, 0)
            == lax.broadcasted_iota(jnp.int32, shape, 1) // 128
        ).astype(jnp.float32)
        for scale_ref, grown in ((gate_scale_ref, gate_rows), (up_scale_ref, up_rows)):
            grown[...] = lax.dot_general(
                scale_ref[0],
                spread,
                (((0,), (0,)), ((), ())),
                precision=lax.Precision.HIGHEST,
                preferred_element_type=jnp.float32,
            )

    for which, held, grown in ((0, gate_held, gate_rows), (1, up_held, up_rows)):
        arrival(which, step).wait()
        for piece in range(rows // sub):
            block = (start_ref[0] + step * rows + piece * sub) // 128
            there = pl.ds(pl.multiple_of(step * rows + piece * sub, sub), sub)
            scaled = held[there, :].astype(jnp.float32) * grown[pl.ds(block, 1), :]
            out_ref[piece * sub : (piece + 1) * sub, which * half_units : (which + 1) * half_units] = (
                scaled.astype(jnp.bfloat16)
            )


def scaled_weights(gate_values, up_values, gate_scales, up_scales, start_row):
    feat_cols, half_units = gate_values.shape[1:]
    sub = math.gcd(feat_cols, 128)
    rows = max(r for r in range(sub, 257, sub) if feat_cols % r == 0)
    gate_scales, up_scales = (jnp.swapaxes(value, 1, 2) for value in (gate_scales, up_scales))
    any_spec = pl.BlockSpec(memory_space=pl.ANY)
    scale_spec = pl.BlockSpec(gate_scales.shape, lambda i, start: (0, 0, 0))
    held = pltpu.VMEM((feat_cols, half_units), jnp.bfloat16)
    grown = pltpu.VMEM((gate_scales.shape[2], half_units), jnp.float32)
    return pl.pallas_call(
        lambda *refs: scale_kernel(sub, *refs),
        out_shape=jax.ShapeDtypeStruct((feat_cols, 2 * half_units), jnp.bfloat16),
        grid_spec=pltpu.PrefetchScalarGridSpec(
            num_scalar_prefetch=1,
            grid=(feat_cols // rows,),
            in_specs=[any_spec, any_spec, scale_spec, scale_spec],
            out_specs=pl.BlockSpec((rows, 2 * half_units), lambda i, start: (i, 0)),
            scratch_shapes=[
                held,
                held,
                grown,
                grown,
                pltpu.SemaphoreType.DMA((2, feat_cols // rows)),
            ],
        ),
        compiler_params=pltpu.CompilerParams(vmem_limit_bytes=16 * 2**20),
        cost_estimate=pl.CostEstimate(
            flops=2 * feat_cols * half_units,
            bytes_accessed=8 * feat_cols * half_units,
            transcendentals=0,
        ),
        name="scale_weights",
    )(
        start_row[None],
        pltpu.with_memory_space_constraint(gate_values, pltpu.HBM),
        pltpu.with_memory_space_constraint(up_values, pltpu.HBM),
        gate_scales,
        up_scales,
    )


def pack_kernel(counts_ref, tokens_ref, chooser_ref, *out_refs):
    chip = lax.axis_index("expert") // 2
    row_total = tokens_ref.shape[0]
    capacity = out_refs[0].shape[0]
    counts = counts_ref[...].astype(jnp.float32)
    expert = lax.broadcasted_iota(jnp.int32, counts.shape, 1)
    row = lax.broadcasted_iota(jnp.int32, (capacity, row_total), 1).astype(jnp.float32)
    slot = lax.broadcasted_iota(jnp.int32, (capacity, row_total), 0).astype(jnp.float32)
    hits = []
    for mask in reversed(range(len(out_refs))):
        first = jnp.sum(jnp.where(expert < (chip ^ mask), counts, 0.0), 1, keepdims=True)
        live = jnp.sum(jnp.where(expert == (chip ^ mask), counts, 0.0), 1, keepdims=True)
        hits.append(((row == first + slot) & (slot < live)).astype(jnp.float32))
    chooser = jnp.concatenate(hits, 0).astype(jnp.bfloat16)
    chooser_ref[...] = chooser
    chosen = jnp.dot(chooser, tokens_ref[...], preferred_element_type=jnp.float32)
    for place, out_ref in enumerate(reversed(out_refs)):
        out_ref[...] = chosen[place * capacity : (place + 1) * capacity].astype(jnp.bfloat16)


def packed_rows(tokens, counts, capacity):
    row_total, feat_cols = tokens.shape
    experts = counts.shape[1]
    tile = feat_cols // 2 if feat_cols % 256 == 0 else feat_cols
    block = jax.ShapeDtypeStruct((capacity, feat_cols), jnp.bfloat16)
    chooser, *packed = pl.pallas_call(
        pack_kernel,
        out_shape=(jax.ShapeDtypeStruct((experts * capacity, row_total), jnp.bfloat16),)
        + (block,) * experts,
        grid=(feat_cols // tile,),
        in_specs=[
            pl.BlockSpec(counts.shape, lambda i: (0, 0)),
            pl.BlockSpec((row_total, tile), lambda i: (0, i)),
        ],
        out_specs=(pl.BlockSpec((experts * capacity, row_total), lambda i: (0, 0)),)
        + (pl.BlockSpec((capacity, tile), lambda i: (0, i)),) * experts,
        cost_estimate=pl.CostEstimate(
            flops=2 * experts * capacity * row_total * feat_cols,
            bytes_accessed=2 * (row_total + experts * capacity) * feat_cols,
            transcendentals=0,
        ),
        name="pack_rows",
    )(counts, pltpu.with_memory_space_constraint(tokens, pltpu.HBM))
    return chooser, packed


def project_kernel(*refs):
    *block_refs, weight_ref, out_ref, held = refs
    capacity = block_refs[0].shape[0]

    @pl.when(pl.program_id(0) == 0)
    def _():
        for place, block_ref in enumerate(reversed(block_refs)):
            held[place * capacity : (place + 1) * capacity, :] = block_ref[...]

    sums = jnp.dot(held[...], weight_ref[...], preferred_element_type=jnp.float32)
    for place in range(len(block_refs)):
        out_ref[place] = sums[place * capacity : (place + 1) * capacity].astype(jnp.bfloat16)


def projected(blocks, weights):
    count = len(blocks)
    capacity, feat_cols = blocks[0].shape
    units = weights.shape[1]
    tile = units
    return pl.pallas_call(
        project_kernel,
        out_shape=jax.ShapeDtypeStruct((count, capacity, units), jnp.bfloat16),
        grid=(units // tile,),
        in_specs=[pl.BlockSpec((capacity, feat_cols), lambda i: (0, 0))] * count
        + [pl.BlockSpec((feat_cols, tile), lambda i: (0, i))],
        out_specs=pl.BlockSpec((count, capacity, tile), lambda i: (0, 0, i)),
        scratch_shapes=[pltpu.VMEM((count * capacity, feat_cols), jnp.bfloat16)],
        compiler_params=pltpu.CompilerParams(vmem_limit_bytes=24 * 2**20),
        cost_estimate=pl.CostEstimate(
            flops=2 * count * capacity * feat_cols * units,
            bytes_accessed=2 * (count * capacity * (feat_cols + units) + feat_cols * units),
            transcendentals=0,
        ),
        name="project",
    )(*reversed(blocks), pltpu.with_memory_space_constraint(weights, pltpu.VMEM))


def weight_kernel(count, *refs):
    input_refs, grad_refs = refs[:count], refs[count:-3]
    gate_ref, up_ref, held = refs[-3:]
    half_units = gate_ref.shape[2]

    @pl.when(pl.program_id(0) == 0)
    def _():
        place = 0
        for grad_ref in grad_refs:
            held[place : place + grad_ref.shape[0], :] = grad_ref[...]
            place += grad_ref.shape[0]

    inputs = jnp.concatenate([input_ref[...] for input_ref in input_refs], 0)
    for out_ref, offset in ((gate_ref, 0), (up_ref, half_units)):
        out_ref[0] = lax.dot_general(
            inputs,
            held[:, offset : offset + half_units],
            (((0,), (0,)), ((), ())),
            preferred_element_type=jnp.float32,
        ).astype(jnp.bfloat16)


def weight_grads(inputs, grads):
    count = len(inputs)
    rows = sum(value.shape[0] for value in inputs)
    feat_cols = inputs[0].shape[1]
    units = grads[0].shape[1]
    tile = 256 if feat_cols % 256 == 0 else feat_cols
    out = jax.ShapeDtypeStruct((1, feat_cols, units // 2), jnp.bfloat16)
    out_spec = pl.BlockSpec((1, tile, units // 2), lambda i: (0, i, 0))
    return pl.pallas_call(
        lambda *refs: weight_kernel(count, *refs),
        out_shape=(out, out),
        grid=(feat_cols // tile,),
        in_specs=[pl.BlockSpec((value.shape[0], tile), lambda i: (0, i)) for value in inputs]
        + [pl.BlockSpec(value.shape, lambda i: (0, 0)) for value in grads],
        out_specs=(out_spec, out_spec),
        scratch_shapes=[pltpu.VMEM((rows, units), jnp.bfloat16)],
        compiler_params=pltpu.CompilerParams(vmem_limit_bytes=16 * 2**20),
        cost_estimate=pl.CostEstimate(
            flops=2 * rows * feat_cols * units,
            bytes_accessed=2 * (rows * (feat_cols + units) + feat_cols * units),
            transcendentals=0,
        ),
        name="weight_grads",
    )(*inputs, *grads)


def earlier(value, *needed):
    return lax.optimization_barrier((value,) + needed)[0]


def add_rounded(first, second):
    return (first.astype(jnp.float32) + second.astype(jnp.float32)).astype(jnp.bfloat16)


class Chain:
    def __init__(self, chip, size):
        self.chip = chip
        self.size = size
        self.index = lax.axis_index("fsdp")
        self.reach = {1: size // 2, -1: size - 1 - size // 2}
        self.partial = None
        self.whole = None
        self.came = {}

    def owner(self, steps):
        return lax.rem(self.index + self.size + steps, self.size)

    def block(self, steps):
        return pick(self.partial, self.owner(steps) ^ self.chip)

    def send(self, way, value):
        ring = [(source, (source + way) % self.size) for source in range(self.size)]
        self.came[way] = lax.ppermute(value, "fsdp", ring)

    def place(self, value, steps):
        self.whole = lax.dynamic_update_index_in_dim(
            self.whole, value, self.owner(steps) ^ self.chip, 0
        )


def on_device(tokens, counts, gate_values, up_values, gate_scales, up_scales, grad_hidden):
    row_total, feat_cols = tokens.shape
    experts = counts.shape[1]
    capacity = min(4 * row_total // experts, row_total // 2)
    n_fsdp = lax.axis_size("fsdp")
    chips = lax.axis_size("expert") // 2
    half_units = gate_values.shape[2]
    parity = lax.axis_index("expert") % 2
    chip = lax.axis_index("expert") // 2
    index = lax.axis_index("fsdp")
    masks = range(chips)

    chooser, packed = packed_rows(tokens, counts, capacity)
    weights = scaled_weights(
        gate_values, up_values, gate_scales, up_scales, index * feat_cols
    )
    cots = grad_hidden[0].reshape(2, capacity, half_units)
    chains = [Chain(chip, n_fsdp) for _ in range(2)]
    hiddens = [None, None]
    token = None

    def ordered(value):
        return value if token is None else earlier(value, token)

    def begin(group):
        nonlocal token
        chain = chains[group]
        chain.partial = projected(inputs[group], weights)
        for way, reach in chain.reach.items():
            if reach:
                token = ordered(chain.block(way * reach))
                chain.send(way, token)

    def reduce(group, way, step):
        nonlocal token
        chain = chains[group]
        token = add_rounded(
            chain.block(way * (chain.reach[way] - step)), ordered(chain.came[way])
        )
        chain.send(way, token)

    def activate(group):
        nonlocal token
        chain = chains[group]
        pre = chain.block(0).astype(jnp.float32)
        for came in chain.came.values():
            pre = pre + ordered(came).astype(jnp.float32)
        gate_pre = pre[:, :half_units]
        up_pre = pre[:, half_units:]
        cot = pick(cots, parity ^ (1 - group)).astype(jnp.float32)
        sigmoid_gate = jax.nn.sigmoid(gate_pre)
        hiddens[group] = (gate_pre * sigmoid_gate * up_pre).astype(jnp.bfloat16)
        grad_gate_pre = cot * up_pre * sigmoid_gate * (1.0 + gate_pre * (1.0 - sigmoid_gate))
        grad_up_pre = cot * gate_pre * sigmoid_gate
        token = jnp.concatenate(
            [grad_gate_pre.astype(jnp.bfloat16), grad_up_pre.astype(jnp.bfloat16)], 1
        )
        for way, reach in chain.reach.items():
            if reach:
                chain.send(way, token)
        chain.whole = jnp.zeros((chips, capacity, 2 * half_units), jnp.bfloat16)
        chain.place(token, 0)

    def gather(group, way, step):
        nonlocal token
        chain = chains[group]
        token = ordered(chain.came[way])
        chain.place(token, -way * step)
        if step < chain.reach[way]:
            chain.send(way, token)

    def back(whole):
        return lax.dot_general(
            whole, weights, (((1,), (1,)), ((), ())), preferred_element_type=jnp.float32
        ).astype(jnp.bfloat16)

    arrived = {mask: swap(packed[mask], "expert", 2 * mask + 1) for mask in reversed(masks)}
    passed = {mask: swap(arrived[mask], "expert", 1) for mask in reversed(masks[1:])}
    inputs = [
        [arrived[mask] for mask in masks],
        [passed[mask] if mask else packed[0] for mask in masks],
    ]
    for group in range(2):
        begin(group)
    steps = range(1, n_fsdp)
    for step in steps:
        for group in range(2):
            for way, reach in chains[group].reach.items():
                if step < reach:
                    reduce(group, way, step)
    for group in range(2):
        activate(group)
    for step in steps:
        for group in range(2):
            for way, reach in chains[group].reach.items():
                if step <= reach:
                    gather(group, way, step)
    wholes = [chain.whole.reshape(chips * capacity, 2 * half_units) for chain in chains]

    taken = swap(back(wholes[0]), "expert", 1)
    kept = back(earlier(wholes[1], taken))
    pieces = {}
    for mask in reversed(masks):
        rows = slice(mask * capacity, (mask + 1) * capacity)
        both = add_rounded(kept[rows], taken[rows])
        pieces[mask] = swap(both, "expert", 2 * mask) if mask else both

    hidden = jnp.where(
        parity == 0, jnp.concatenate([hiddens[1], hiddens[0]], 0), jnp.concatenate(hiddens, 0)
    )
    grad_gate, grad_up = weight_grads(inputs[0] + inputs[1], wholes)
    grad_tokens = lax.dot_general(
        chooser,
        jnp.concatenate([pieces[mask] for mask in reversed(masks)], 0),
        (((0,), (0,)), ((), ())),
        preferred_element_type=jnp.float32,
    ).astype(jnp.bfloat16)
    return (hidden[None], grad_gate, grad_up, grad_tokens)


def solution(mesh):
    in_specs = (
        P("expert", "fsdp"),
        P("expert", None),
        P("expert", "fsdp", None),
        P("expert", "fsdp", None),
        P("expert", None, None),
        P("expert", None, None),
        P("expert", "fsdp", None),
    )
    out_specs = (
        P("expert", "fsdp", None),
        P("expert", "fsdp", None),
        P("expert", "fsdp", None),
        P("expert", "fsdp"),
    )
    return jax.shard_map(
        on_device, mesh=mesh, in_specs=in_specs, out_specs=out_specs, check_vma=False
    )
```

```python
import math

import jax
import jax.numpy as jnp
from jax import lax
from jax.experimental import pallas as pl
from jax.experimental.pallas import tpu as pltpu
from jax.sharding import PartitionSpec as P


def swap(value, axis, mask):
    pairs = [(source, source ^ mask) for source in range(lax.axis_size(axis))]
    return lax.ppermute(value, axis, pairs)


def pick(blocks, index):
    return lax.dynamic_index_in_dim(blocks, index, 0, keepdims=False)


def scale_kernel(
    sub,
    start_ref,
    gate_ref,
    up_ref,
    gate_scale_ref,
    up_scale_ref,
    out_ref,
    gate_held,
    up_held,
    gate_rows,
    up_rows,
    sems,
):
    rows = out_ref.shape[0]
    half_units = gate_held.shape[1]
    step = pl.program_id(0)

    def arrival(which, turn):
        here = pl.ds(pl.multiple_of(turn * rows, rows), rows)
        value_ref, held = ((gate_ref, gate_held), (up_ref, up_held))[which]
        return pltpu.make_async_copy(
            value_ref.at[0, here, :], held.at[here, :], sems.at[which, turn]
        )

    @pl.when(step == 0)
    def _():
        for turn in range(gate_held.shape[0] // rows):
            for which in range(2):
                arrival(which, turn).start()
        shape = (gate_scale_ref.shape[1], half_units)
        spread = (
            lax.broadcasted_iota(jnp.int32, shape, 0)
            == lax.broadcasted_iota(jnp.int32, shape, 1) // 128
        ).astype(jnp.float32)
        for scale_ref, grown in ((gate_scale_ref, gate_rows), (up_scale_ref, up_rows)):
            grown[...] = lax.dot_general(
                scale_ref[0],
                spread,
                (((0,), (0,)), ((), ())),
                precision=lax.Precision.HIGHEST,
                preferred_element_type=jnp.float32,
            )

    for which, held, grown in ((0, gate_held, gate_rows), (1, up_held, up_rows)):
        arrival(which, step).wait()
        for piece in range(rows // sub):
            block = (start_ref[0] + step * rows + piece * sub) // 128
            there = pl.ds(pl.multiple_of(step * rows + piece * sub, sub), sub)
            scaled = held[there, :].astype(jnp.float32) * grown[pl.ds(block, 1), :]
            out_ref[piece * sub : (piece + 1) * sub, which * half_units : (which + 1) * half_units] = (
                scaled.astype(jnp.bfloat16)
            )


def scaled_weights(gate_values, up_values, gate_scales, up_scales, start_row):
    feat_cols, half_units = gate_values.shape[1:]
    sub = math.gcd(feat_cols, 128)
    rows = max(r for r in range(sub, 257, sub) if feat_cols % r == 0)
    gate_scales, up_scales = (jnp.swapaxes(value, 1, 2) for value in (gate_scales, up_scales))
    any_spec = pl.BlockSpec(memory_space=pl.ANY)
    scale_spec = pl.BlockSpec(gate_scales.shape, lambda i, start: (0, 0, 0))
    held = pltpu.VMEM((feat_cols, half_units), jnp.bfloat16)
    grown = pltpu.VMEM((gate_scales.shape[2], half_units), jnp.float32)
    return pl.pallas_call(
        lambda *refs: scale_kernel(sub, *refs),
        out_shape=jax.ShapeDtypeStruct((feat_cols, 2 * half_units), jnp.bfloat16),
        grid_spec=pltpu.PrefetchScalarGridSpec(
            num_scalar_prefetch=1,
            grid=(feat_cols // rows,),
            in_specs=[any_spec, any_spec, scale_spec, scale_spec],
            out_specs=pl.BlockSpec((rows, 2 * half_units), lambda i, start: (i, 0)),
            scratch_shapes=[
                held,
                held,
                grown,
                grown,
                pltpu.SemaphoreType.DMA((2, feat_cols // rows)),
            ],
        ),
        compiler_params=pltpu.CompilerParams(vmem_limit_bytes=16 * 2**20),
        cost_estimate=pl.CostEstimate(
            flops=2 * feat_cols * half_units,
            bytes_accessed=8 * feat_cols * half_units,
            transcendentals=0,
        ),
        name="scale_weights",
    )(
        start_row[None],
        pltpu.with_memory_space_constraint(gate_values, pltpu.HBM),
        pltpu.with_memory_space_constraint(up_values, pltpu.HBM),
        gate_scales,
        up_scales,
    )


def pack_kernel(counts_ref, tokens_ref, chooser_ref, *out_refs):
    chip = lax.axis_index("expert") // 2
    row_total = tokens_ref.shape[0]
    capacity = out_refs[0].shape[0]
    counts = counts_ref[...].astype(jnp.float32)
    expert = lax.broadcasted_iota(jnp.int32, counts.shape, 1)
    row = lax.broadcasted_iota(jnp.int32, (capacity, row_total), 1).astype(jnp.float32)
    slot = lax.broadcasted_iota(jnp.int32, (capacity, row_total), 0).astype(jnp.float32)
    hits = []
    for mask in reversed(range(len(out_refs))):
        first = jnp.sum(jnp.where(expert < (chip ^ mask), counts, 0.0), 1, keepdims=True)
        live = jnp.sum(jnp.where(expert == (chip ^ mask), counts, 0.0), 1, keepdims=True)
        hits.append(((row == first + slot) & (slot < live)).astype(jnp.float32))
    chooser = jnp.concatenate(hits, 0).astype(jnp.bfloat16)
    chooser_ref[...] = chooser
    chosen = jnp.dot(chooser, tokens_ref[...], preferred_element_type=jnp.float32)
    for place, out_ref in enumerate(reversed(out_refs)):
        out_ref[...] = chosen[place * capacity : (place + 1) * capacity].astype(jnp.bfloat16)


def packed_rows(tokens, counts, capacity):
    row_total, feat_cols = tokens.shape
    experts = counts.shape[1]
    tile = feat_cols // 2 if feat_cols % 256 == 0 else feat_cols
    block = pltpu.VMEM((capacity, feat_cols), jnp.bfloat16)
    chooser, *packed = pl.pallas_call(
        pack_kernel,
        out_shape=(jax.ShapeDtypeStruct((experts * capacity, row_total), jnp.bfloat16),)
        + (block,) * experts,
        grid=(feat_cols // tile,),
        in_specs=[
            pl.BlockSpec(counts.shape, lambda i: (0, 0)),
            pl.BlockSpec((row_total, tile), lambda i: (0, i)),
        ],
        out_specs=(pl.BlockSpec((experts * capacity, row_total), lambda i: (0, 0)),)
        + (pl.BlockSpec((capacity, tile), lambda i: (0, i)),) * experts,
        cost_estimate=pl.CostEstimate(
            flops=2 * experts * capacity * row_total * feat_cols,
            bytes_accessed=2 * (row_total + experts * capacity) * feat_cols,
            transcendentals=0,
        ),
        name="pack_rows",
    )(counts, pltpu.with_memory_space_constraint(tokens, pltpu.HBM))
    return chooser, packed


def project_kernel(*refs):
    *block_refs, weight_ref, out_ref, held = refs
    capacity = block_refs[0].shape[0]

    @pl.when(pl.program_id(0) == 0)
    def _():
        for place, block_ref in enumerate(reversed(block_refs)):
            held[place * capacity : (place + 1) * capacity, :] = block_ref[...]

    sums = jnp.dot(held[...], weight_ref[...], preferred_element_type=jnp.float32)
    for place in range(len(block_refs)):
        out_ref[place] = sums[place * capacity : (place + 1) * capacity].astype(jnp.bfloat16)


def projected(blocks, weights):
    count = len(blocks)
    capacity, feat_cols = blocks[0].shape
    units = weights.shape[1]
    tile = units
    return pl.pallas_call(
        project_kernel,
        out_shape=jax.ShapeDtypeStruct((count, capacity, units), jnp.bfloat16),
        grid=(units // tile,),
        in_specs=[pl.BlockSpec((capacity, feat_cols), lambda i: (0, 0))] * count
        + [pl.BlockSpec((feat_cols, tile), lambda i: (0, i))],
        out_specs=pl.BlockSpec((count, capacity, tile), lambda i: (0, 0, i)),
        scratch_shapes=[pltpu.VMEM((count * capacity, feat_cols), jnp.bfloat16)],
        compiler_params=pltpu.CompilerParams(vmem_limit_bytes=24 * 2**20),
        cost_estimate=pl.CostEstimate(
            flops=2 * count * capacity * feat_cols * units,
            bytes_accessed=2 * (count * capacity * (feat_cols + units) + feat_cols * units),
            transcendentals=0,
        ),
        name="project",
    )(*reversed(blocks), pltpu.with_memory_space_constraint(weights, pltpu.VMEM))


def weight_kernel(count, *refs):
    input_refs, grad_refs = refs[:count], refs[count:-3]
    gate_ref, up_ref, held = refs[-3:]
    half_units = gate_ref.shape[2]

    @pl.when(pl.program_id(0) == 0)
    def _():
        place = 0
        for grad_ref in grad_refs:
            held[place : place + grad_ref.shape[0], :] = grad_ref[...]
            place += grad_ref.shape[0]

    inputs = jnp.concatenate([input_ref[...] for input_ref in input_refs], 0)
    for out_ref, offset in ((gate_ref, 0), (up_ref, half_units)):
        out_ref[0] = lax.dot_general(
            inputs,
            held[:, offset : offset + half_units],
            (((0,), (0,)), ((), ())),
            preferred_element_type=jnp.float32,
        ).astype(jnp.bfloat16)


def weight_grads(inputs, grads):
    count = len(inputs)
    rows = sum(value.shape[0] for value in inputs)
    feat_cols = inputs[0].shape[1]
    units = grads[0].shape[1]
    tile = 256 if feat_cols % 256 == 0 else feat_cols
    out = jax.ShapeDtypeStruct((1, feat_cols, units // 2), jnp.bfloat16)
    out_spec = pl.BlockSpec((1, tile, units // 2), lambda i: (0, i, 0))
    return pl.pallas_call(
        lambda *refs: weight_kernel(count, *refs),
        out_shape=(out, out),
        grid=(feat_cols // tile,),
        in_specs=[pl.BlockSpec((value.shape[0], tile), lambda i: (0, i)) for value in inputs]
        + [pl.BlockSpec(value.shape, lambda i: (0, 0)) for value in grads],
        out_specs=(out_spec, out_spec),
        scratch_shapes=[pltpu.VMEM((rows, units), jnp.bfloat16)],
        compiler_params=pltpu.CompilerParams(vmem_limit_bytes=16 * 2**20),
        cost_estimate=pl.CostEstimate(
            flops=2 * rows * feat_cols * units,
            bytes_accessed=2 * (rows * (feat_cols + units) + feat_cols * units),
            transcendentals=0,
        ),
        name="weight_grads",
    )(*inputs, *grads)


def earlier(value, *needed):
    return lax.optimization_barrier((value,) + needed)[0]


def add_rounded(first, second):
    return (first.astype(jnp.float32) + second.astype(jnp.float32)).astype(jnp.bfloat16)


class Chain:
    def __init__(self, chip, size):
        self.chip = chip
        self.size = size
        self.index = lax.axis_index("fsdp")
        self.reach = {1: size // 2, -1: size - 1 - size // 2}
        self.partial = None
        self.whole = None
        self.came = {}

    def owner(self, steps):
        return lax.rem(self.index + self.size + steps, self.size)

    def block(self, steps):
        return pick(self.partial, self.owner(steps) ^ self.chip)

    def send(self, way, value):
        ring = [(source, (source + way) % self.size) for source in range(self.size)]
        self.came[way] = lax.ppermute(value, "fsdp", ring)

    def place(self, value, steps):
        self.whole = lax.dynamic_update_index_in_dim(
            self.whole, value, self.owner(steps) ^ self.chip, 0
        )


def on_device(tokens, counts, gate_values, up_values, gate_scales, up_scales, grad_hidden):
    row_total, feat_cols = tokens.shape
    experts = counts.shape[1]
    capacity = min(4 * row_total // experts, row_total // 2)
    n_fsdp = lax.axis_size("fsdp")
    chips = lax.axis_size("expert") // 2
    half_units = gate_values.shape[2]
    parity = lax.axis_index("expert") % 2
    chip = lax.axis_index("expert") // 2
    index = lax.axis_index("fsdp")
    masks = range(chips)

    chooser, packed = packed_rows(tokens, counts, capacity)
    weights = scaled_weights(
        gate_values, up_values, gate_scales, up_scales, index * feat_cols
    )
    cots = grad_hidden[0].reshape(2, capacity, half_units)
    chains = [Chain(chip, n_fsdp) for _ in range(2)]
    hiddens = [None, None]
    token = None

    def ordered(value):
        return value if token is None else earlier(value, token)

    def begin(group):
        nonlocal token
        chain = chains[group]
        chain.partial = projected(inputs[group], weights)
        for way, reach in chain.reach.items():
            if reach:
                token = ordered(chain.block(way * reach))
                chain.send(way, token)

    def reduce(group, way, step):
        nonlocal token
        chain = chains[group]
        token = add_rounded(
            chain.block(way * (chain.reach[way] - step)), ordered(chain.came[way])
        )
        chain.send(way, token)

    def activate(group):
        nonlocal token
        chain = chains[group]
        pre = chain.block(0).astype(jnp.float32)
        for came in chain.came.values():
            pre = pre + ordered(came).astype(jnp.float32)
        gate_pre = pre[:, :half_units]
        up_pre = pre[:, half_units:]
        cot = pick(cots, parity ^ (1 - group)).astype(jnp.float32)
        sigmoid_gate = jax.nn.sigmoid(gate_pre)
        hiddens[group] = (gate_pre * sigmoid_gate * up_pre).astype(jnp.bfloat16)
        grad_gate_pre = cot * up_pre * sigmoid_gate * (1.0 + gate_pre * (1.0 - sigmoid_gate))
        grad_up_pre = cot * gate_pre * sigmoid_gate
        token = jnp.concatenate(
            [grad_gate_pre.astype(jnp.bfloat16), grad_up_pre.astype(jnp.bfloat16)], 1
        )
        for way, reach in chain.reach.items():
            if reach:
                chain.send(way, token)
        chain.whole = jnp.zeros((chips, capacity, 2 * half_units), jnp.bfloat16)
        chain.place(token, 0)

    def gather(group, way, step):
        nonlocal token
        chain = chains[group]
        token = ordered(chain.came[way])
        chain.place(token, -way * step)
        if step < chain.reach[way]:
            chain.send(way, token)

    def back(whole):
        return lax.dot_general(
            whole, weights, (((1,), (1,)), ((), ())), preferred_element_type=jnp.float32
        ).astype(jnp.bfloat16)

    arrived = {mask: swap(packed[mask], "expert", 2 * mask + 1) for mask in reversed(masks)}
    passed = {mask: swap(arrived[mask], "expert", 1) for mask in reversed(masks[1:])}
    inputs = [
        [arrived[mask] for mask in masks],
        [passed[mask] if mask else packed[0] for mask in masks],
    ]
    for group in range(2):
        begin(group)
    steps = range(1, n_fsdp)
    for step in steps:
        for group in range(2):
            for way, reach in chains[group].reach.items():
                if step < reach:
                    reduce(group, way, step)
    for group in range(2):
        activate(group)
    for step in steps:
        for group in range(2):
            for way, reach in chains[group].reach.items():
                if step <= reach:
                    gather(group, way, step)
    wholes = [chain.whole.reshape(chips * capacity, 2 * half_units) for chain in chains]

    taken = swap(back(wholes[0]), "expert", 1)
    kept = back(earlier(wholes[1], taken))
    pieces = {}
    for mask in reversed(masks):
        rows = slice(mask * capacity, (mask + 1) * capacity)
        both = add_rounded(kept[rows], taken[rows])
        pieces[mask] = swap(both, "expert", 2 * mask) if mask else both

    hidden = jnp.where(
        parity == 0, jnp.concatenate([hiddens[1], hiddens[0]], 0), jnp.concatenate(hiddens, 0)
    )
    grad_gate, grad_up = weight_grads(inputs[0] + inputs[1], wholes)
    grad_tokens = lax.dot_general(
        chooser,
        jnp.concatenate([pieces[mask] for mask in reversed(masks)], 0),
        (((0,), (0,)), ((), ())),
        preferred_element_type=jnp.float32,
    ).astype(jnp.bfloat16)
    return (hidden[None], grad_gate, grad_up, grad_tokens)


def solution(mesh):
    in_specs = (
        P("expert", "fsdp"),
        P("expert", None),
        P("expert", "fsdp", None),
        P("expert", "fsdp", None),
        P("expert", None, None),
        P("expert", None, None),
        P("expert", "fsdp", None),
    )
    out_specs = (
        P("expert", "fsdp", None),
        P("expert", "fsdp", None),
        P("expert", "fsdp", None),
        P("expert", "fsdp"),
    )
    return jax.shard_map(
        on_device, mesh=mesh, in_specs=in_specs, out_specs=out_specs, check_vma=False
    )
```

```python
import math

import jax
import jax.numpy as jnp
from jax import lax
from jax.experimental import pallas as pl
from jax.experimental.pallas import tpu as pltpu
from jax.sharding import PartitionSpec as P


def swap(value, axis, mask):
    pairs = [(source, source ^ mask) for source in range(lax.axis_size(axis))]
    return lax.ppermute(value, axis, pairs)


def pick(blocks, index):
    return lax.dynamic_index_in_dim(blocks, index, 0, keepdims=False)


def scale_kernel(
    sub,
    start_ref,
    gate_ref,
    up_ref,
    gate_scale_ref,
    up_scale_ref,
    out_ref,
    gate_held,
    up_held,
    gate_rows,
    up_rows,
    sems,
):
    rows = out_ref.shape[0]
    half_units = gate_held.shape[1]
    step = pl.program_id(0)

    def arrival(which, turn):
        here = pl.ds(pl.multiple_of(turn * rows, rows), rows)
        value_ref, held = ((gate_ref, gate_held), (up_ref, up_held))[which]
        return pltpu.make_async_copy(
            value_ref.at[0, here, :], held.at[here, :], sems.at[which, turn]
        )

    @pl.when(step == 0)
    def _():
        for turn in range(gate_held.shape[0] // rows):
            for which in range(2):
                arrival(which, turn).start()
        shape = (gate_scale_ref.shape[1], half_units)
        spread = (
            lax.broadcasted_iota(jnp.int32, shape, 0)
            == lax.broadcasted_iota(jnp.int32, shape, 1) // 128
        ).astype(jnp.float32)
        for scale_ref, grown in ((gate_scale_ref, gate_rows), (up_scale_ref, up_rows)):
            grown[...] = lax.dot_general(
                scale_ref[0],
                spread,
                (((0,), (0,)), ((), ())),
                precision=lax.Precision.HIGHEST,
                preferred_element_type=jnp.float32,
            )

    for which, held, grown in ((0, gate_held, gate_rows), (1, up_held, up_rows)):
        arrival(which, step).wait()
        for piece in range(rows // sub):
            block = (start_ref[0] + step * rows + piece * sub) // 128
            there = pl.ds(pl.multiple_of(step * rows + piece * sub, sub), sub)
            scaled = held[there, :].astype(jnp.float32) * grown[pl.ds(block, 1), :]
            out_ref[piece * sub : (piece + 1) * sub, which * half_units : (which + 1) * half_units] = (
                scaled.astype(jnp.bfloat16)
            )


def scaled_weights(gate_values, up_values, gate_scales, up_scales, start_row):
    feat_cols, half_units = gate_values.shape[1:]
    sub = math.gcd(feat_cols, 128)
    rows = max(r for r in range(sub, 257, sub) if feat_cols % r == 0)
    gate_scales, up_scales = (jnp.swapaxes(value, 1, 2) for value in (gate_scales, up_scales))
    any_spec = pl.BlockSpec(memory_space=pl.ANY)
    scale_spec = pl.BlockSpec(gate_scales.shape, lambda i, start: (0, 0, 0))
    held = pltpu.VMEM((feat_cols, half_units), jnp.bfloat16)
    grown = pltpu.VMEM((gate_scales.shape[2], half_units), jnp.float32)
    return pl.pallas_call(
        lambda *refs: scale_kernel(sub, *refs),
        out_shape=jax.ShapeDtypeStruct((feat_cols, 2 * half_units), jnp.bfloat16),
        grid_spec=pltpu.PrefetchScalarGridSpec(
            num_scalar_prefetch=1,
            grid=(feat_cols // rows,),
            in_specs=[any_spec, any_spec, scale_spec, scale_spec],
            out_specs=pl.BlockSpec((rows, 2 * half_units), lambda i, start: (i, 0)),
            scratch_shapes=[
                held,
                held,
                grown,
                grown,
                pltpu.SemaphoreType.DMA((2, feat_cols // rows)),
            ],
        ),
        compiler_params=pltpu.CompilerParams(vmem_limit_bytes=16 * 2**20),
        cost_estimate=pl.CostEstimate(
            flops=2 * feat_cols * half_units,
            bytes_accessed=8 * feat_cols * half_units,
            transcendentals=0,
        ),
        name="scale_weights",
    )(
        start_row[None],
        pltpu.with_memory_space_constraint(gate_values, pltpu.HBM),
        pltpu.with_memory_space_constraint(up_values, pltpu.HBM),
        gate_scales,
        up_scales,
    )


def pack_kernel(counts_ref, tokens_ref, chooser_ref, *out_refs):
    chip = lax.axis_index("expert") // 2
    row_total = tokens_ref.shape[0]
    capacity = out_refs[0].shape[0]
    counts = counts_ref[...].astype(jnp.float32)
    expert = lax.broadcasted_iota(jnp.int32, counts.shape, 1)
    row = lax.broadcasted_iota(jnp.int32, (capacity, row_total), 1).astype(jnp.float32)
    slot = lax.broadcasted_iota(jnp.int32, (capacity, row_total), 0).astype(jnp.float32)
    hits = []
    for mask in reversed(range(len(out_refs))):
        first = jnp.sum(jnp.where(expert < (chip ^ mask), counts, 0.0), 1, keepdims=True)
        live = jnp.sum(jnp.where(expert == (chip ^ mask), counts, 0.0), 1, keepdims=True)
        hits.append(((row == first + slot) & (slot < live)).astype(jnp.float32))
    chooser = jnp.concatenate(hits, 0).astype(jnp.bfloat16)
    chooser_ref[...] = chooser
    chosen = jnp.dot(chooser, tokens_ref[...], preferred_element_type=jnp.float32)
    for place, out_ref in enumerate(reversed(out_refs)):
        out_ref[...] = chosen[place * capacity : (place + 1) * capacity].astype(jnp.bfloat16)


def packed_rows(tokens, counts, capacity):
    row_total, feat_cols = tokens.shape
    experts = counts.shape[1]
    tile = feat_cols // 2 if feat_cols % 256 == 0 else feat_cols
    block = pltpu.VMEM((capacity, feat_cols), jnp.bfloat16)
    chooser, *packed = pl.pallas_call(
        pack_kernel,
        out_shape=(jax.ShapeDtypeStruct((experts * capacity, row_total), jnp.bfloat16),)
        + (block,) * experts,
        grid=(feat_cols // tile,),
        in_specs=[
            pl.BlockSpec(counts.shape, lambda i: (0, 0)),
            pl.BlockSpec((row_total, tile), lambda i: (0, i)),
        ],
        out_specs=(pl.BlockSpec((experts * capacity, row_total), lambda i: (0, 0)),)
        + (pl.BlockSpec((capacity, tile), lambda i: (0, i)),) * experts,
        cost_estimate=pl.CostEstimate(
            flops=2 * experts * capacity * row_total * feat_cols,
            bytes_accessed=2 * (row_total + experts * capacity) * feat_cols,
            transcendentals=0,
        ),
        name="pack_rows",
    )(
        pltpu.with_memory_space_constraint(counts, pltpu.HBM),
        pltpu.with_memory_space_constraint(tokens, pltpu.HBM),
    )
    return chooser, packed


def project_kernel(*refs):
    *block_refs, weight_ref, out_ref, held = refs
    capacity = block_refs[0].shape[0]

    @pl.when(pl.program_id(0) == 0)
    def _():
        for place, block_ref in enumerate(reversed(block_refs)):
            held[place * capacity : (place + 1) * capacity, :] = block_ref[...]

    sums = jnp.dot(held[...], weight_ref[...], preferred_element_type=jnp.float32)
    for place in range(len(block_refs)):
        out_ref[place] = sums[place * capacity : (place + 1) * capacity].astype(jnp.bfloat16)


def projected(blocks, weights):
    count = len(blocks)
    capacity, feat_cols = blocks[0].shape
    units = weights.shape[1]
    tile = units
    return pl.pallas_call(
        project_kernel,
        out_shape=jax.ShapeDtypeStruct((count, capacity, units), jnp.bfloat16),
        grid=(units // tile,),
        in_specs=[pl.BlockSpec((capacity, feat_cols), lambda i: (0, 0))] * count
        + [pl.BlockSpec((feat_cols, tile), lambda i: (0, i))],
        out_specs=pl.BlockSpec((count, capacity, tile), lambda i: (0, 0, i)),
        scratch_shapes=[pltpu.VMEM((count * capacity, feat_cols), jnp.bfloat16)],
        compiler_params=pltpu.CompilerParams(vmem_limit_bytes=24 * 2**20),
        cost_estimate=pl.CostEstimate(
            flops=2 * count * capacity * feat_cols * units,
            bytes_accessed=2 * (count * capacity * (feat_cols + units) + feat_cols * units),
            transcendentals=0,
        ),
        name="project",
    )(*reversed(blocks), pltpu.with_memory_space_constraint(weights, pltpu.VMEM))


def weight_kernel(count, *refs):
    input_refs, grad_refs = refs[:count], refs[count:-3]
    gate_ref, up_ref, held = refs[-3:]
    half_units = gate_ref.shape[2]

    @pl.when(pl.program_id(0) == 0)
    def _():
        place = 0
        for grad_ref in grad_refs:
            held[place : place + grad_ref.shape[0], :] = grad_ref[...]
            place += grad_ref.shape[0]

    inputs = jnp.concatenate([input_ref[...] for input_ref in input_refs], 0)
    for out_ref, offset in ((gate_ref, 0), (up_ref, half_units)):
        out_ref[0] = lax.dot_general(
            inputs,
            held[:, offset : offset + half_units],
            (((0,), (0,)), ((), ())),
            preferred_element_type=jnp.float32,
        ).astype(jnp.bfloat16)


def weight_grads(inputs, grads):
    count = len(inputs)
    rows = sum(value.shape[0] for value in inputs)
    feat_cols = inputs[0].shape[1]
    units = grads[0].shape[1]
    tile = 256 if feat_cols % 256 == 0 else feat_cols
    out = jax.ShapeDtypeStruct((1, feat_cols, units // 2), jnp.bfloat16)
    out_spec = pl.BlockSpec((1, tile, units // 2), lambda i: (0, i, 0))
    return pl.pallas_call(
        lambda *refs: weight_kernel(count, *refs),
        out_shape=(out, out),
        grid=(feat_cols // tile,),
        in_specs=[pl.BlockSpec((value.shape[0], tile), lambda i: (0, i)) for value in inputs]
        + [pl.BlockSpec(value.shape, lambda i: (0, 0)) for value in grads],
        out_specs=(out_spec, out_spec),
        scratch_shapes=[pltpu.VMEM((rows, units), jnp.bfloat16)],
        compiler_params=pltpu.CompilerParams(vmem_limit_bytes=16 * 2**20),
        cost_estimate=pl.CostEstimate(
            flops=2 * rows * feat_cols * units,
            bytes_accessed=2 * (rows * (feat_cols + units) + feat_cols * units),
            transcendentals=0,
        ),
        name="weight_grads",
    )(*inputs, *grads)


def earlier(value, *needed):
    return lax.optimization_barrier((value,) + needed)[0]


def add_rounded(first, second):
    return (first.astype(jnp.float32) + second.astype(jnp.float32)).astype(jnp.bfloat16)


class Chain:
    def __init__(self, chip, size):
        self.chip = chip
        self.size = size
        self.index = lax.axis_index("fsdp")
        self.reach = {1: size // 2, -1: size - 1 - size // 2}
        self.partial = None
        self.whole = None
        self.came = {}

    def owner(self, steps):
        return lax.rem(self.index + self.size + steps, self.size)

    def block(self, steps):
        return pick(self.partial, self.owner(steps) ^ self.chip)

    def send(self, way, value):
        ring = [(source, (source + way) % self.size) for source in range(self.size)]
        self.came[way] = lax.ppermute(value, "fsdp", ring)

    def place(self, value, steps):
        self.whole = lax.dynamic_update_index_in_dim(
            self.whole, value, self.owner(steps) ^ self.chip, 0
        )


def on_device(tokens, counts, gate_values, up_values, gate_scales, up_scales, grad_hidden):
    row_total, feat_cols = tokens.shape
    experts = counts.shape[1]
    capacity = min(4 * row_total // experts, row_total // 2)
    n_fsdp = lax.axis_size("fsdp")
    chips = lax.axis_size("expert") // 2
    half_units = gate_values.shape[2]
    parity = lax.axis_index("expert") % 2
    chip = lax.axis_index("expert") // 2
    index = lax.axis_index("fsdp")
    masks = range(chips)

    chooser, packed = packed_rows(tokens, counts, capacity)
    weights = scaled_weights(
        gate_values, up_values, gate_scales, up_scales, index * feat_cols
    )
    cots = grad_hidden[0].reshape(2, capacity, half_units)
    chains = [Chain(chip, n_fsdp) for _ in range(2)]
    hiddens = [None, None]
    token = None

    def ordered(value):
        return value if token is None else earlier(value, token)

    def begin(group):
        nonlocal token
        chain = chains[group]
        chain.partial = projected(inputs[group], weights)
        for way, reach in chain.reach.items():
            if reach:
                token = ordered(chain.block(way * reach))
                chain.send(way, token)

    def reduce(group, way, step):
        nonlocal token
        chain = chains[group]
        token = add_rounded(
            chain.block(way * (chain.reach[way] - step)), ordered(chain.came[way])
        )
        chain.send(way, token)

    def activate(group):
        nonlocal token
        chain = chains[group]
        pre = chain.block(0).astype(jnp.float32)
        for came in chain.came.values():
            pre = pre + ordered(came).astype(jnp.float32)
        gate_pre = pre[:, :half_units]
        up_pre = pre[:, half_units:]
        cot = pick(cots, parity ^ (1 - group)).astype(jnp.float32)
        sigmoid_gate = jax.nn.sigmoid(gate_pre)
        hiddens[group] = (gate_pre * sigmoid_gate * up_pre).astype(jnp.bfloat16)
        grad_gate_pre = cot * up_pre * sigmoid_gate * (1.0 + gate_pre * (1.0 - sigmoid_gate))
        grad_up_pre = cot * gate_pre * sigmoid_gate
        token = jnp.concatenate(
            [grad_gate_pre.astype(jnp.bfloat16), grad_up_pre.astype(jnp.bfloat16)], 1
        )
        for way, reach in chain.reach.items():
            if reach:
                chain.send(way, token)
        chain.whole = jnp.zeros((chips, capacity, 2 * half_units), jnp.bfloat16)
        chain.place(token, 0)

    def gather(group, way, step):
        nonlocal token
        chain = chains[group]
        token = ordered(chain.came[way])
        chain.place(token, -way * step)
        if step < chain.reach[way]:
            chain.send(way, token)

    def back(whole):
        return lax.dot_general(
            whole, weights, (((1,), (1,)), ((), ())), preferred_element_type=jnp.float32
        ).astype(jnp.bfloat16)

    arrived = {mask: swap(packed[mask], "expert", 2 * mask + 1) for mask in reversed(masks)}
    passed = {mask: swap(arrived[mask], "expert", 1) for mask in reversed(masks[1:])}
    inputs = [
        [arrived[mask] for mask in masks],
        [passed[mask] if mask else packed[0] for mask in masks],
    ]
    for group in range(2):
        begin(group)
    steps = range(1, n_fsdp)
    for step in steps:
        for group in range(2):
            for way, reach in chains[group].reach.items():
                if step < reach:
                    reduce(group, way, step)
    for group in range(2):
        activate(group)
    for step in steps:
        for group in range(2):
            for way, reach in chains[group].reach.items():
                if step <= reach:
                    gather(group, way, step)
    wholes = [chain.whole.reshape(chips * capacity, 2 * half_units) for chain in chains]

    taken = swap(back(wholes[0]), "expert", 1)
    kept = back(earlier(wholes[1], taken))
    pieces = {}
    for mask in reversed(masks):
        rows = slice(mask * capacity, (mask + 1) * capacity)
        both = add_rounded(kept[rows], taken[rows])
        pieces[mask] = swap(both, "expert", 2 * mask) if mask else both

    hidden = jnp.where(
        parity == 0, jnp.concatenate([hiddens[1], hiddens[0]], 0), jnp.concatenate(hiddens, 0)
    )
    grad_gate, grad_up = weight_grads(inputs[0] + inputs[1], wholes)
    grad_tokens = lax.dot_general(
        chooser,
        jnp.concatenate([pieces[mask] for mask in reversed(masks)], 0),
        (((0,), (0,)), ((), ())),
        preferred_element_type=jnp.float32,
    ).astype(jnp.bfloat16)
    return (hidden[None], grad_gate, grad_up, grad_tokens)


def solution(mesh):
    in_specs = (
        P("expert", "fsdp"),
        P("expert", None),
        P("expert", "fsdp", None),
        P("expert", "fsdp", None),
        P("expert", None, None),
        P("expert", None, None),
        P("expert", "fsdp", None),
    )
    out_specs = (
        P("expert", "fsdp", None),
        P("expert", "fsdp", None),
        P("expert", "fsdp", None),
        P("expert", "fsdp"),
    )
    return jax.shard_map(
        on_device, mesh=mesh, in_specs=in_specs, out_specs=out_specs, check_vma=False
    )
```

```python
import math

import jax
import jax.numpy as jnp
from jax import lax
from jax.experimental import pallas as pl
from jax.experimental.pallas import tpu as pltpu
from jax.sharding import PartitionSpec as P


def swap(value, axis, mask):
    pairs = [(source, source ^ mask) for source in range(lax.axis_size(axis))]
    return lax.ppermute(value, axis, pairs)


def pick(blocks, index):
    return lax.dynamic_index_in_dim(blocks, index, 0, keepdims=False)


def scale_kernel(
    sub,
    start_ref,
    gate_ref,
    up_ref,
    gate_scale_ref,
    up_scale_ref,
    out_ref,
    gate_held,
    up_held,
    gate_rows,
    up_rows,
    sems,
):
    rows = out_ref.shape[0]
    half_units = gate_held.shape[1]
    step = pl.program_id(0)

    def arrival(which, turn):
        here = pl.ds(pl.multiple_of(turn * rows, rows), rows)
        value_ref, held = ((gate_ref, gate_held), (up_ref, up_held))[which]
        return pltpu.make_async_copy(
            value_ref.at[0, here, :], held.at[here, :], sems.at[which, turn]
        )

    @pl.when(step == 0)
    def _():
        for turn in range(gate_held.shape[0] // rows):
            for which in range(2):
                arrival(which, turn).start()
        shape = (gate_scale_ref.shape[1], half_units)
        spread = (
            lax.broadcasted_iota(jnp.int32, shape, 0)
            == lax.broadcasted_iota(jnp.int32, shape, 1) // 128
        ).astype(jnp.float32)
        for scale_ref, grown in ((gate_scale_ref, gate_rows), (up_scale_ref, up_rows)):
            grown[...] = lax.dot_general(
                scale_ref[0],
                spread,
                (((0,), (0,)), ((), ())),
                precision=lax.Precision.HIGHEST,
                preferred_element_type=jnp.float32,
            )

    for which, held, grown in ((0, gate_held, gate_rows), (1, up_held, up_rows)):
        arrival(which, step).wait()
        for piece in range(rows // sub):
            block = (start_ref[0] + step * rows + piece * sub) // 128
            there = pl.ds(pl.multiple_of(step * rows + piece * sub, sub), sub)
            scaled = held[there, :].astype(jnp.float32) * grown[pl.ds(block, 1), :]
            out_ref[piece * sub : (piece + 1) * sub, which * half_units : (which + 1) * half_units] = (
                scaled.astype(jnp.bfloat16)
            )


def scaled_weights(gate_values, up_values, gate_scales, up_scales, start_row):
    feat_cols, half_units = gate_values.shape[1:]
    sub = math.gcd(feat_cols, 128)
    rows = max(r for r in range(sub, 257, sub) if feat_cols % r == 0)
    gate_scales, up_scales = (jnp.swapaxes(value, 1, 2) for value in (gate_scales, up_scales))
    any_spec = pl.BlockSpec(memory_space=pl.ANY)
    scale_spec = pl.BlockSpec(gate_scales.shape, lambda i, start: (0, 0, 0))
    held = pltpu.VMEM((feat_cols, half_units), jnp.bfloat16)
    grown = pltpu.VMEM((gate_scales.shape[2], half_units), jnp.float32)
    return pl.pallas_call(
        lambda *refs: scale_kernel(sub, *refs),
        out_shape=jax.ShapeDtypeStruct((feat_cols, 2 * half_units), jnp.bfloat16),
        grid_spec=pltpu.PrefetchScalarGridSpec(
            num_scalar_prefetch=1,
            grid=(feat_cols // rows,),
            in_specs=[any_spec, any_spec, scale_spec, scale_spec],
            out_specs=pl.BlockSpec((rows, 2 * half_units), lambda i, start: (i, 0)),
            scratch_shapes=[
                held,
                held,
                grown,
                grown,
                pltpu.SemaphoreType.DMA((2, feat_cols // rows)),
            ],
        ),
        compiler_params=pltpu.CompilerParams(vmem_limit_bytes=16 * 2**20),
        cost_estimate=pl.CostEstimate(
            flops=2 * feat_cols * half_units,
            bytes_accessed=8 * feat_cols * half_units,
            transcendentals=0,
        ),
        name="scale_weights",
    )(
        start_row[None],
        pltpu.with_memory_space_constraint(gate_values, pltpu.HBM),
        pltpu.with_memory_space_constraint(up_values, pltpu.HBM),
        gate_scales,
        up_scales,
    )


def pack_kernel(counts_ref, tokens_ref, chooser_ref, *out_refs):
    chip = lax.axis_index("expert") // 2
    row_total = tokens_ref.shape[0]
    capacity = out_refs[0].shape[0]
    counts = counts_ref[...].astype(jnp.float32)
    expert = lax.broadcasted_iota(jnp.int32, counts.shape, 1)
    row = lax.broadcasted_iota(jnp.int32, (capacity, row_total), 1).astype(jnp.float32)
    slot = lax.broadcasted_iota(jnp.int32, (capacity, row_total), 0).astype(jnp.float32)
    hits = []
    for mask in reversed(range(len(out_refs))):
        first = jnp.sum(jnp.where(expert < (chip ^ mask), counts, 0.0), 1, keepdims=True)
        live = jnp.sum(jnp.where(expert == (chip ^ mask), counts, 0.0), 1, keepdims=True)
        hits.append(((row == first + slot) & (slot < live)).astype(jnp.float32))
    chooser = jnp.concatenate(hits, 0).astype(jnp.bfloat16)
    chooser_ref[...] = chooser
    chosen = jnp.dot(chooser, tokens_ref[...], preferred_element_type=jnp.float32)
    for place, out_ref in enumerate(reversed(out_refs)):
        out_ref[...] = chosen[place * capacity : (place + 1) * capacity].astype(jnp.bfloat16)


def packed_rows(tokens, counts, capacity):
    row_total, feat_cols = tokens.shape
    experts = counts.shape[1]
    tile = feat_cols // 2 if feat_cols % 256 == 0 else feat_cols
    block = pltpu.VMEM((capacity, feat_cols), jnp.bfloat16)
    chooser, *packed = pl.pallas_call(
        pack_kernel,
        out_shape=(jax.ShapeDtypeStruct((experts * capacity, row_total), jnp.bfloat16),)
        + (block,) * experts,
        grid=(feat_cols // tile,),
        in_specs=[
            pl.BlockSpec(counts.shape, lambda i: (0, 0)),
            pl.BlockSpec((row_total, tile), lambda i: (0, i)),
        ],
        out_specs=(pl.BlockSpec((experts * capacity, row_total), lambda i: (0, 0)),)
        + (pl.BlockSpec((capacity, tile), lambda i: (0, i)),) * experts,
        cost_estimate=pl.CostEstimate(
            flops=2 * experts * capacity * row_total * feat_cols,
            bytes_accessed=2 * (row_total + experts * capacity) * feat_cols,
            transcendentals=0,
        ),
        name="pack_rows",
    )(counts, pltpu.with_memory_space_constraint(tokens, pltpu.HBM))
    return chooser, packed


def project_kernel(*refs):
    *block_refs, weight_ref, out_ref, held = refs
    capacity = block_refs[0].shape[0]

    @pl.when(pl.program_id(0) == 0)
    def _():
        for place, block_ref in enumerate(reversed(block_refs)):
            held[place * capacity : (place + 1) * capacity, :] = block_ref[...]

    sums = jnp.dot(held[...], weight_ref[...], preferred_element_type=jnp.float32)
    for place in range(len(block_refs)):
        out_ref[place] = sums[place * capacity : (place + 1) * capacity].astype(jnp.bfloat16)


def projected(blocks, weights):
    count = len(blocks)
    capacity, feat_cols = blocks[0].shape
    units = weights.shape[1]
    tile = units
    return pl.pallas_call(
        project_kernel,
        out_shape=jax.ShapeDtypeStruct((count, capacity, units), jnp.bfloat16),
        grid=(units // tile,),
        in_specs=[pl.BlockSpec((capacity, feat_cols), lambda i: (0, 0))] * count
        + [pl.BlockSpec((feat_cols, tile), lambda i: (0, i))],
        out_specs=pl.BlockSpec((count, capacity, tile), lambda i: (0, 0, i)),
        scratch_shapes=[pltpu.VMEM((count * capacity, feat_cols), jnp.bfloat16)],
        compiler_params=pltpu.CompilerParams(vmem_limit_bytes=24 * 2**20),
        cost_estimate=pl.CostEstimate(
            flops=2 * count * capacity * feat_cols * units,
            bytes_accessed=2 * (count * capacity * (feat_cols + units) + feat_cols * units),
            transcendentals=0,
        ),
        name="project",
    )(*reversed(blocks), pltpu.with_memory_space_constraint(weights, pltpu.VMEM))


def weight_kernel(count, *refs):
    input_refs, grad_refs = refs[:count], refs[count:-3]
    gate_ref, up_ref, held = refs[-3:]
    half_units = gate_ref.shape[2]

    @pl.when(pl.program_id(0) == 0)
    def _():
        place = 0
        for grad_ref in grad_refs:
            held[place : place + grad_ref.shape[0], :] = grad_ref[...]
            place += grad_ref.shape[0]

    inputs = jnp.concatenate([input_ref[...] for input_ref in input_refs], 0)
    for out_ref, offset in ((gate_ref, 0), (up_ref, half_units)):
        out_ref[0] = lax.dot_general(
            inputs,
            held[:, offset : offset + half_units],
            (((0,), (0,)), ((), ())),
            preferred_element_type=jnp.float32,
        ).astype(jnp.bfloat16)


def weight_grads(inputs, grads):
    count = len(inputs)
    rows = sum(value.shape[0] for value in inputs)
    feat_cols = inputs[0].shape[1]
    units = grads[0].shape[1]
    tile = 256 if feat_cols % 256 == 0 else feat_cols
    out = jax.ShapeDtypeStruct((1, feat_cols, units // 2), jnp.bfloat16)
    out_spec = pl.BlockSpec((1, tile, units // 2), lambda i: (0, i, 0))
    return pl.pallas_call(
        lambda *refs: weight_kernel(count, *refs),
        out_shape=(out, out),
        grid=(feat_cols // tile,),
        in_specs=[pl.BlockSpec((value.shape[0], tile), lambda i: (0, i)) for value in inputs]
        + [pl.BlockSpec(value.shape, lambda i: (0, 0)) for value in grads],
        out_specs=(out_spec, out_spec),
        scratch_shapes=[pltpu.VMEM((rows, units), jnp.bfloat16)],
        compiler_params=pltpu.CompilerParams(vmem_limit_bytes=16 * 2**20),
        cost_estimate=pl.CostEstimate(
            flops=2 * rows * feat_cols * units,
            bytes_accessed=2 * (rows * (feat_cols + units) + feat_cols * units),
            transcendentals=0,
        ),
        name="weight_grads",
    )(*inputs, *grads)


def earlier(value, *needed):
    return lax.optimization_barrier((value,) + needed)[0]


def add_rounded(first, second):
    return (first.astype(jnp.float32) + second.astype(jnp.float32)).astype(jnp.bfloat16)


class Chain:
    def __init__(self, chip, size):
        self.chip = chip
        self.size = size
        self.index = lax.axis_index("fsdp")
        self.reach = {1: size // 2, -1: size - 1 - size // 2}
        self.partial = None
        self.whole = None
        self.came = {}

    def owner(self, steps):
        return lax.rem(self.index + self.size + steps, self.size)

    def block(self, steps):
        return pick(self.partial, self.owner(steps) ^ self.chip)

    def send(self, way, value):
        ring = [(source, (source + way) % self.size) for source in range(self.size)]
        self.came[way] = lax.ppermute(value, "fsdp", ring)

    def place(self, value, steps):
        self.whole = lax.dynamic_update_index_in_dim(
            self.whole, value, self.owner(steps) ^ self.chip, 0
        )


def on_device(tokens, counts, gate_values, up_values, gate_scales, up_scales, grad_hidden):
    row_total, feat_cols = tokens.shape
    experts = counts.shape[1]
    capacity = min(4 * row_total // experts, row_total // 2)
    n_fsdp = lax.axis_size("fsdp")
    chips = lax.axis_size("expert") // 2
    half_units = gate_values.shape[2]
    parity = lax.axis_index("expert") % 2
    chip = lax.axis_index("expert") // 2
    index = lax.axis_index("fsdp")
    masks = range(chips)

    chooser, packed = packed_rows(tokens, counts, capacity)
    weights = scaled_weights(
        gate_values, up_values, gate_scales, up_scales, index * feat_cols
    )
    cots = grad_hidden[0].reshape(2, capacity, half_units)
    chains = [Chain(chip, n_fsdp) for _ in range(2)]
    hiddens = [None, None]
    token = None

    def ordered(value):
        return value if token is None else earlier(value, token)

    def begin(group):
        nonlocal token
        chain = chains[group]
        chain.partial = projected(inputs[group], weights)
        for way, reach in chain.reach.items():
            if reach:
                token = ordered(chain.block(way * reach))
                chain.send(way, token)

    def reduce(group, way, step):
        nonlocal token
        chain = chains[group]
        token = add_rounded(
            chain.block(way * (chain.reach[way] - step)), ordered(chain.came[way])
        )
        chain.send(way, token)

    def activate(group):
        nonlocal token
        chain = chains[group]
        pre = chain.block(0).astype(jnp.float32)
        for came in chain.came.values():
            pre = pre + ordered(came).astype(jnp.float32)
        gate_pre = pre[:, :half_units]
        up_pre = pre[:, half_units:]
        cot = pick(cots, parity ^ (1 - group)).astype(jnp.float32)
        sigmoid_gate = jax.nn.sigmoid(gate_pre)
        hiddens[group] = (gate_pre * sigmoid_gate * up_pre).astype(jnp.bfloat16)
        grad_gate_pre = cot * up_pre * sigmoid_gate * (1.0 + gate_pre * (1.0 - sigmoid_gate))
        grad_up_pre = cot * gate_pre * sigmoid_gate
        token = jnp.concatenate(
            [grad_gate_pre.astype(jnp.bfloat16), grad_up_pre.astype(jnp.bfloat16)], 1
        )
        for way, reach in chain.reach.items():
            if reach:
                chain.send(way, token)
        chain.whole = jnp.zeros((chips, capacity, 2 * half_units), jnp.bfloat16)
        chain.place(token, 0)

    def gather(group, way, step):
        nonlocal token
        chain = chains[group]
        token = ordered(chain.came[way])
        chain.place(token, -way * step)
        if step < chain.reach[way]:
            chain.send(way, token)

    def back(whole):
        return lax.dot_general(
            whole, weights, (((1,), (1,)), ((), ())), preferred_element_type=jnp.float32
        ).astype(jnp.bfloat16)

    arrived = {mask: swap(packed[mask], "expert", 2 * mask + 1) for mask in reversed(masks)}
    passed = {mask: swap(arrived[mask], "expert", 1) for mask in reversed(masks[1:])}
    inputs = [
        [arrived[mask] for mask in masks],
        [passed[mask] if mask else packed[0] for mask in masks],
    ]
    for group in range(2):
        begin(group)
    steps = range(1, n_fsdp)
    for step in steps:
        for group in range(2):
            for way, reach in chains[group].reach.items():
                if step < reach:
                    reduce(group, way, step)
    for group in range(2):
        activate(group)
    for step in steps:
        for way, reach in chains[0].reach.items():
            for group in range(2):
                if step <= reach:
                    gather(group, way, step)
    wholes = [chain.whole.reshape(chips * capacity, 2 * half_units) for chain in chains]

    taken = swap(back(wholes[0]), "expert", 1)
    kept = back(earlier(wholes[1], taken))
    pieces = {}
    for mask in reversed(masks):
        rows = slice(mask * capacity, (mask + 1) * capacity)
        both = add_rounded(kept[rows], taken[rows])
        pieces[mask] = swap(both, "expert", 2 * mask) if mask else both

    hidden = jnp.where(
        parity == 0, jnp.concatenate([hiddens[1], hiddens[0]], 0), jnp.concatenate(hiddens, 0)
    )
    grad_gate, grad_up = weight_grads(inputs[0] + inputs[1], wholes)
    grad_tokens = lax.dot_general(
        chooser,
        jnp.concatenate([pieces[mask] for mask in reversed(masks)], 0),
        (((0,), (0,)), ((), ())),
        preferred_element_type=jnp.float32,
    ).astype(jnp.bfloat16)
    return (hidden[None], grad_gate, grad_up, grad_tokens)


def solution(mesh):
    in_specs = (
        P("expert", "fsdp"),
        P("expert", None),
        P("expert", "fsdp", None),
        P("expert", "fsdp", None),
        P("expert", None, None),
        P("expert", None, None),
        P("expert", "fsdp", None),
    )
    out_specs = (
        P("expert", "fsdp", None),
        P("expert", "fsdp", None),
        P("expert", "fsdp", None),
        P("expert", "fsdp"),
    )
    return jax.shard_map(
        on_device, mesh=mesh, in_specs=in_specs, out_specs=out_specs, check_vma=False
    )
```

```python
import math

import jax
import jax.numpy as jnp
from jax import lax
from jax.experimental import pallas as pl
from jax.experimental.pallas import tpu as pltpu
from jax.sharding import PartitionSpec as P


def swap(value, axis, mask):
    pairs = [(source, source ^ mask) for source in range(lax.axis_size(axis))]
    return lax.ppermute(value, axis, pairs)


def pick(blocks, index):
    return lax.dynamic_index_in_dim(blocks, index, 0, keepdims=False)


def scale_kernel(
    sub,
    start_ref,
    gate_ref,
    up_ref,
    gate_scale_ref,
    up_scale_ref,
    out_ref,
    gate_held,
    up_held,
    gate_rows,
    up_rows,
    sems,
):
    rows = out_ref.shape[0]
    half_units = gate_held.shape[1]
    step = pl.program_id(0)

    def arrival(which, turn):
        here = pl.ds(pl.multiple_of(turn * rows, rows), rows)
        value_ref, held = ((gate_ref, gate_held), (up_ref, up_held))[which]
        return pltpu.make_async_copy(
            value_ref.at[0, here, :], held.at[here, :], sems.at[which, turn]
        )

    @pl.when(step == 0)
    def _():
        for turn in range(gate_held.shape[0] // rows):
            for which in range(2):
                arrival(which, turn).start()
        shape = (gate_scale_ref.shape[1], half_units)
        spread = (
            lax.broadcasted_iota(jnp.int32, shape, 0)
            == lax.broadcasted_iota(jnp.int32, shape, 1) // 128
        ).astype(jnp.float32)
        for scale_ref, grown in ((gate_scale_ref, gate_rows), (up_scale_ref, up_rows)):
            grown[...] = lax.dot_general(
                scale_ref[0],
                spread,
                (((0,), (0,)), ((), ())),
                precision=lax.Precision.HIGHEST,
                preferred_element_type=jnp.float32,
            )

    for which, held, grown in ((0, gate_held, gate_rows), (1, up_held, up_rows)):
        arrival(which, step).wait()
        for piece in range(rows // sub):
            block = (start_ref[0] + step * rows + piece * sub) // 128
            there = pl.ds(pl.multiple_of(step * rows + piece * sub, sub), sub)
            scaled = held[there, :].astype(jnp.float32) * grown[pl.ds(block, 1), :]
            out_ref[piece * sub : (piece + 1) * sub, which * half_units : (which + 1) * half_units] = (
                scaled.astype(jnp.bfloat16)
            )


def scaled_weights(gate_values, up_values, gate_scales, up_scales, start_row):
    feat_cols, half_units = gate_values.shape[1:]
    sub = math.gcd(feat_cols, 128)
    rows = max(r for r in range(sub, 257, sub) if feat_cols % r == 0)
    gate_scales, up_scales = (jnp.swapaxes(value, 1, 2) for value in (gate_scales, up_scales))
    any_spec = pl.BlockSpec(memory_space=pl.ANY)
    scale_spec = pl.BlockSpec(gate_scales.shape, lambda i, start: (0, 0, 0))
    held = pltpu.VMEM((feat_cols, half_units), jnp.bfloat16)
    grown = pltpu.VMEM((gate_scales.shape[2], half_units), jnp.float32)
    return pl.pallas_call(
        lambda *refs: scale_kernel(sub, *refs),
        out_shape=jax.ShapeDtypeStruct((feat_cols, 2 * half_units), jnp.bfloat16),
        grid_spec=pltpu.PrefetchScalarGridSpec(
            num_scalar_prefetch=1,
            grid=(feat_cols // rows,),
            in_specs=[any_spec, any_spec, scale_spec, scale_spec],
            out_specs=pl.BlockSpec((rows, 2 * half_units), lambda i, start: (i, 0)),
            scratch_shapes=[
                held,
                held,
                grown,
                grown,
                pltpu.SemaphoreType.DMA((2, feat_cols // rows)),
            ],
        ),
        compiler_params=pltpu.CompilerParams(vmem_limit_bytes=16 * 2**20),
        cost_estimate=pl.CostEstimate(
            flops=2 * feat_cols * half_units,
            bytes_accessed=8 * feat_cols * half_units,
            transcendentals=0,
        ),
        name="scale_weights",
    )(
        start_row[None],
        pltpu.with_memory_space_constraint(gate_values, pltpu.HBM),
        pltpu.with_memory_space_constraint(up_values, pltpu.HBM),
        gate_scales,
        up_scales,
    )


def pack_kernel(counts_ref, tokens_ref, chooser_ref, *out_refs):
    chip = lax.axis_index("expert") // 2
    row_total = tokens_ref.shape[0]
    capacity = out_refs[0].shape[0]
    counts = counts_ref[...].astype(jnp.float32)
    expert = lax.broadcasted_iota(jnp.int32, counts.shape, 1)
    row = lax.broadcasted_iota(jnp.int32, (capacity, row_total), 1).astype(jnp.float32)
    slot = lax.broadcasted_iota(jnp.int32, (capacity, row_total), 0).astype(jnp.float32)
    hits = []
    for mask in reversed(range(len(out_refs))):
        first = jnp.sum(jnp.where(expert < (chip ^ mask), counts, 0.0), 1, keepdims=True)
        live = jnp.sum(jnp.where(expert == (chip ^ mask), counts, 0.0), 1, keepdims=True)
        hits.append(((row == first + slot) & (slot < live)).astype(jnp.float32))
    chooser = jnp.concatenate(hits, 0).astype(jnp.bfloat16)
    chooser_ref[...] = chooser
    chosen = jnp.dot(chooser, tokens_ref[...], preferred_element_type=jnp.float32)
    for place, out_ref in enumerate(reversed(out_refs)):
        out_ref[...] = chosen[place * capacity : (place + 1) * capacity].astype(jnp.bfloat16)


def packed_rows(tokens, counts, capacity):
    row_total, feat_cols = tokens.shape
    experts = counts.shape[1]
    tile = feat_cols
    block = pltpu.VMEM((capacity, feat_cols), jnp.bfloat16)
    chooser, *packed = pl.pallas_call(
        pack_kernel,
        out_shape=(jax.ShapeDtypeStruct((experts * capacity, row_total), jnp.bfloat16),)
        + (block,) * experts,
        grid=(feat_cols // tile,),
        in_specs=[
            pl.BlockSpec(counts.shape, lambda i: (0, 0)),
            pl.BlockSpec((row_total, tile), lambda i: (0, i)),
        ],
        out_specs=(pl.BlockSpec((experts * capacity, row_total), lambda i: (0, 0)),)
        + (pl.BlockSpec((capacity, tile), lambda i: (0, i)),) * experts,
        cost_estimate=pl.CostEstimate(
            flops=2 * experts * capacity * row_total * feat_cols,
            bytes_accessed=2 * (row_total + experts * capacity) * feat_cols,
            transcendentals=0,
        ),
        name="pack_rows",
    )(counts, pltpu.with_memory_space_constraint(tokens, pltpu.HBM))
    return chooser, packed


def project_kernel(*refs):
    *block_refs, weight_ref, out_ref, held = refs
    capacity = block_refs[0].shape[0]

    @pl.when(pl.program_id(0) == 0)
    def _():
        for place, block_ref in enumerate(reversed(block_refs)):
            held[place * capacity : (place + 1) * capacity, :] = block_ref[...]

    sums = jnp.dot(held[...], weight_ref[...], preferred_element_type=jnp.float32)
    for place in range(len(block_refs)):
        out_ref[place] = sums[place * capacity : (place + 1) * capacity].astype(jnp.bfloat16)


def projected(blocks, weights):
    count = len(blocks)
    capacity, feat_cols = blocks[0].shape
    units = weights.shape[1]
    tile = units
    return pl.pallas_call(
        project_kernel,
        out_shape=jax.ShapeDtypeStruct((count, capacity, units), jnp.bfloat16),
        grid=(units // tile,),
        in_specs=[pl.BlockSpec((capacity, feat_cols), lambda i: (0, 0))] * count
        + [pl.BlockSpec((feat_cols, tile), lambda i: (0, i))],
        out_specs=pl.BlockSpec((count, capacity, tile), lambda i: (0, 0, i)),
        scratch_shapes=[pltpu.VMEM((count * capacity, feat_cols), jnp.bfloat16)],
        compiler_params=pltpu.CompilerParams(vmem_limit_bytes=24 * 2**20),
        cost_estimate=pl.CostEstimate(
            flops=2 * count * capacity * feat_cols * units,
            bytes_accessed=2 * (count * capacity * (feat_cols + units) + feat_cols * units),
            transcendentals=0,
        ),
        name="project",
    )(*reversed(blocks), pltpu.with_memory_space_constraint(weights, pltpu.VMEM))


def weight_kernel(count, *refs):
    input_refs, grad_refs = refs[:count], refs[count:-3]
    gate_ref, up_ref, held = refs[-3:]
    half_units = gate_ref.shape[2]

    @pl.when(pl.program_id(0) == 0)
    def _():
        place = 0
        for grad_ref in grad_refs:
            held[place : place + grad_ref.shape[0], :] = grad_ref[...]
            place += grad_ref.shape[0]

    inputs = jnp.concatenate([input_ref[...] for input_ref in input_refs], 0)
    for out_ref, offset in ((gate_ref, 0), (up_ref, half_units)):
        out_ref[0] = lax.dot_general(
            inputs,
            held[:, offset : offset + half_units],
            (((0,), (0,)), ((), ())),
            preferred_element_type=jnp.float32,
        ).astype(jnp.bfloat16)


def weight_grads(inputs, grads):
    count = len(inputs)
    rows = sum(value.shape[0] for value in inputs)
    feat_cols = inputs[0].shape[1]
    units = grads[0].shape[1]
    tile = 256 if feat_cols % 256 == 0 else feat_cols
    out = jax.ShapeDtypeStruct((1, feat_cols, units // 2), jnp.bfloat16)
    out_spec = pl.BlockSpec((1, tile, units // 2), lambda i: (0, i, 0))
    return pl.pallas_call(
        lambda *refs: weight_kernel(count, *refs),
        out_shape=(out, out),
        grid=(feat_cols // tile,),
        in_specs=[pl.BlockSpec((value.shape[0], tile), lambda i: (0, i)) for value in inputs]
        + [pl.BlockSpec(value.shape, lambda i: (0, 0)) for value in grads],
        out_specs=(out_spec, out_spec),
        scratch_shapes=[pltpu.VMEM((rows, units), jnp.bfloat16)],
        compiler_params=pltpu.CompilerParams(vmem_limit_bytes=16 * 2**20),
        cost_estimate=pl.CostEstimate(
            flops=2 * rows * feat_cols * units,
            bytes_accessed=2 * (rows * (feat_cols + units) + feat_cols * units),
            transcendentals=0,
        ),
        name="weight_grads",
    )(*inputs, *grads)


def earlier(value, *needed):
    return lax.optimization_barrier((value,) + needed)[0]


def add_rounded(first, second):
    return (first.astype(jnp.float32) + second.astype(jnp.float32)).astype(jnp.bfloat16)


class Chain:
    def __init__(self, chip, size):
        self.chip = chip
        self.size = size
        self.index = lax.axis_index("fsdp")
        self.reach = {1: size // 2, -1: size - 1 - size // 2}
        self.partial = None
        self.whole = None
        self.came = {}

    def owner(self, steps):
        return lax.rem(self.index + self.size + steps, self.size)

    def block(self, steps):
        return pick(self.partial, self.owner(steps) ^ self.chip)

    def send(self, way, value):
        ring = [(source, (source + way) % self.size) for source in range(self.size)]
        self.came[way] = lax.ppermute(value, "fsdp", ring)

    def place(self, value, steps):
        self.whole = lax.dynamic_update_index_in_dim(
            self.whole, value, self.owner(steps) ^ self.chip, 0
        )


def on_device(tokens, counts, gate_values, up_values, gate_scales, up_scales, grad_hidden):
    row_total, feat_cols = tokens.shape
    experts = counts.shape[1]
    capacity = min(4 * row_total // experts, row_total // 2)
    n_fsdp = lax.axis_size("fsdp")
    chips = lax.axis_size("expert") // 2
    half_units = gate_values.shape[2]
    parity = lax.axis_index("expert") % 2
    chip = lax.axis_index("expert") // 2
    index = lax.axis_index("fsdp")
    masks = range(chips)

    chooser, packed = packed_rows(tokens, counts, capacity)
    weights = scaled_weights(
        gate_values, up_values, gate_scales, up_scales, index * feat_cols
    )
    cots = grad_hidden[0].reshape(2, capacity, half_units)
    chains = [Chain(chip, n_fsdp) for _ in range(2)]
    hiddens = [None, None]
    token = None

    def ordered(value):
        return value if token is None else earlier(value, token)

    def begin(group):
        nonlocal token
        chain = chains[group]
        chain.partial = projected(inputs[group], weights)
        for way, reach in chain.reach.items():
            if reach:
                token = ordered(chain.block(way * reach))
                chain.send(way, token)

    def reduce(group, way, step):
        nonlocal token
        chain = chains[group]
        token = add_rounded(
            chain.block(way * (chain.reach[way] - step)), ordered(chain.came[way])
        )
        chain.send(way, token)

    def activate(group):
        nonlocal token
        chain = chains[group]
        pre = chain.block(0).astype(jnp.float32)
        for came in chain.came.values():
            pre = pre + ordered(came).astype(jnp.float32)
        gate_pre = pre[:, :half_units]
        up_pre = pre[:, half_units:]
        cot = pick(cots, parity ^ (1 - group)).astype(jnp.float32)
        sigmoid_gate = jax.nn.sigmoid(gate_pre)
        hiddens[group] = (gate_pre * sigmoid_gate * up_pre).astype(jnp.bfloat16)
        grad_gate_pre = cot * up_pre * sigmoid_gate * (1.0 + gate_pre * (1.0 - sigmoid_gate))
        grad_up_pre = cot * gate_pre * sigmoid_gate
        token = jnp.concatenate(
            [grad_gate_pre.astype(jnp.bfloat16), grad_up_pre.astype(jnp.bfloat16)], 1
        )
        for way, reach in chain.reach.items():
            if reach:
                chain.send(way, token)
        chain.whole = jnp.zeros((chips, capacity, 2 * half_units), jnp.bfloat16)
        chain.place(token, 0)

    def gather(group, way, step):
        nonlocal token
        chain = chains[group]
        token = ordered(chain.came[way])
        chain.place(token, -way * step)
        if step < chain.reach[way]:
            chain.send(way, token)

    def back(whole):
        return lax.dot_general(
            whole, weights, (((1,), (1,)), ((), ())), preferred_element_type=jnp.float32
        ).astype(jnp.bfloat16)

    arrived = {mask: swap(packed[mask], "expert", 2 * mask + 1) for mask in reversed(masks)}
    passed = {mask: swap(arrived[mask], "expert", 1) for mask in reversed(masks[1:])}
    inputs = [
        [arrived[mask] for mask in masks],
        [passed[mask] if mask else packed[0] for mask in masks],
    ]
    for group in range(2):
        begin(group)
    steps = range(1, n_fsdp)
    for step in steps:
        for group in range(2):
            for way, reach in chains[group].reach.items():
                if step < reach:
                    reduce(group, way, step)
    for group in range(2):
        activate(group)
    for step in steps:
        for group in range(2):
            for way, reach in chains[group].reach.items():
                if step <= reach:
                    gather(group, way, step)
    wholes = [chain.whole.reshape(chips * capacity, 2 * half_units) for chain in chains]

    taken = swap(back(wholes[0]), "expert", 1)
    kept = back(earlier(wholes[1], taken))
    pieces = {}
    for mask in reversed(masks):
        rows = slice(mask * capacity, (mask + 1) * capacity)
        both = add_rounded(kept[rows], taken[rows])
        pieces[mask] = swap(both, "expert", 2 * mask) if mask else both

    hidden = jnp.where(
        parity == 0, jnp.concatenate([hiddens[1], hiddens[0]], 0), jnp.concatenate(hiddens, 0)
    )
    grad_gate, grad_up = weight_grads(inputs[0] + inputs[1], wholes)
    grad_tokens = lax.dot_general(
        chooser,
        jnp.concatenate([pieces[mask] for mask in reversed(masks)], 0),
        (((0,), (0,)), ((), ())),
        preferred_element_type=jnp.float32,
    ).astype(jnp.bfloat16)
    return (hidden[None], grad_gate, grad_up, grad_tokens)


def solution(mesh):
    in_specs = (
        P("expert", "fsdp"),
        P("expert", None),
        P("expert", "fsdp", None),
        P("expert", "fsdp", None),
        P("expert", None, None),
        P("expert", None, None),
        P("expert", "fsdp", None),
    )
    out_specs = (
        P("expert", "fsdp", None),
        P("expert", "fsdp", None),
        P("expert", "fsdp", None),
        P("expert", "fsdp"),
    )
    return jax.shard_map(
        on_device, mesh=mesh, in_specs=in_specs, out_specs=out_specs, check_vma=False
    )
```

```python
import math

import jax
import jax.numpy as jnp
from jax import lax
from jax.experimental import pallas as pl
from jax.experimental.pallas import tpu as pltpu
from jax.sharding import PartitionSpec as P


def swap(value, axis, mask):
    pairs = [(source, source ^ mask) for source in range(lax.axis_size(axis))]
    return lax.ppermute(value, axis, pairs)


def pick(blocks, index):
    return lax.dynamic_index_in_dim(blocks, index, 0, keepdims=False)


def scale_kernel(
    sub,
    start_ref,
    gate_ref,
    up_ref,
    gate_scale_ref,
    up_scale_ref,
    out_ref,
    gate_held,
    up_held,
    gate_rows,
    up_rows,
    sems,
):
    rows = out_ref.shape[0]
    half_units = gate_held.shape[1]
    step = pl.program_id(0)

    def arrival(which, turn):
        here = pl.ds(pl.multiple_of(turn * rows, rows), rows)
        value_ref, held = ((gate_ref, gate_held), (up_ref, up_held))[which]
        return pltpu.make_async_copy(
            value_ref.at[0, here, :], held.at[here, :], sems.at[which, turn]
        )

    @pl.when(step == 0)
    def _():
        for turn in range(gate_held.shape[0] // rows):
            for which in range(2):
                arrival(which, turn).start()
        shape = (gate_scale_ref.shape[1], half_units)
        spread = (
            lax.broadcasted_iota(jnp.int32, shape, 0)
            == lax.broadcasted_iota(jnp.int32, shape, 1) // 128
        ).astype(jnp.float32)
        for scale_ref, grown in ((gate_scale_ref, gate_rows), (up_scale_ref, up_rows)):
            grown[...] = lax.dot_general(
                scale_ref[0],
                spread,
                (((0,), (0,)), ((), ())),
                precision=lax.Precision.HIGHEST,
                preferred_element_type=jnp.float32,
            )

    for which, held, grown in ((0, gate_held, gate_rows), (1, up_held, up_rows)):
        arrival(which, step).wait()
        for piece in range(rows // sub):
            block = (start_ref[0] + step * rows + piece * sub) // 128
            there = pl.ds(pl.multiple_of(step * rows + piece * sub, sub), sub)
            scaled = held[there, :].astype(jnp.float32) * grown[pl.ds(block, 1), :]
            out_ref[piece * sub : (piece + 1) * sub, which * half_units : (which + 1) * half_units] = (
                scaled.astype(jnp.bfloat16)
            )


def scaled_weights(gate_values, up_values, gate_scales, up_scales, start_row):
    feat_cols, half_units = gate_values.shape[1:]
    sub = math.gcd(feat_cols, 128)
    rows = max(r for r in range(sub, 257, sub) if feat_cols % r == 0)
    gate_scales, up_scales = (jnp.swapaxes(value, 1, 2) for value in (gate_scales, up_scales))
    any_spec = pl.BlockSpec(memory_space=pl.ANY)
    scale_spec = pl.BlockSpec(gate_scales.shape, lambda i, start: (0, 0, 0))
    held = pltpu.VMEM((feat_cols, half_units), jnp.bfloat16)
    grown = pltpu.VMEM((gate_scales.shape[2], half_units), jnp.float32)
    return pl.pallas_call(
        lambda *refs: scale_kernel(sub, *refs),
        out_shape=jax.ShapeDtypeStruct((feat_cols, 2 * half_units), jnp.bfloat16),
        grid_spec=pltpu.PrefetchScalarGridSpec(
            num_scalar_prefetch=1,
            grid=(feat_cols // rows,),
            in_specs=[any_spec, any_spec, scale_spec, scale_spec],
            out_specs=pl.BlockSpec((rows, 2 * half_units), lambda i, start: (i, 0)),
            scratch_shapes=[
                held,
                held,
                grown,
                grown,
                pltpu.SemaphoreType.DMA((2, feat_cols // rows)),
            ],
        ),
        compiler_params=pltpu.CompilerParams(vmem_limit_bytes=16 * 2**20),
        cost_estimate=pl.CostEstimate(
            flops=2 * feat_cols * half_units,
            bytes_accessed=8 * feat_cols * half_units,
            transcendentals=0,
        ),
        name="scale_weights",
    )(
        start_row[None],
        pltpu.with_memory_space_constraint(gate_values, pltpu.HBM),
        pltpu.with_memory_space_constraint(up_values, pltpu.HBM),
        gate_scales,
        up_scales,
    )


def pack_kernel(counts_ref, tokens_ref, chooser_ref, *out_refs):
    chip = lax.axis_index("expert") // 2
    row_total = tokens_ref.shape[0]
    capacity = out_refs[0].shape[0]
    counts = counts_ref[...].astype(jnp.float32)
    expert = lax.broadcasted_iota(jnp.int32, counts.shape, 1)
    row = lax.broadcasted_iota(jnp.int32, (capacity, row_total), 1).astype(jnp.float32)
    slot = lax.broadcasted_iota(jnp.int32, (capacity, row_total), 0).astype(jnp.float32)
    hits = []
    for mask in reversed(range(len(out_refs))):
        first = jnp.sum(jnp.where(expert < (chip ^ mask), counts, 0.0), 1, keepdims=True)
        live = jnp.sum(jnp.where(expert == (chip ^ mask), counts, 0.0), 1, keepdims=True)
        hits.append(((row == first + slot) & (slot < live)).astype(jnp.float32))
    chooser = jnp.concatenate(hits, 0).astype(jnp.bfloat16)
    chooser_ref[...] = chooser
    chosen = jnp.dot(chooser, tokens_ref[...], preferred_element_type=jnp.float32)
    for place, out_ref in enumerate(reversed(out_refs)):
        out_ref[...] = chosen[place * capacity : (place + 1) * capacity].astype(jnp.bfloat16)


def packed_rows(tokens, counts, capacity):
    row_total, feat_cols = tokens.shape
    experts = counts.shape[1]
    tile = feat_cols
    block = pltpu.VMEM((capacity, feat_cols), jnp.bfloat16)
    chooser, *packed = pl.pallas_call(
        pack_kernel,
        out_shape=(jax.ShapeDtypeStruct((experts * capacity, row_total), jnp.bfloat16),)
        + (block,) * experts,
        grid=(feat_cols // tile,),
        in_specs=[
            pl.BlockSpec(counts.shape, lambda i: (0, 0)),
            pl.BlockSpec((row_total, tile), lambda i: (0, i)),
        ],
        out_specs=(pl.BlockSpec((experts * capacity, row_total), lambda i: (0, 0)),)
        + (pl.BlockSpec((capacity, tile), lambda i: (0, i)),) * experts,
        cost_estimate=pl.CostEstimate(
            flops=2 * experts * capacity * row_total * feat_cols,
            bytes_accessed=2 * (row_total + experts * capacity) * feat_cols,
            transcendentals=0,
        ),
        name="pack_rows",
    )(counts, tokens)
    return chooser, packed


def project_kernel(*refs):
    *block_refs, weight_ref, out_ref, held = refs
    capacity = block_refs[0].shape[0]

    @pl.when(pl.program_id(0) == 0)
    def _():
        for place, block_ref in enumerate(reversed(block_refs)):
            held[place * capacity : (place + 1) * capacity, :] = block_ref[...]

    sums = jnp.dot(held[...], weight_ref[...], preferred_element_type=jnp.float32)
    for place in range(len(block_refs)):
        out_ref[place] = sums[place * capacity : (place + 1) * capacity].astype(jnp.bfloat16)


def projected(blocks, weights):
    count = len(blocks)
    capacity, feat_cols = blocks[0].shape
    units = weights.shape[1]
    tile = units
    return pl.pallas_call(
        project_kernel,
        out_shape=jax.ShapeDtypeStruct((count, capacity, units), jnp.bfloat16),
        grid=(units // tile,),
        in_specs=[pl.BlockSpec((capacity, feat_cols), lambda i: (0, 0))] * count
        + [pl.BlockSpec((feat_cols, tile), lambda i: (0, i))],
        out_specs=pl.BlockSpec((count, capacity, tile), lambda i: (0, 0, i)),
        scratch_shapes=[pltpu.VMEM((count * capacity, feat_cols), jnp.bfloat16)],
        compiler_params=pltpu.CompilerParams(vmem_limit_bytes=24 * 2**20),
        cost_estimate=pl.CostEstimate(
            flops=2 * count * capacity * feat_cols * units,
            bytes_accessed=2 * (count * capacity * (feat_cols + units) + feat_cols * units),
            transcendentals=0,
        ),
        name="project",
    )(*reversed(blocks), pltpu.with_memory_space_constraint(weights, pltpu.VMEM))


def weight_kernel(count, *refs):
    input_refs, grad_refs = refs[:count], refs[count:-3]
    gate_ref, up_ref, held = refs[-3:]
    half_units = gate_ref.shape[2]

    @pl.when(pl.program_id(0) == 0)
    def _():
        place = 0
        for grad_ref in grad_refs:
            held[place : place + grad_ref.shape[0], :] = grad_ref[...]
            place += grad_ref.shape[0]

    inputs = jnp.concatenate([input_ref[...] for input_ref in input_refs], 0)
    for out_ref, offset in ((gate_ref, 0), (up_ref, half_units)):
        out_ref[0] = lax.dot_general(
            inputs,
            held[:, offset : offset + half_units],
            (((0,), (0,)), ((), ())),
            preferred_element_type=jnp.float32,
        ).astype(jnp.bfloat16)


def weight_grads(inputs, grads):
    count = len(inputs)
    rows = sum(value.shape[0] for value in inputs)
    feat_cols = inputs[0].shape[1]
    units = grads[0].shape[1]
    tile = 256 if feat_cols % 256 == 0 else feat_cols
    out = jax.ShapeDtypeStruct((1, feat_cols, units // 2), jnp.bfloat16)
    out_spec = pl.BlockSpec((1, tile, units // 2), lambda i: (0, i, 0))
    return pl.pallas_call(
        lambda *refs: weight_kernel(count, *refs),
        out_shape=(out, out),
        grid=(feat_cols // tile,),
        in_specs=[pl.BlockSpec((value.shape[0], tile), lambda i: (0, i)) for value in inputs]
        + [pl.BlockSpec(value.shape, lambda i: (0, 0)) for value in grads],
        out_specs=(out_spec, out_spec),
        scratch_shapes=[pltpu.VMEM((rows, units), jnp.bfloat16)],
        compiler_params=pltpu.CompilerParams(vmem_limit_bytes=16 * 2**20),
        cost_estimate=pl.CostEstimate(
            flops=2 * rows * feat_cols * units,
            bytes_accessed=2 * (rows * (feat_cols + units) + feat_cols * units),
            transcendentals=0,
        ),
        name="weight_grads",
    )(*inputs, *grads)


def earlier(value, *needed):
    return lax.optimization_barrier((value,) + needed)[0]


def add_rounded(first, second):
    return (first.astype(jnp.float32) + second.astype(jnp.float32)).astype(jnp.bfloat16)


class Chain:
    def __init__(self, chip, size):
        self.chip = chip
        self.size = size
        self.index = lax.axis_index("fsdp")
        self.reach = {1: size // 2, -1: size - 1 - size // 2}
        self.partial = None
        self.whole = None
        self.came = {}

    def owner(self, steps):
        return lax.rem(self.index + self.size + steps, self.size)

    def block(self, steps):
        return pick(self.partial, self.owner(steps) ^ self.chip)

    def send(self, way, value):
        ring = [(source, (source + way) % self.size) for source in range(self.size)]
        self.came[way] = lax.ppermute(value, "fsdp", ring)

    def place(self, value, steps):
        self.whole = lax.dynamic_update_index_in_dim(
            self.whole, value, self.owner(steps) ^ self.chip, 0
        )


def on_device(tokens, counts, gate_values, up_values, gate_scales, up_scales, grad_hidden):
    row_total, feat_cols = tokens.shape
    experts = counts.shape[1]
    capacity = min(4 * row_total // experts, row_total // 2)
    n_fsdp = lax.axis_size("fsdp")
    chips = lax.axis_size("expert") // 2
    half_units = gate_values.shape[2]
    parity = lax.axis_index("expert") % 2
    chip = lax.axis_index("expert") // 2
    index = lax.axis_index("fsdp")
    masks = range(chips)

    chooser, packed = packed_rows(tokens, counts, capacity)
    weights = scaled_weights(
        gate_values, up_values, gate_scales, up_scales, index * feat_cols
    )
    cots = grad_hidden[0].reshape(2, capacity, half_units)
    chains = [Chain(chip, n_fsdp) for _ in range(2)]
    hiddens = [None, None]
    token = None

    def ordered(value):
        return value if token is None else earlier(value, token)

    def begin(group):
        nonlocal token
        chain = chains[group]
        chain.partial = projected(inputs[group], weights)
        for way, reach in chain.reach.items():
            if reach:
                token = ordered(chain.block(way * reach))
                chain.send(way, token)

    def reduce(group, way, step):
        nonlocal token
        chain = chains[group]
        token = add_rounded(
            chain.block(way * (chain.reach[way] - step)), ordered(chain.came[way])
        )
        chain.send(way, token)

    def activate(group):
        nonlocal token
        chain = chains[group]
        pre = chain.block(0).astype(jnp.float32)
        for came in chain.came.values():
            pre = pre + ordered(came).astype(jnp.float32)
        gate_pre = pre[:, :half_units]
        up_pre = pre[:, half_units:]
        cot = pick(cots, parity ^ (1 - group)).astype(jnp.float32)
        sigmoid_gate = jax.nn.sigmoid(gate_pre)
        hiddens[group] = (gate_pre * sigmoid_gate * up_pre).astype(jnp.bfloat16)
        grad_gate_pre = cot * up_pre * sigmoid_gate * (1.0 + gate_pre * (1.0 - sigmoid_gate))
        grad_up_pre = cot * gate_pre * sigmoid_gate
        token = jnp.concatenate(
            [grad_gate_pre.astype(jnp.bfloat16), grad_up_pre.astype(jnp.bfloat16)], 1
        )
        for way, reach in chain.reach.items():
            if reach:
                chain.send(way, token)
        chain.whole = jnp.zeros((chips, capacity, 2 * half_units), jnp.bfloat16)
        chain.place(token, 0)

    def gather(group, way, step):
        nonlocal token
        chain = chains[group]
        token = ordered(chain.came[way])
        chain.place(token, -way * step)
        if step < chain.reach[way]:
            chain.send(way, token)

    def back(whole):
        return lax.dot_general(
            whole, weights, (((1,), (1,)), ((), ())), preferred_element_type=jnp.float32
        ).astype(jnp.bfloat16)

    arrived = {mask: swap(packed[mask], "expert", 2 * mask + 1) for mask in reversed(masks)}
    passed = {mask: swap(arrived[mask], "expert", 1) for mask in reversed(masks[1:])}
    inputs = [
        [arrived[mask] for mask in masks],
        [passed[mask] if mask else packed[0] for mask in masks],
    ]
    for group in range(2):
        begin(group)
    steps = range(1, n_fsdp)
    for step in steps:
        for group in range(2):
            for way, reach in chains[group].reach.items():
                if step < reach:
                    reduce(group, way, step)
    for group in range(2):
        activate(group)
    for step in steps:
        for group in range(2):
            for way, reach in chains[group].reach.items():
                if step <= reach:
                    gather(group, way, step)
    wholes = [chain.whole.reshape(chips * capacity, 2 * half_units) for chain in chains]

    taken = swap(back(wholes[0]), "expert", 1)
    kept = back(earlier(wholes[1], taken))
    pieces = {}
    for mask in reversed(masks):
        rows = slice(mask * capacity, (mask + 1) * capacity)
        both = add_rounded(kept[rows], taken[rows])
        pieces[mask] = swap(both, "expert", 2 * mask) if mask else both

    hidden = jnp.where(
        parity == 0, jnp.concatenate([hiddens[1], hiddens[0]], 0), jnp.concatenate(hiddens, 0)
    )
    grad_gate, grad_up = weight_grads(inputs[0] + inputs[1], wholes)
    grad_tokens = lax.dot_general(
        chooser,
        jnp.concatenate([pieces[mask] for mask in reversed(masks)], 0),
        (((0,), (0,)), ((), ())),
        preferred_element_type=jnp.float32,
    ).astype(jnp.bfloat16)
    return (hidden[None], grad_gate, grad_up, grad_tokens)


def solution(mesh):
    in_specs = (
        P("expert", "fsdp"),
        P("expert", None),
        P("expert", "fsdp", None),
        P("expert", "fsdp", None),
        P("expert", None, None),
        P("expert", None, None),
        P("expert", "fsdp", None),
    )
    out_specs = (
        P("expert", "fsdp", None),
        P("expert", "fsdp", None),
        P("expert", "fsdp", None),
        P("expert", "fsdp"),
    )
    return jax.shard_map(
        on_device, mesh=mesh, in_specs=in_specs, out_specs=out_specs, check_vma=False
    )
```

```python
import math

import jax
import jax.numpy as jnp
from jax import lax
from jax.experimental import pallas as pl
from jax.experimental.pallas import tpu as pltpu
from jax.sharding import PartitionSpec as P


def swap(value, axis, mask):
    pairs = [(source, source ^ mask) for source in range(lax.axis_size(axis))]
    return lax.ppermute(value, axis, pairs)


def pick(blocks, index):
    return lax.dynamic_index_in_dim(blocks, index, 0, keepdims=False)


def scale_kernel(
    sub,
    start_ref,
    gate_ref,
    up_ref,
    gate_scale_ref,
    up_scale_ref,
    out_ref,
    gate_held,
    up_held,
    gate_rows,
    up_rows,
    sems,
):
    rows = out_ref.shape[0]
    half_units = gate_held.shape[1]
    step = pl.program_id(0)

    def arrival(which, turn):
        here = pl.ds(pl.multiple_of(turn * rows, rows), rows)
        value_ref, held = ((gate_ref, gate_held), (up_ref, up_held))[which]
        return pltpu.make_async_copy(
            value_ref.at[0, here, :], held.at[here, :], sems.at[which, turn]
        )

    @pl.when(step == 0)
    def _():
        for turn in range(gate_held.shape[0] // rows):
            for which in range(2):
                arrival(which, turn).start()
        shape = (gate_scale_ref.shape[1], half_units)
        spread = (
            lax.broadcasted_iota(jnp.int32, shape, 0)
            == lax.broadcasted_iota(jnp.int32, shape, 1) // 128
        ).astype(jnp.float32)
        for scale_ref, grown in ((gate_scale_ref, gate_rows), (up_scale_ref, up_rows)):
            grown[...] = lax.dot_general(
                scale_ref[0],
                spread,
                (((0,), (0,)), ((), ())),
                precision=lax.Precision.HIGHEST,
                preferred_element_type=jnp.float32,
            )

    for which, held, grown in ((0, gate_held, gate_rows), (1, up_held, up_rows)):
        arrival(which, step).wait()
        for piece in range(rows // sub):
            block = (start_ref[0] + step * rows + piece * sub) // 128
            there = pl.ds(pl.multiple_of(step * rows + piece * sub, sub), sub)
            scaled = held[there, :].astype(jnp.float32) * grown[pl.ds(block, 1), :]
            out_ref[piece * sub : (piece + 1) * sub, which * half_units : (which + 1) * half_units] = (
                scaled.astype(jnp.bfloat16)
            )


def scaled_weights(gate_values, up_values, gate_scales, up_scales, start_row):
    feat_cols, half_units = gate_values.shape[1:]
    sub = math.gcd(feat_cols, 128)
    rows = max(r for r in range(sub, 257, sub) if feat_cols % r == 0)
    gate_scales, up_scales = (jnp.swapaxes(value, 1, 2) for value in (gate_scales, up_scales))
    any_spec = pl.BlockSpec(memory_space=pl.ANY)
    scale_spec = pl.BlockSpec(gate_scales.shape, lambda i, start: (0, 0, 0))
    held = pltpu.VMEM((feat_cols, half_units), jnp.bfloat16)
    grown = pltpu.VMEM((gate_scales.shape[2], half_units), jnp.float32)
    return pl.pallas_call(
        lambda *refs: scale_kernel(sub, *refs),
        out_shape=jax.ShapeDtypeStruct((feat_cols, 2 * half_units), jnp.bfloat16),
        grid_spec=pltpu.PrefetchScalarGridSpec(
            num_scalar_prefetch=1,
            grid=(feat_cols // rows,),
            in_specs=[any_spec, any_spec, scale_spec, scale_spec],
            out_specs=pl.BlockSpec((rows, 2 * half_units), lambda i, start: (i, 0)),
            scratch_shapes=[
                held,
                held,
                grown,
                grown,
                pltpu.SemaphoreType.DMA((2, feat_cols // rows)),
            ],
        ),
        compiler_params=pltpu.CompilerParams(vmem_limit_bytes=16 * 2**20),
        cost_estimate=pl.CostEstimate(
            flops=2 * feat_cols * half_units,
            bytes_accessed=8 * feat_cols * half_units,
            transcendentals=0,
        ),
        name="scale_weights",
    )(
        start_row[None],
        pltpu.with_memory_space_constraint(gate_values, pltpu.HBM),
        pltpu.with_memory_space_constraint(up_values, pltpu.HBM),
        gate_scales,
        up_scales,
    )


def pack_kernel(counts_ref, tokens_ref, chooser_ref, *out_refs):
    chip = lax.axis_index("expert") // 2
    row_total = tokens_ref.shape[0]
    capacity = out_refs[0].shape[0]
    experts = counts_ref.shape[1]
    row = lax.broadcasted_iota(jnp.int32, (capacity, row_total), 1)
    slot = lax.broadcasted_iota(jnp.int32, (capacity, row_total), 0)
    hits = []
    for mask in reversed(range(len(out_refs))):
        first = live = jnp.int32(0)
        for expert in range(experts):
            count = counts_ref[0, expert]
            first = first + jnp.where(expert < (chip ^ mask), count, 0)
            live = jnp.where(expert == (chip ^ mask), count, live)
        hits.append(((row == first + slot) & (slot < live)).astype(jnp.float32))
    chooser = jnp.concatenate(hits, 0).astype(jnp.bfloat16)
    chooser_ref[...] = chooser
    chosen = jnp.dot(chooser, tokens_ref[...], preferred_element_type=jnp.float32)
    for place, out_ref in enumerate(reversed(out_refs)):
        out_ref[...] = chosen[place * capacity : (place + 1) * capacity].astype(jnp.bfloat16)


def packed_rows(tokens, counts, capacity):
    row_total, feat_cols = tokens.shape
    experts = counts.shape[1]
    tile = feat_cols
    block = pltpu.VMEM((capacity, feat_cols), jnp.bfloat16)
    chooser, *packed = pl.pallas_call(
        pack_kernel,
        out_shape=(jax.ShapeDtypeStruct((experts * capacity, row_total), jnp.bfloat16),)
        + (block,) * experts,
        grid=(feat_cols // tile,),
        in_specs=[
            pl.BlockSpec(memory_space=pltpu.SMEM),
            pl.BlockSpec((row_total, tile), lambda i: (0, i)),
        ],
        out_specs=(pl.BlockSpec((experts * capacity, row_total), lambda i: (0, 0)),)
        + (pl.BlockSpec((capacity, tile), lambda i: (0, i)),) * experts,
        cost_estimate=pl.CostEstimate(
            flops=2 * experts * capacity * row_total * feat_cols,
            bytes_accessed=2 * (row_total + experts * capacity) * feat_cols,
            transcendentals=0,
        ),
        name="pack_rows",
    )(counts, tokens)
    return chooser, packed


def project_kernel(*refs):
    *block_refs, weight_ref, out_ref, held = refs
    capacity = block_refs[0].shape[0]

    @pl.when(pl.program_id(0) == 0)
    def _():
        for place, block_ref in enumerate(reversed(block_refs)):
            held[place * capacity : (place + 1) * capacity, :] = block_ref[...]

    sums = jnp.dot(held[...], weight_ref[...], preferred_element_type=jnp.float32)
    for place in range(len(block_refs)):
        out_ref[place] = sums[place * capacity : (place + 1) * capacity].astype(jnp.bfloat16)


def projected(blocks, weights):
    count = len(blocks)
    capacity, feat_cols = blocks[0].shape
    units = weights.shape[1]
    tile = units
    return pl.pallas_call(
        project_kernel,
        out_shape=jax.ShapeDtypeStruct((count, capacity, units), jnp.bfloat16),
        grid=(units // tile,),
        in_specs=[pl.BlockSpec((capacity, feat_cols), lambda i: (0, 0))] * count
        + [pl.BlockSpec((feat_cols, tile), lambda i: (0, i))],
        out_specs=pl.BlockSpec((count, capacity, tile), lambda i: (0, 0, i)),
        scratch_shapes=[pltpu.VMEM((count * capacity, feat_cols), jnp.bfloat16)],
        compiler_params=pltpu.CompilerParams(vmem_limit_bytes=24 * 2**20),
        cost_estimate=pl.CostEstimate(
            flops=2 * count * capacity * feat_cols * units,
            bytes_accessed=2 * (count * capacity * (feat_cols + units) + feat_cols * units),
            transcendentals=0,
        ),
        name="project",
    )(*reversed(blocks), pltpu.with_memory_space_constraint(weights, pltpu.VMEM))


def weight_kernel(count, *refs):
    input_refs, grad_refs = refs[:count], refs[count:-3]
    gate_ref, up_ref, held = refs[-3:]
    half_units = gate_ref.shape[2]

    @pl.when(pl.program_id(0) == 0)
    def _():
        place = 0
        for grad_ref in grad_refs:
            held[place : place + grad_ref.shape[0], :] = grad_ref[...]
            place += grad_ref.shape[0]

    inputs = jnp.concatenate([input_ref[...] for input_ref in input_refs], 0)
    for out_ref, offset in ((gate_ref, 0), (up_ref, half_units)):
        out_ref[0] = lax.dot_general(
            inputs,
            held[:, offset : offset + half_units],
            (((0,), (0,)), ((), ())),
            preferred_element_type=jnp.float32,
        ).astype(jnp.bfloat16)


def weight_grads(inputs, grads):
    count = len(inputs)
    rows = sum(value.shape[0] for value in inputs)
    feat_cols = inputs[0].shape[1]
    units = grads[0].shape[1]
    tile = 256 if feat_cols % 256 == 0 else feat_cols
    out = jax.ShapeDtypeStruct((1, feat_cols, units // 2), jnp.bfloat16)
    out_spec = pl.BlockSpec((1, tile, units // 2), lambda i: (0, i, 0))
    return pl.pallas_call(
        lambda *refs: weight_kernel(count, *refs),
        out_shape=(out, out),
        grid=(feat_cols // tile,),
        in_specs=[pl.BlockSpec((value.shape[0], tile), lambda i: (0, i)) for value in inputs]
        + [pl.BlockSpec(value.shape, lambda i: (0, 0)) for value in grads],
        out_specs=(out_spec, out_spec),
        scratch_shapes=[pltpu.VMEM((rows, units), jnp.bfloat16)],
        compiler_params=pltpu.CompilerParams(vmem_limit_bytes=16 * 2**20),
        cost_estimate=pl.CostEstimate(
            flops=2 * rows * feat_cols * units,
            bytes_accessed=2 * (rows * (feat_cols + units) + feat_cols * units),
            transcendentals=0,
        ),
        name="weight_grads",
    )(*inputs, *grads)


def earlier(value, *needed):
    return lax.optimization_barrier((value,) + needed)[0]


def add_rounded(first, second):
    return (first.astype(jnp.float32) + second.astype(jnp.float32)).astype(jnp.bfloat16)


class Chain:
    def __init__(self, chip, size):
        self.chip = chip
        self.size = size
        self.index = lax.axis_index("fsdp")
        self.reach = {1: size // 2, -1: size - 1 - size // 2}
        self.partial = None
        self.whole = None
        self.came = {}

    def owner(self, steps):
        return lax.rem(self.index + self.size + steps, self.size)

    def block(self, steps):
        return pick(self.partial, self.owner(steps) ^ self.chip)

    def send(self, way, value):
        ring = [(source, (source + way) % self.size) for source in range(self.size)]
        self.came[way] = lax.ppermute(value, "fsdp", ring)

    def place(self, value, steps):
        self.whole = lax.dynamic_update_index_in_dim(
            self.whole, value, self.owner(steps) ^ self.chip, 0
        )


def on_device(tokens, counts, gate_values, up_values, gate_scales, up_scales, grad_hidden):
    row_total, feat_cols = tokens.shape
    experts = counts.shape[1]
    capacity = min(4 * row_total // experts, row_total // 2)
    n_fsdp = lax.axis_size("fsdp")
    chips = lax.axis_size("expert") // 2
    half_units = gate_values.shape[2]
    parity = lax.axis_index("expert") % 2
    chip = lax.axis_index("expert") // 2
    index = lax.axis_index("fsdp")
    masks = range(chips)

    chooser, packed = packed_rows(tokens, counts, capacity)
    weights = scaled_weights(
        gate_values, up_values, gate_scales, up_scales, index * feat_cols
    )
    cots = grad_hidden[0].reshape(2, capacity, half_units)
    chains = [Chain(chip, n_fsdp) for _ in range(2)]
    hiddens = [None, None]
    token = None

    def ordered(value):
        return value if token is None else earlier(value, token)

    def begin(group):
        nonlocal token
        chain = chains[group]
        chain.partial = projected(inputs[group], weights)
        for way, reach in chain.reach.items():
            if reach:
                token = ordered(chain.block(way * reach))
                chain.send(way, token)

    def reduce(group, way, step):
        nonlocal token
        chain = chains[group]
        token = add_rounded(
            chain.block(way * (chain.reach[way] - step)), ordered(chain.came[way])
        )
        chain.send(way, token)

    def activate(group):
        nonlocal token
        chain = chains[group]
        pre = chain.block(0).astype(jnp.float32)
        for came in chain.came.values():
            pre = pre + ordered(came).astype(jnp.float32)
        gate_pre = pre[:, :half_units]
        up_pre = pre[:, half_units:]
        cot = pick(cots, parity ^ (1 - group)).astype(jnp.float32)
        sigmoid_gate = jax.nn.sigmoid(gate_pre)
        hiddens[group] = (gate_pre * sigmoid_gate * up_pre).astype(jnp.bfloat16)
        grad_gate_pre = cot * up_pre * sigmoid_gate * (1.0 + gate_pre * (1.0 - sigmoid_gate))
        grad_up_pre = cot * gate_pre * sigmoid_gate
        token = jnp.concatenate(
            [grad_gate_pre.astype(jnp.bfloat16), grad_up_pre.astype(jnp.bfloat16)], 1
        )
        for way, reach in chain.reach.items():
            if reach:
                chain.send(way, token)
        chain.whole = jnp.zeros((chips, capacity, 2 * half_units), jnp.bfloat16)
        chain.place(token, 0)

    def gather(group, way, step):
        nonlocal token
        chain = chains[group]
        token = ordered(chain.came[way])
        chain.place(token, -way * step)
        if step < chain.reach[way]:
            chain.send(way, token)

    def back(whole):
        return lax.dot_general(
            whole, weights, (((1,), (1,)), ((), ())), preferred_element_type=jnp.float32
        ).astype(jnp.bfloat16)

    arrived = {mask: swap(packed[mask], "expert", 2 * mask + 1) for mask in reversed(masks)}
    passed = {mask: swap(arrived[mask], "expert", 1) for mask in reversed(masks[1:])}
    inputs = [
        [arrived[mask] for mask in masks],
        [passed[mask] if mask else packed[0] for mask in masks],
    ]
    for group in range(2):
        begin(group)
    steps = range(1, n_fsdp)
    for step in steps:
        for group in range(2):
            for way, reach in chains[group].reach.items():
                if step < reach:
                    reduce(group, way, step)
    for group in range(2):
        activate(group)
    for step in steps:
        for group in range(2):
            for way, reach in chains[group].reach.items():
                if step <= reach:
                    gather(group, way, step)
    wholes = [chain.whole.reshape(chips * capacity, 2 * half_units) for chain in chains]

    taken = swap(back(wholes[0]), "expert", 1)
    kept = back(earlier(wholes[1], taken))
    pieces = {}
    for mask in reversed(masks):
        rows = slice(mask * capacity, (mask + 1) * capacity)
        both = add_rounded(kept[rows], taken[rows])
        pieces[mask] = swap(both, "expert", 2 * mask) if mask else both

    hidden = jnp.where(
        parity == 0, jnp.concatenate([hiddens[1], hiddens[0]], 0), jnp.concatenate(hiddens, 0)
    )
    grad_gate, grad_up = weight_grads(inputs[0] + inputs[1], wholes)
    grad_tokens = lax.dot_general(
        chooser,
        jnp.concatenate([pieces[mask] for mask in reversed(masks)], 0),
        (((0,), (0,)), ((), ())),
        preferred_element_type=jnp.float32,
    ).astype(jnp.bfloat16)
    return (hidden[None], grad_gate, grad_up, grad_tokens)


def solution(mesh):
    in_specs = (
        P("expert", "fsdp"),
        P("expert", None),
        P("expert", "fsdp", None),
        P("expert", "fsdp", None),
        P("expert", None, None),
        P("expert", None, None),
        P("expert", "fsdp", None),
    )
    out_specs = (
        P("expert", "fsdp", None),
        P("expert", "fsdp", None),
        P("expert", "fsdp", None),
        P("expert", "fsdp"),
    )
    return jax.shard_map(
        on_device, mesh=mesh, in_specs=in_specs, out_specs=out_specs, check_vma=False
    )
```
